128 devices in a mesh: ctx: 16 (over x, y_lo, core), expert: 8 (over z, y_hi).
Axes of the slice: x: 4, y: 4 (y_hi: 2, y_lo: 2; y = y_hi * 2 + y_lo), z: 4, core: 2. Of those that a mesh axis runs over, the one named last changes fastest.
Arguments:
- block_input: bfloat16 [8, 2048, 768], P('expert', 'ctx'), may hold values from -6 to 6
- gain_one: float32 [768], replicated, may hold values from 0.5 to 1.5
- qkv_weight: bfloat16 [3, 768, 768], replicated, may hold values from -0.21875 to 0.21875
- out_weight: bfloat16 [768, 768], replicated, may hold values from -0.5 to 0.5
- rel_table: float32 [32, 12], replicated, may hold values from -4 to 4
- gain_two: float32 [768], replicated, may hold values from 0.5 to 1.5
- router_weight: bfloat16 [768, 8], replicated, may hold values from -0.15625 to 0.15625
- routes: int32 [8, 2048, 1], P('expert', 'ctx'), may hold values from 0 to 7; in each aligned block of 128 rows (0 to 127, 128 to 255, ..., all dimensions but the last counted through in order) at most 24 rows name the same one
- w_in: bfloat16 [8, 768, 3072], P('expert'), may hold values from -0.21875 to 0.21875
- w_out: bfloat16 [8, 3072, 768], P('expert'), may hold values from -0.875 to 0.875
- cotangent: bfloat16 [8, 2048, 768], P('expert', 'ctx'), may hold values from -6 to 6
Outputs:
- block_output: bfloat16 [8, 2048, 768], P('expert', 'ctx')
- grad_input: float32 [8, 2048, 768], P('expert', 'ctx')
- grad_gain_one: float32 [768], P(('ctx', 'expert'))
- grad_qkv: float32 [3, 768, 768], P(None, ('ctx', 'expert'))
- grad_out: float32 [768, 768], P(('ctx', 'expert'))
- grad_table: float32 [32, 12], replicated
- grad_gain_two: float32 [768], P(('ctx', 'expert'))
- grad_router: float32 [768, 8], P(('ctx', 'expert'))
- grad_w_in: float32 [8, 768, 3072], P('expert', 'ctx')
- grad_w_out: float32 [8, 3072, 768], P('expert', 'ctx')
The draws below stay inside these ranges and needn't reach their ends.
Inputs may be any that keep to these rules, and one draw needn't show every extreme that they name: `routes`: each token names one expert; taking all sequences' tokens in order in aligned blocks of 128 (the rows of one device), no expert is named more than 24 times in a block, a bound that some block reaches.
All inputs are finite; a program needn't handle non-finite values.
Results may differ from the reference program's by a relative error of at most 0.04.
Values may be sent and summed in bfloat16 or wider, within the bound.
A program may use at most 128 MiB of HBM per device.

```python
import math
import jax
import jax.numpy as jnp
import numpy as np
from jax import lax

D = 768
HEADS = 12
HEAD_DIM = 64
FF = 3072
BUCKETS = 32
MAX_DISTANCE = 128
TOK_DEV = 128
LENGTH = 2048
SEQS = 8
TOKENS = 16384
EXPERTS = 8
CAP = 24


def level_of(rng, dims, cuts, least, top_value):
    level, own = 1.0, jax.random.fold_in(rng, 6)
    for position, parts in cuts:
        heights = jnp.exp(jax.random.uniform(jax.random.fold_in(own, position), (parts,), jnp.float32, least / len(cuts), top_value / len(cuts)))
        level = level * jnp.repeat(heights, dims[position] // parts).reshape([-1 if axis == position else 1 for axis in range(len(dims))])
    return level


def deal_out(rng, own, number, rows, number_of, top, limit, skew):
    sequence = jax.random.permutation(rng, number_of)
    heavy_load, ordinary = load_shares(number_of, rows * top, limit, skew, True), load_shares(number_of, rows * top, limit, skew, False)
    places = jnp.arange(number_of)

    def named(sizes, offset_by):
        used = int((sizes > 0).sum())
        fixed = max(1, used // 4)
        moved = fixed + (places - fixed + offset_by * (used - fixed)) % max(1, number_of - fixed)
        return jnp.zeros((number_of,), jnp.int32).at[sequence[jnp.where(places < fixed, places, moved)]].set(jnp.asarray(sizes, jnp.int32))

    sizes = jnp.where(number % 4 == 0, named(heavy_load, number // 4), named(ordinary, number - number // 4 - 1))
    mixed = jax.random.permutation(jax.random.fold_in(own, 3), number_of)
    donor, taker = mixed[0:number_of // 2 * 2:2], mixed[1:number_of // 2 * 2:2]
    margin = jnp.minimum(sizes[donor] - 1, limit - sizes[taker]) // 2
    margin = jnp.where((donor == sequence[0]) | (taker == sequence[0]) | (sizes[taker] == 0), 0, jnp.maximum(margin, 0))
    moved = jax.random.randint(jax.random.fold_in(own, 4), (number_of // 2,), 0, 1 << 20) % (margin + 1)
    sizes = sizes.at[donor].add(-moved).at[taker].add(moved)
    items = jnp.searchsorted(jnp.cumsum(sizes), jnp.arange(rows * top), side="right").astype(jnp.int32)
    table = items.reshape(top, rows).T
    table = table[jax.random.permutation(jax.random.fold_in(own, 1), rows)]
    offset_by = jax.random.randint(jax.random.fold_in(own, 2), (rows, 1), 0, top)
    return jnp.take_along_axis(table, (jnp.arange(top)[None, :] + offset_by) % top, axis=1)


def load_shares(amount, total, most, lean, full):
    portions = [(1 << 20) // math.isqrt(grade ** lean) + 1 for grade in range(1, amount + 1)]
    largest = most if full else min(most, max(-(-total // amount), total * portions[0] // sum(portions)))
    least = 1 if total - largest >= amount - 1 else 0
    holding, rest = [largest] + [least] * (amount - 1), total - largest - least * (amount - 1)
    while rest > 0:
        free = [i for i in range(1, amount) if holding[i] < largest] or [i for i in range(1, amount) if holding[i] < most]
        mass, remaining = sum([portions[i] for i in free]), rest
        for i in free:
            addition = min(most - holding[i], max(1, remaining * portions[i] // mass), rest)
            holding[i] = holding[i] + addition
            rest = rest - addition
    return np.array(holding)


def gaussian(rng, extent, deviation, bound, cuts=(), held_as=jnp.bfloat16):
    drawn = jax.random.normal(rng, extent, jnp.float32) * deviation
    if len(cuts) > 0:
        drawn = level_of(rng, extent, cuts, -0.22, 0.18) * drawn
    return jnp.clip(drawn, min=-bound, max=bound).astype(held_as)


def setup_inputs(seed: int = 0) -> dict:
    streams_of = jax.random.split(jax.random.key(seed), 12)
    block_input = gaussian(streams_of[0], (SEQS, LENGTH, D), 1.0, 6.0, ((0, 8), (1, 16)))
    gain_one = jnp.clip(1.0 + 0.1 * jax.random.normal(streams_of[1], (D,), jnp.float32), 0.5, 1.5)
    qkv_weight = gaussian(streams_of[2], (3, D, D), D ** -0.5, 0.21875)
    out_weight = gaussian(streams_of[3], (D, D), ((0.37 * LENGTH * D ** -1) ** 0.5 * D ** -0.5), 0.5)
    rel_table = gaussian(streams_of[4], (BUCKETS, HEADS), 1.0, 4.0, (), jnp.float32)
    gain_two = jnp.clip(1.0 + 0.1 * jax.random.normal(streams_of[5], (D,), jnp.float32), 0.5, 1.5)
    router_weight = gaussian(streams_of[6], (D, EXPERTS), (2 * D) ** -0.5, 0.15625)
    routes_keys = jax.random.split(jax.random.fold_in(streams_of[7], 1), SEQS * LENGTH // TOK_DEV)
    routes_turns = jax.random.permutation(jax.random.fold_in(streams_of[7], 3), SEQS * LENGTH // TOK_DEV)
    routes = jax.vmap(lambda own, number: deal_out(jax.random.fold_in(streams_of[7], 2), own, number, TOK_DEV, EXPERTS, 1, CAP, 2))(routes_keys, routes_turns).reshape((SEQS, LENGTH, 1))
    w_in = gaussian(streams_of[8], (EXPERTS, D, FF), D ** -0.5, 0.21875, ((0, 8),))
    w_out = gaussian(streams_of[9], (EXPERTS, FF, D), (FF // 64) ** -0.5, 0.875, ((0, 8),))
    cotangent = gaussian(streams_of[10], (SEQS, LENGTH, D), 1.0, 6.0, ((0, 8), (1, 16)))
    return {"block_input": block_input, "gain_one": gain_one, "qkv_weight": qkv_weight, "out_weight": out_weight, "rel_table": rel_table, "gain_two": gain_two, "router_weight": router_weight, "routes": routes, "w_in": w_in, "w_out": w_out, "cotangent": cotangent}


@jax.custom_vjp
def low(v):
    return lax.optimization_barrier(v.astype(jnp.bfloat16)).astype(jnp.float32)

@jax.custom_vjp
def low_back(v):
    return v

def low_keep(v):
    return (low(v), None)

def low_pass(kept, grad):
    return (grad,)

def back_keep(v):
    return (v, None)

def back_low(kept, grad):
    return (low(grad),)
low.defvjp(low_keep, low_pass)
low_back.defvjp(back_keep, back_low)
EPSILON = 1e-06
HIGH = lax.Precision.HIGHEST

def bucket_edges(buckets, reach):
    half = buckets // 2
    exact = half // 2
    spans = np.arange(1, reach + 1)
    spread = np.log(np.maximum(spans, exact) / exact) / np.log(reach / exact) * (half - exact)
    large = np.minimum(exact + spread.astype(np.int64), half - 1)
    level = np.where(spans < exact, spans, large)
    return [int(np.argmax(level >= b)) + 1 for b in range(1, half)]

def bucket_of(offset):
    half = BUCKETS // 2
    length = jnp.abs(offset)
    level = jnp.where(offset > 0, half, 0).astype(jnp.int32)
    for edge in bucket_edges(BUCKETS, MAX_DISTANCE):
        level = level + (length >= edge).astype(jnp.int32)
    return level

def rms_norm(rows, gain):
    return rows * lax.rsqrt(lax.optimization_barrier(jnp.mean(rows * rows, axis=-1, keepdims=True)) + EPSILON) * gain

def attention_rows(query_rows, first, keys, values, table):
    count = query_rows.shape[0]
    raw = low_back(jnp.einsum('qhd,khd->hqk', query_rows, keys, precision=HIGH))
    query_pos = first + jnp.arange(count, dtype=jnp.int32)
    offset = jnp.arange(LENGTH, dtype=jnp.int32)[None, :] - query_pos[:, None]
    half = BUCKETS // 2
    bias_full = jnp.where(offset[None] > 0, table[BUCKETS - 1][:, None, None], table[half - 1][:, None, None])
    window = min(count + 2 * MAX_DISTANCE, LENGTH)
    window_first = jnp.clip(first - MAX_DISTANCE, 0, LENGTH - window).astype(jnp.int32)
    near_offset = (window_first + jnp.arange(window, dtype=jnp.int32))[None, :] - query_pos[:, None]
    indicator = (bucket_of(near_offset)[:, :, None] == jnp.arange(BUCKETS, dtype=jnp.int32)).astype(jnp.float32)
    near_bias = jnp.einsum('qkb,bh->hqk', indicator, table, precision=HIGH)
    anchor = jnp.zeros((), jnp.int32)
    bias_full = lax.dynamic_update_slice(bias_full, near_bias, (anchor, anchor, window_first))
    scores = raw * HEAD_DIM ** (-0.5) + bias_full
    top = lax.optimization_barrier(jnp.max(scores, axis=2, keepdims=True))
    weights = jnp.exp(scores - top)
    probs = low(weights / lax.optimization_barrier(jnp.sum(weights, axis=2, keepdims=True)))
    return jnp.einsum('hqk,khd->qhd', probs, values, precision=HIGH).reshape(count, D)

def layer(whole_inputs, gain_one, qkv_weight, out_weight, rel_table, gain_two, router_weight, w_in, w_out, routes):
    inputs = whole_inputs.reshape(TOKENS, D)
    normed = low(rms_norm(inputs, gain_one))
    projected = [low_back(low(jnp.dot(normed, qkv_weight[p], precision=HIGH))) for p in range(3)]
    heads = [p.reshape(SEQS, LENGTH, HEADS, HEAD_DIM) for p in projected]
    block = min(256, LENGTH)
    blocks = LENGTH // block
    numbers = jnp.arange(SEQS * blocks, dtype=jnp.int32)
    starts = numbers % blocks * block
    owners = numbers // blocks
    query_blocks = heads[0].reshape(SEQS * blocks, block, HEADS, HEAD_DIM)
    key_heads = heads[1]
    value_heads = heads[2]

    def one_block(triple):
        keys = lax.dynamic_index_in_dim(key_heads, triple[2], 0, keepdims=False)
        values = lax.dynamic_index_in_dim(value_heads, triple[2], 0, keepdims=False)
        return attention_rows(triple[0], triple[1], keys, values, rel_table)
    core = lax.map(jax.checkpoint(one_block), (query_blocks, starts, owners)).reshape(TOKENS, D)
    attended = low_back(low(core))
    mixed = low_back(jnp.dot(attended, out_weight, precision=HIGH))
    middle = inputs + mixed
    normed_two = low(rms_norm(middle, gain_two))
    logits = jnp.dot(normed_two, router_weight, precision=HIGH)
    shifted = jnp.exp(logits - lax.optimization_barrier(jnp.max(logits, axis=1, keepdims=True)))
    router = shifted / lax.optimization_barrier(jnp.sum(shifted, axis=1, keepdims=True))
    choose = routes[:, 0:1] == jnp.arange(EXPERTS, dtype=jnp.int32)[None, :]
    gate = lax.optimization_barrier(jnp.sum(jnp.where(choose, router, 0.0), axis=1))
    places = TOKENS // TOK_DEV
    ranks = jnp.cumsum(choose.astype(jnp.int32).reshape(places, TOK_DEV, EXPERTS), axis=1).reshape(TOKENS, EXPERTS) - 1
    slot = lax.optimization_barrier(jnp.sum(jnp.where(choose, ranks, 0), axis=1))
    row_of = routes[:, 0] * (places * CAP) + jnp.arange(TOKENS, dtype=jnp.int32) // TOK_DEV * CAP + slot
    buffer = jnp.zeros((EXPERTS * places * CAP, D), jnp.float32).at[row_of].set(normed_two)
    buffer = low_back(buffer).reshape(EXPERTS, places * CAP, D)
    inner = low_back(jnp.einsum('erd,edf->erf', buffer, w_in, precision=HIGH))
    hidden = low(jax.nn.gelu(inner, approximate=True))
    produced = low(jnp.einsum('erf,efd->erd', hidden, w_out, precision=HIGH)).reshape(EXPERTS * places * CAP, D)
    returned = low_back(produced[row_of])
    return (middle + gate[:, None] * returned).reshape(SEQS, LENGTH, D)

def reference(block_input, gain_one, qkv_weight, out_weight, rel_table, gain_two, router_weight, routes, w_in, w_out, cotangent):
    floats = (block_input.astype(jnp.float32), gain_one, qkv_weight.astype(jnp.float32), out_weight.astype(jnp.float32), rel_table, gain_two, router_weight.astype(jnp.float32), w_in.astype(jnp.float32), w_out.astype(jnp.float32))
    flat_routes = routes.reshape(TOKENS, 1)

    def forward(*pieces):
        return layer(*pieces, flat_routes)
    result, pullback = jax.vjp(forward, *floats)
    grads = pullback(cotangent.astype(jnp.float32))
    return (result.astype(jnp.bfloat16), grads[0], grads[1], grads[2], grads[3], grads[4], grads[5], grads[6], grads[7], grads[8])
```

```python
import jax
import jax.numpy as jnp
import numpy as np
from jax import lax
from jax.experimental import pallas as pl
from jax.experimental.pallas import tpu as pltpu
from jax.sharding import PartitionSpec as P

HEADS = 12
HEAD_DIM = 64
BUCKETS = 32
MAX_DISTANCE = 128
EPSILON = 1e-06
SCALE = HEAD_DIM ** (-0.5)
TOK = 128
WIDTH = 768
FF = 3072
CAP = 24
F32 = jnp.float32
BF16 = jnp.bfloat16
MESH = pl.DeviceIdType.MESH
VMEM = pl.BlockSpec(memory_space=pltpu.VMEM)
SMEM = pl.BlockSpec(memory_space=pltpu.SMEM)
ANY = pl.BlockSpec(memory_space=pl.ANY)
VMEM_LIMIT = 60 * 1024 * 1024


def bucket_edges(buckets, reach):
    half = buckets // 2
    exact = half // 2
    spans = np.arange(1, reach + 1)
    spread = np.log(np.maximum(spans, exact) / exact) / np.log(reach / exact) * (half - exact)
    large = np.minimum(exact + spread.astype(np.int64), half - 1)
    level = np.where(spans < exact, spans, large)
    return [int(np.argmax(level >= b)) + 1 for b in range(1, half)]


EDGES = bucket_edges(BUCKETS, MAX_DISTANCE)


def dot(a, b):
    return jnp.dot(a, b, preferred_element_type=F32)


def dot_nt(a, b):
    return lax.dot_general(a, b, (((1,), (1,)), ((), ())), preferred_element_type=F32)


def dot_tn(a, b):
    return lax.dot_general(a, b, (((0,), (0,)), ((), ())), preferred_element_type=F32)


def iota(shape, dim):
    return lax.broadcasted_iota(jnp.int32, shape, dim)


class Place:
    def __init__(self):
        self.i = lax.axis_index("ctx")
        self.e = lax.axis_index("expert")
        self.x = lax.div(self.i, 4)
        self.y = lax.rem(lax.div(self.i, 2), 2)
        self.c = lax.rem(self.i, 2)
        self.z = lax.div(self.e, 2)
        self.h = lax.rem(self.e, 2)
        self.q = self.h * 2 + self.y

    def x_of(self, step):
        return lax.rem(self.x + 4 + step, 4)

    def x_peer(self, step):
        return (4 * self.x_of(step) + 2 * self.y + self.c, self.e)

    def core_peer(self):
        return (4 * self.x + 2 * self.y + 1 - self.c, self.e)

    def y_peer(self):
        return (4 * self.x + 2 * (1 - self.y) + self.c, self.e)

    def z_of(self, step):
        return lax.rem(self.z + 4 + step, 4)

    def z_peer(self, step):
        return (self.i, 2 * self.z_of(step) + self.h)

    def q_of(self, step):
        return lax.rem(self.q + 4 + step, 4)

    def q_peer(self, step):
        q = self.q_of(step)
        return (4 * self.x + 2 * lax.rem(q, 2) + self.c, 2 * self.z + lax.div(q, 2))

    def e_of(self, step):
        return lax.rem(self.e + 8 + step, 8)

    def e_peer(self, step):
        return (self.i, self.e_of(step))


def greet(peers):
    barrier = pltpu.get_barrier_semaphore()
    for peer in peers:
        pl.semaphore_signal(barrier, inc=1, device_id=peer, device_id_type=MESH)
    pl.semaphore_wait(barrier, len(peers))


def rcopy(src, dst, send, recv, slot, peer):
    return pltpu.make_async_remote_copy(
        src_ref=src,
        dst_ref=dst,
        send_sem=send.at[slot],
        recv_sem=recv.at[slot],
        device_id=peer,
        device_id_type=MESH,
    )


def rows(index, size):
    return pl.ds(pl.multiple_of(index * size, size), size)


def pair(first, half_first, second, half_second):
    if first is second and (half_first, half_second) == (0, 1):
        return first
    low = pltpu.roll(first, 64, 1) if half_first else first
    high = second if half_second else pltpu.roll(second, 64, 1)
    return jnp.where(iota(low.shape, 1) < 64, low, high)


def norm_places():
    col = iota((1, 1024), 1)
    r = col & 7
    xx = (col >> 3) & 3
    yl = (col >> 5) & 1
    e = (((col >> 7) & 3) << 1) + ((col >> 6) & 1)
    c = (col >> 9) & 1
    d = jnp.where(r < 6, 192 * xx + 96 * yl + 48 * c + 6 * e + r, -1)
    return (iota((WIDTH, 1024), 0) == d).astype(F32).astype(BF16)


def out_places():
    col = iota((1, 1024), 1)
    r = col & 7
    xx = (col >> 3) & 3
    yl = (col >> 5) & 1
    e = (((col >> 7) & 3) << 1) + ((col >> 6) & 1)
    c = (col >> 9) & 1
    f = 96 * yl + 48 * c + 6 * e + 2 * xx + r - 6
    f = jnp.where((r >= 6) & (xx < 3), f, -1)
    lane = iota((256, 1024), 0)
    feature = jnp.where(lane >= 128, lane - 128, jnp.where(lane >= 64, lane + 64, -2))
    return (feature == f).astype(F32).astype(BF16)


def bucket_tile(offset):
    length = jnp.abs(offset)
    level = jnp.where(offset > 0, BUCKETS // 2, 0)
    for edge in EDGES:
        level = level + (length >= edge).astype(jnp.int32)
    return level


def forward_kernel(
    inp_ref, gain_ref, w_ref, table_ref,
    att_ref, own_ref, q_ref, kv_ref, p_ref, inv_ref, norm_ref,
    proj, q_send, kv_send, norm_send, qexp, bias, s_ref, m_ref, l_ref, acc, o_t, send, recv,
):
    me = Place()
    greet([me.x_peer(1), me.x_peer(2), me.x_peer(3), me.core_peer(), me.y_peer()])
    inputs = inp_ref[...].astype(F32)
    root = lax.rsqrt(jnp.mean(inputs * inputs, axis=1, keepdims=True) + EPSILON)
    normed = (inputs * root * gain_ref[...]).astype(BF16)
    for p in range(3):
        proj[p] = dot(normed, w_ref[p])

    def group(p, piece):
        return proj[p, :, pl.ds(128 * (piece // 2), 128)]

    def join(p, a, s, b):
        first = group(p, a)
        second = first if (p == s and a // 2 == b // 2) else group(s, b)
        return pair(first, a % 2, second, b % 2)

    lane = iota((TOK, 128), 1)
    for g in range(4):
        a = 3 * g
        kv_send[g, :, pl.ds(0, 128)] = join(1, a, 1, a + 1).astype(BF16)
        kv_send[g, :, pl.ds(128, 128)] = join(1, a + 2, 2, a + 2).astype(BF16)
        kv_send[g, :, pl.ds(256, 128)] = join(2, a, 2, a + 1).astype(BF16)
        q_send[g, :, pl.ds(0, 128)] = join(0, a, 0, a + 1).astype(BF16)
        q_send[g, :, pl.ds(128, 128)] = jnp.where(lane < 64, join(0, a + 2, 0, a + 2), 0.0).astype(BF16)
    block = rows(me.i, TOK)
    copies = {}
    for step in (1, 3, 2):
        peer = me.x_peer(step)
        copies["kv", step] = rcopy(kv_send.at[me.x_of(step)], kv_ref.at[block], send, recv, step, peer)
        copies["kv", step].start()
    for step in (1, 3, 2):
        copies["q", step] = rcopy(
            q_send.at[me.x_of(step)], q_ref.at[rows(me.x, TOK)], send, recv, 4 + step, me.x_peer(step)
        )
        copies["q", step].start()
    kv_ref[block, :] = kv_send[me.x]
    q_ref[rows(me.x, TOK), :] = q_send[me.x]

    def source(step, y, c):
        return rows(4 * me.x_of(-step) + 2 * y + c, TOK)

    def pass_on(step):
        part = kv_ref.at[source(step, me.y, me.c)]
        copies["y", step] = rcopy(part, part, send, recv, 8 + step, me.y_peer())
        copies["y", step].start()
        copies["c", step] = rcopy(part, part, send, recv, 12 + step, me.core_peer())
        copies["c", step].start()

    pass_on(0)
    normed_wide = dot(normed, norm_places()).astype(BF16)
    norm_send[...] = normed_wide
    norm_ref[rows(me.x, TOK), :] = normed_wide
    tile = iota((128, 128), 0) - iota((128, 128), 1)
    for h in range(3):
        head = 3 * me.x + h

        def chain(first, n):
            value = jnp.full((128, 128), 1.0, F32) * table_ref[first, head]
            for level, edge in enumerate(EDGES):
                value = jnp.where(n >= edge, table_ref[first + level + 1, head], value)
            return value

        bias[h, 0] = jnp.full((128, 128), 1.0, F32) * table_ref[BUCKETS // 2 - 1, head]
        bias[h, 1] = chain(0, 128 - tile)
        bias[h, 2] = jnp.where(tile > 0, chain(BUCKETS // 2, tile), chain(0, -tile))
        bias[h, 3] = chain(BUCKETS // 2, 128 + tile)
        bias[h, 4] = jnp.full((128, 128), 1.0, F32) * table_ref[BUCKETS - 1, head]
        m_ref[h] = jnp.full((8, 512), -jnp.inf, F32)
        l_ref[h] = jnp.zeros((8, 512), F32)
    for step in (1, 3, 2):
        copies["q", step].wait_recv()
    lanes = iota((512, 256), 1)
    for h in range(3):
        mine = (lanes >= 64 * h) & (lanes < 64 * h + 64)
        qexp[h] = jnp.where(mine, q_ref[...].astype(F32) * SCALE, 0.0).astype(BF16)

    def score_blocks(first, last, y, c):
        def one(step, carry):
            b = 4 * me.x_of(-step) + 2 * y + c
            keys = kv_ref[rows(b, TOK), pl.ds(0, 256)]
            for h in range(3):
                s = dot_nt(keys, qexp[h])
                for t in range(4):
                    kind = jnp.clip(b - (4 * t + 2 * me.y + me.c), -2, 2) + 2
                    part = s[:, 128 * t : 128 * t + 128] + bias[h, kind]
                    cols = pl.ds(128 * t, 128)
                    s_ref[h, rows(b, TOK), cols] = part
                    m_ref[h, :, cols] = jnp.maximum(m_ref[h, :, cols], jnp.max(part.reshape(16, 8, 128), axis=0))
            return carry

        lax.fori_loop(first, last, one, 0)

    score_blocks(0, 1, me.y, me.c)
    for step in (1, 3, 2):
        copies["kv", step].wait_recv()
        pass_on(step)
    score_blocks(1, 4, me.y, me.c)
    for step in (0, 1, 3, 2):
        copies["y", step].wait_recv()
        part = kv_ref.at[source(step, 1 - me.y, me.c)]
        copies["f", step] = rcopy(part, part, send, recv, 16 + step, me.core_peer())
        copies["f", step].start()
        if step == 2:
            for other in (1, 3, 2):
                copies["n", other] = rcopy(
                    norm_send, norm_ref.at[rows(me.x, TOK)], send, recv, 20 + other, me.x_peer(other)
                )
                copies["n", other].start()
    for step in range(4):
        copies["c", step].wait_recv()
    score_blocks(0, 4, me.y, 1 - me.c)
    score_blocks(0, 4, 1 - me.y, me.c)
    for step in range(4):
        copies["f", step].wait_recv()
    score_blocks(0, 4, 1 - me.y, 1 - me.c)
    o_t[...] = jnp.zeros_like(o_t)
    inv_rows = jnp.zeros((128, 512), F32)
    for h in range(3):
        top = jnp.max(m_ref[h], axis=0, keepdims=True)
        acc[...] = jnp.zeros_like(acc)

        def weigh(j, carry):
            part = jnp.exp(s_ref[h, rows(j, 256), :] - top)
            l_ref[h] += jnp.sum(part.reshape(32, 8, 512), axis=0)
            low = part.astype(BF16)
            p_ref[rows(j, 256), pl.ds(512 * h, 512)] = low
            acc[...] += dot_tn(kv_ref[rows(j, 256), pl.ds(128, 256)], low)
            return carry

        lax.fori_loop(0, 8, weigh, 0)
        inv = 1.0 / jnp.sum(l_ref[h], axis=0, keepdims=True)
        at = (128, 192, 64)[h]
        o_t[pl.ds(at, 64), :] = acc[pl.ds(at, 64), :] * inv
        inv_rows = jnp.where(iota((128, 512), 0) == h, inv, inv_rows)
    inv_ref[...] = inv_rows.T
    own_ref[...] = o_t[...].T.astype(BF16)
    for step in (1, 3, 2):
        copies["o", step] = rcopy(
            own_ref.at[rows(me.x_of(step), TOK)], att_ref.at[me.x], send, recv, 24 + step, me.x_peer(step)
        )
        copies["o", step].start()
    att_ref[me.x] = own_ref[rows(me.x, TOK), :]
    for step in (1, 3, 2):
        copies["n", step].wait_recv()
        copies["o", step].wait_recv()
    for copy in copies.values():
        copy.wait_send()


def forward(inputs, gain, weights, table):
    shape = jax.ShapeDtypeStruct
    return pl.pallas_call(
        forward_kernel,
        out_shape=(
            shape((4, TOK, 256), BF16),
            shape((512, 256), BF16),
            shape((512, 256), BF16),
            shape((2048, 384), BF16),
            shape((2048, 1536), BF16),
            shape((512, 128), F32),
            shape((512, 1024), BF16),
        ),
        in_specs=[VMEM, VMEM, VMEM, SMEM],
        out_specs=(VMEM,) * 7,
        scratch_shapes=[
            pltpu.VMEM((3, TOK, WIDTH), F32),
            pltpu.VMEM((4, TOK, 256), BF16),
            pltpu.VMEM((4, TOK, 384), BF16),
            pltpu.VMEM((TOK, 1024), BF16),
            pltpu.VMEM((3, 512, 256), BF16),
            pltpu.VMEM((3, 5, 128, 128), F32),
            pltpu.VMEM((3, 2048, 512), F32),
            pltpu.VMEM((3, 8, 512), F32),
            pltpu.VMEM((3, 8, 512), F32),
            pltpu.VMEM((256, 512), F32),
            pltpu.VMEM((256, 512), F32),
            pltpu.SemaphoreType.DMA((28,)),
            pltpu.SemaphoreType.DMA((28,)),
        ],
        compiler_params=pltpu.CompilerParams(
            collective_id=0, has_side_effects=True, vmem_limit_bytes=VMEM_LIMIT
        ),
    )(inputs, gain, weights, table)


def expert_kernel(
    att_ref, inp_ref, out_w_ref, gain_ref, router_ref, routes_ref, w_in_hbm, w_out_hbm, cot_ref,
    y_ref, gmid_ref, gmix_ref, small_ref, da_ref, gwi_hbm, gwo_hbm,
    w_in, w_out, middle, select, send_rows, recv_rows, send_back, recv_back, hidden, ginner,
    arrived, gprod, made, garr, gwi, gwo, da_send, local, send, recv,
):
    me = Place()
    load_in = pltpu.make_async_copy(w_in_hbm.at[0], w_in, local.at[0])
    load_in.start()
    load_out = pltpu.make_async_copy(w_out_hbm.at[0], w_out, local.at[1])
    load_out.start()
    greet([me.e_peer(k) for k in range(1, 8)] + [me.x_peer(k) for k in range(1, 4)])
    mixed = inp_ref[...].astype(F32)
    for g in range(4):
        mixed = mixed + dot(att_ref[g, :, pl.ds(0, 128)], out_w_ref[pl.ds(192 * g + 64, 128), :])
        mixed = mixed + dot(att_ref[g, :, pl.ds(128, 128)], out_w_ref[pl.ds(192 * g, 128), :])
    middle[...] = mixed
    root = lax.rsqrt(jnp.mean(mixed * mixed, axis=1, keepdims=True) + EPSILON)
    normed = (mixed * root * gain_ref[...]).astype(BF16)
    logits = dot(normed, router_ref[...])
    shifted = jnp.exp(logits - jnp.max(logits, axis=1, keepdims=True))
    router = shifted / jnp.sum(shifted, axis=1, keepdims=True)
    choose = routes_ref[...] == iota((TOK, 8), 1)
    chosen = choose.astype(F32)
    gate = jnp.sum(chosen * router, axis=1, keepdims=True)
    earlier = (iota((TOK, TOK), 0) > iota((TOK, TOK), 1)).astype(F32).astype(BF16)
    ranks = dot(earlier, chosen.astype(BF16))
    slot = jnp.sum(chosen * ranks, axis=1, keepdims=True).astype(jnp.int32)
    target = routes_ref[...] * (2 * CAP) + slot
    column = iota((TOK, 16 * CAP), 1)
    select[pl.ds(0, TOK), :] = (column == target).astype(F32).astype(BF16)
    select[pl.ds(TOK, TOK), :] = (column == target + CAP).astype(F32).astype(BF16)
    dy = cot_ref[...].astype(F32)
    both = jnp.concatenate([normed, (gate * dy).astype(BF16)], axis=0)
    send_rows[...] = dot_tn(select[...], both).astype(BF16)
    mine = rows(me.e, 2 * CAP)
    there = []
    for k in (1, 7, 2, 6, 3, 5, 4):
        copy = rcopy(
            send_rows.at[rows(me.e_of(k), 2 * CAP)], recv_rows.at[mine], send, recv, k, me.e_peer(k)
        )
        copy.start()
        there.append(copy)
    recv_rows[mine, :] = send_rows[mine, :]
    made[...] = jnp.zeros_like(made)
    garr[...] = jnp.zeros_like(garr)
    load_in.wait()
    load_out.wait()
    for copy in there:
        copy.wait_recv()
    got = recv_rows[...].astype(F32).reshape(8, 2 * CAP, WIDTH)
    arrived[...] = got[:, :CAP].reshape(8 * CAP, WIDTH).astype(BF16)
    gprod[...] = got[:, CAP:].reshape(8 * CAP, WIDTH).astype(BF16)
    chunk = 512

    def through(j, carry):
        cols = rows(j, chunk)
        inner = dot(arrived[...], w_in[:, cols])
        square = inner * inner
        slope = np.float32(np.sqrt(2 / np.pi))
        t = jnp.tanh(slope * inner * (1.0 + 0.044715 * square))
        half = 0.5 * (1.0 + t)
        low = (inner * half).astype(BF16)
        hidden[:, cols] = low
        made[...] += dot(low, w_out[cols, :])
        back = dot_nt(gprod[...], w_out[cols, :])
        lean = half + 0.5 * inner * (1.0 - t * t) * slope * (1.0 + 3 * 0.044715 * square)
        grad = (lean * back).astype(BF16)
        ginner[:, cols] = grad
        garr[...] += dot_nt(grad, w_in[:, cols])
        return carry

    lax.fori_loop(0, FF // chunk, through, 0)
    back = jnp.concatenate([made[...].reshape(8, CAP, WIDTH), garr[...].reshape(8, CAP, WIDTH)], axis=1)
    send_back[...] = back.reshape(16 * CAP, WIDTH).astype(BF16)
    home = []
    for k in (1, 7, 2, 6, 3, 5, 4):
        copy = rcopy(
            send_back.at[rows(me.e_of(k), 2 * CAP)], recv_back.at[mine], send, recv, 8 + k, me.e_peer(k)
        )
        copy.start()
        home.append(copy)
    recv_back[mine, :] = send_back[mine, :]

    def weight_grads(j, carry):
        cols = rows(j, chunk)
        gwo[cols, :] = dot_tn(hidden[:, cols], gprod[...]).astype(BF16)
        gwi[:, cols] = dot_tn(arrived[...], ginner[:, cols]).astype(BF16)
        return carry

    lax.fori_loop(0, FF // chunk, weight_grads, 0)
    keep_in = pltpu.make_async_copy(gwi, gwi_hbm, local.at[2])
    keep_in.start()
    keep_out = pltpu.make_async_copy(gwo, gwo_hbm, local.at[3])
    keep_out.start()
    for copy in home:
        copy.wait_recv()
    returned = dot(select[pl.ds(0, TOK), :], recv_back[...])
    gnorm = dot(select[pl.ds(TOK, TOK), :], recv_back[...])
    mid = middle[...]
    y_ref[...] = (mid + gate * returned).astype(BF16)
    ggate = jnp.sum(dy * returned, axis=1, keepdims=True)
    glogits = ggate * gate * (chosen - router)
    high = glogits.astype(BF16)
    rest = (glogits - high.astype(F32)).astype(BF16)
    gnorm = gnorm + dot_nt(high, router_ref[...]) + dot_nt(rest, router_ref[...])
    small_ref[...] = jnp.zeros_like(small_ref)
    small_ref[pl.ds(8, 8), :] = dot_tn(high, normed) + dot_tn(rest, normed)
    small_ref[pl.ds(1, 1), :] = jnp.sum(gnorm * mid * root, axis=0, keepdims=True)
    u = gain_ref[...] * gnorm
    gmid = dy + root * u - mid * (root * root * root * jnp.mean(u * mid, axis=1, keepdims=True))
    gmid_ref[...] = gmid
    gmix = gmid.astype(BF16)
    gmix_ref[...] = gmix
    upper = iota((TOK, 128), 1) >= 64
    for g in range(4):
        front = dot_nt(gmix, out_w_ref[pl.ds(192 * g + 64, 128), :])
        da_send[g, :, pl.ds(0, 128)] = jnp.where(upper, front, 0.0).astype(BF16)
        da_send[g, :, pl.ds(128, 128)] = dot_nt(gmix, out_w_ref[pl.ds(192 * g, 128), :]).astype(BF16)
    away = []
    for k in (1, 3, 2):
        copy = rcopy(da_send.at[me.x_of(k)], da_ref.at[rows(me.x, TOK)], send, recv, 16 + k, me.x_peer(k))
        copy.start()
        away.append(copy)
    da_ref[rows(me.x, TOK), :] = da_send[me.x]
    for copy in away:
        copy.wait_recv()
    for copy in there + home + away:
        copy.wait_send()
    keep_in.wait()
    keep_out.wait()


def expert(att, inputs, out_w, gain, router_w, routes, w_in, w_out, cotangent):
    shape = jax.ShapeDtypeStruct
    return pl.pallas_call(
        expert_kernel,
        out_shape=(
            shape((TOK, WIDTH), BF16),
            shape((TOK, WIDTH), F32),
            shape((TOK, WIDTH), BF16),
            shape((16, WIDTH), F32),
            shape((512, 256), BF16),
            shape((WIDTH, FF), BF16),
            shape((FF, WIDTH), BF16),
        ),
        in_specs=[VMEM] * 6 + [ANY] * 2 + [VMEM],
        out_specs=(VMEM,) * 5 + (ANY,) * 2,
        scratch_shapes=[
            pltpu.VMEM((WIDTH, FF), BF16),
            pltpu.VMEM((FF, WIDTH), BF16),
            pltpu.VMEM((TOK, WIDTH), F32),
            pltpu.VMEM((2 * TOK, 16 * CAP), BF16),
            pltpu.VMEM((16 * CAP, WIDTH), BF16),
            pltpu.VMEM((16 * CAP, WIDTH), BF16),
            pltpu.VMEM((16 * CAP, WIDTH), BF16),
            pltpu.VMEM((16 * CAP, WIDTH), BF16),
            pltpu.VMEM((8 * CAP, FF), BF16),
            pltpu.VMEM((8 * CAP, FF), BF16),
            pltpu.VMEM((8 * CAP, WIDTH), BF16),
            pltpu.VMEM((8 * CAP, WIDTH), BF16),
            pltpu.VMEM((8 * CAP, WIDTH), F32),
            pltpu.VMEM((8 * CAP, WIDTH), F32),
            pltpu.VMEM((WIDTH, FF), BF16),
            pltpu.VMEM((FF, WIDTH), BF16),
            pltpu.VMEM((4, TOK, 256), BF16),
            pltpu.SemaphoreType.DMA((4,)),
            pltpu.SemaphoreType.DMA((20,)),
            pltpu.SemaphoreType.DMA((20,)),
        ],
        compiler_params=pltpu.CompilerParams(
            collective_id=1, has_side_effects=True, vmem_limit_bytes=VMEM_LIMIT
        ),
    )(att, inputs, out_w, gain, router_w, routes, w_in, w_out, cotangent)


SEM = {
    "gm": 0, "core_in": 4, "core_out": 5, "x_in": 6, "y_in": 10, "y_out": 11, "x_out": 12, "core_kv": 16, "y_kv": 24,
    "x_q": 28, "x_kv": 32, "a_core": 36, "a_z": 36, "a_q": 40, "a_x": 44, "t_core": 48, "t_z": 48, "t_q": 52, "t_x": 56,
}


def backward_kernel(
    p_ref, q_ref, kv_ref, own_ref, inv_ref, da_ref, norm_ref, gmix_ref, small_ref, inp_ref, gain_ref, w_ref,
    gmid_ref, gwi_hbm, gwo_hbm,
    gin_ref, gwin_ref, gwout_ref, b_ref, a_out_ref, table_ref,
    qexp, doexp, drow, accb, ds, dq, dkv, core_kv, y_send, y_kv, fin_kv, fin_q, home_q, home_kv, gm_all,
    dproj, wide, a_low, a_core, a_mid, a_z, a_mid2, a_q, a_last, small, trow, tabs, t_got,
    own_in, own_out, got_in, got_out, x_in, mid_in, y_in, y_out, x_out, local, send, recv,
):
    me = Place()
    load_in = pltpu.make_async_copy(gwi_hbm.at[:, me.c], own_in, local.at[0])
    load_in.start()
    load_out = pltpu.make_async_copy(gwo_hbm.at[:, me.c], own_out, local.at[1])
    load_out.start()
    greet(
        [me.core_peer()]
        + [me.x_peer(k) for k in (1, 2, 3)]
        + [me.z_peer(k) for k in (1, 2, 3)]
        + [me.q_peer(k) for k in (1, 2, 3)]
    )
    started = []

    def go(src, dst, name, step, peer):
        copy = rcopy(src, dst, send, recv, SEM[name] + step, peer)
        copy.start()
        started.append(copy)
        return copy

    core_in = go(gwi_hbm.at[:, 1 - me.c], got_in, "core_in", 0, me.core_peer())
    core_out = go(gwo_hbm.at[:, 1 - me.c], got_out, "core_out", 0, me.core_peer())
    gm = [go(gmix_ref, gm_all.at[rows(me.x, TOK)], "gm", k, me.x_peer(k)) for k in (1, 3, 2)]
    gm_all[rows(me.x, TOK), :] = gmix_ref[...]

    lanes = iota((512, 256), 1)
    queries = q_ref[...].astype(F32) * SCALE
    da = da_ref[...].astype(F32)
    product = da * own_ref[...].astype(F32)
    sums = jnp.zeros((512, 128), F32)
    for h in range(3):
        inside = (lanes >= 64 * h) & (lanes < 64 * h + 64)
        qexp[pl.ds(512 * h, 512), :] = jnp.where(inside, queries, 0.0).astype(BF16)
        at = (128, 192, 64)[h]
        inside = (lanes >= at) & (lanes < at + 64)
        inv = inv_ref[:, pl.ds(h, 1)]
        doexp[pl.ds(512 * h, 512), :] = jnp.where(inside, da * inv, 0.0).astype(BF16)
        total = jnp.sum(jnp.where(inside, product, 0.0), axis=1, keepdims=True) * inv
        sums = jnp.where(iota((512, 128), 1) == h, total, sums)
    drow[...] = sums.T
    accb[...] = jnp.zeros_like(accb)
    dq[...] = jnp.zeros_like(dq)

    def core_copy(rel, xx, y):
        block = rows(4 * xx + 2 * y + 1 - me.c, TOK)
        return rcopy(
            dkv.at[block], core_kv.at[4 * rel + xx], send, recv, SEM["core_kv"] + 4 * rel + xx, me.core_peer()
        )

    def attend(rel, y):
        def one(xx, carry):
            span = rows(2 * xx + y, 256)
            keys = kv_ref[span, pl.ds(0, 256)]
            values = kv_ref[span, pl.ds(128, 256)]
            for h in range(3):
                cols = pl.ds(512 * h, 512)
                grads = dot_nt(values, doexp[cols, :])
                part = p_ref[span, cols].astype(F32) * (grads - drow[pl.ds(h, 1), :])
                ds[:, cols] = part.astype(BF16)
                for k in range(2):
                    for t in range(4):
                        kind = jnp.clip(4 * xx + 2 * y + k - (4 * t + 2 * me.y + me.c), -2, 2) + 2
                        accb[h, kind] += part[128 * k : 128 * k + 128, 128 * t : 128 * t + 128]
            dq[...] += dot_tn(keys, ds[...])
            gk = dot(ds[...], qexp[...])
            gv = dot(p_ref[span, :], doexp[...])
            dkv[span, pl.ds(0, 128)] = gk[:, :128].astype(BF16)
            dkv[span, pl.ds(128, 128)] = (gk[:, 128:] + gv[:, :128]).astype(BF16)
            dkv[span, pl.ds(256, 128)] = gv[:, 128:].astype(BF16)
            core_copy(rel, xx, y).start()
            return carry

        lax.fori_loop(0, 4, one, 0)

    attend(0, 1 - me.y)

    def to_y(xx):
        return rcopy(y_send.at[xx], y_kv.at[xx], send, recv, SEM["y_kv"] + xx, me.y_peer())

    def forward_y(xx, carry):
        core_copy(0, xx, 1 - me.y).wait_recv()
        own = dkv[rows(4 * xx + 2 * (1 - me.y) + me.c, TOK), :].astype(F32)
        y_send[xx] = (own + core_kv[xx].astype(F32)).astype(BF16)
        to_y(xx).start()
        return carry

    lax.fori_loop(0, 4, forward_y, 0)
    load_in.wait()
    core_in.wait_recv()

    def add_in(j, carry):
        own_in[j] = (own_in[j].astype(F32) + got_in[j].astype(F32)).astype(BF16)
        return carry

    lax.fori_loop(0, 8, add_in, 0)
    xs_in = [go(own_in.at[pl.ds(2 * me.x_of(k), 2)], x_in.at[k - 1], "x_in", k, me.x_peer(k)) for k in (1, 3, 2)]
    load_out.wait()
    core_out.wait_recv()

    def add_out(j, carry):
        own_out[j] = (own_out[j].astype(F32) + got_out[j].astype(F32)).astype(BF16)
        return carry

    lax.fori_loop(0, 8, add_out, 0)
    ys_out = []
    for xx in range(4):
        copy = rcopy(
            own_out.at[2 * xx + 1 - me.y], y_out.at[xx], send, recv, SEM_Y_OUT + xx, me.y_peer()
        )
        copy.start()
        started.append(copy)
        ys_out.append(copy)

    attend(1, me.y)

    fin_q_t = jnp.concatenate(
        [
            dq[pl.ds(0, 64), pl.ds(0, 512)],
            dq[pl.ds(64, 64), pl.ds(512, 512)],
            dq[pl.ds(128, 64), pl.ds(1024, 512)],
            jnp.zeros((64, 512), F32),
        ],
        axis=0,
    )
    fin_q[...] = (fin_q_t * SCALE).T.astype(BF16)
    xs_q = [
        go(fin_q.at[rows(me.x_of(k), TOK)], home_q.at[me.x], "x_q", k, me.x_peer(k)) for k in (1, 3, 2)
    ]
    home_q[me.x] = fin_q[rows(me.x, TOK), :]
    xs_kv = []
    for k in (1, 3, 2, 0):
        xx = me.x_of(k)
        core_copy(1, xx, me.y).wait_recv()
        to_y(xx).wait_recv()
        own = dkv[rows(4 * xx + 2 * me.y + me.c, TOK), :].astype(F32)
        block = (own + core_kv[4 + xx].astype(F32) + y_kv[xx].astype(F32)).astype(BF16)
        fin_kv[rows(xx, TOK), :] = block
        if k:
            xs_kv.append(go(fin_kv.at[rows(xx, TOK)], home_kv.at[me.x], "x_kv", k, me.x_peer(k)))
        else:
            home_kv[me.x] = block

    tile = iota((128, 128), 0) - iota((128, 128), 1)
    before, middle, after = bucket_tile(tile - 128), bucket_tile(tile), bucket_tile(tile + 128)

    def bucket_sum(b, carry):
        for h in range(3):
            near = (
                jnp.where(before == b, accb[h, 1], 0.0)
                + jnp.where(middle == b, accb[h, 2], 0.0)
                + jnp.where(after == b, accb[h, 3], 0.0)
            )
            trow[h, pl.ds(b, 1), :] = jnp.sum(near, axis=0, keepdims=True)
        return carry

    lax.fori_loop(0, BUCKETS, bucket_sum, 0)
    table = jnp.zeros((BUCKETS, 128), F32)
    for h in range(3):
        trow[h, pl.ds(BUCKETS // 2 - 1, 1), :] += jnp.sum(accb[h, 0], axis=0, keepdims=True)
        trow[h, pl.ds(BUCKETS - 1, 1), :] += jnp.sum(accb[h, 4], axis=0, keepdims=True)
        total = jnp.sum(trow[h], axis=1, keepdims=True)
        table = jnp.where(iota((BUCKETS, 128), 1) == 3 * me.x + h, total, table)
    tabs[0] = table
    t_core = go(tabs.at[0], t_got.at[0], "t_core", 0, me.core_peer())

    wide[:, pl.ds(0, 256)] = dot_tn(norm_ref[...], fin_q[...])
    wide[:, pl.ds(256, 384)] = dot_tn(norm_ref[...], fin_kv[...])
    for copy in gm:
        copy.wait_recv()
    att_wide = dot(own_ref[...], out_places()).astype(BF16)
    from_out = dot_tn(att_wide, gm_all[...])
    wide[:, pl.ds(0, 640)] += from_out[:, :640]
    wide[:, pl.ds(640, 128)] = from_out[:, 640:]

    t_core.wait_recv()
    tabs[1] = tabs[0] + t_got[0]
    ts = [go(tabs.at[1], t_got.at[k], "t_z", k, me.z_peer(k)) for k in (1, 3, 2)]
    for copy in xs_q + xs_kv:
        copy.wait_recv()

    def piece(p, j):
        g, t = j // 3, j % 3
        if p == 0:
            return home_q[g, :, pl.ds(128 * (t // 2), 128)].astype(F32), t % 2
        if p == 1:
            return home_kv[g, :, pl.ds(128 * (t // 2), 128)].astype(F32), t % 2
        at, half = ((2, 0), (2, 1), (1, 1))[t]
        return home_kv[g, :, pl.ds(128 * at, 128)].astype(F32), half

    for p in range(3):
        for n in range(6):
            first, half_first = piece(p, 2 * n)
            second, half_second = piece(p, 2 * n + 1)
            dproj[p, :, pl.ds(128 * n, 128)] = pair(first, half_first, second, half_second).astype(BF16)
    gnorm = dot_nt(dproj[0], w_ref[0]) + dot_nt(dproj[1], w_ref[1]) + dot_nt(dproj[2], w_ref[2])
    inputs = inp_ref[...].astype(F32)
    root = lax.rsqrt(jnp.mean(inputs * inputs, axis=1, keepdims=True) + EPSILON)
    small[...] = jnp.zeros_like(small)
    small[pl.ds(0, 16), :] = small_ref[...]
    small[pl.ds(0, 1), :] = jnp.sum(gnorm * inputs * root, axis=0, keepdims=True)
    u = gain_ref[...] * gnorm
    mean = jnp.mean(u * inputs, axis=1, keepdims=True)
    gin_ref[...] = gmid_ref[...] + root * u - inputs * (root * root * root * mean)
    wide[:, pl.ds(640, 128)] += dot(small[...].astype(BF16), norm_places()).T
    a_low[...] = wide[...].astype(BF16)
    ac = go(a_low.at[rows(1 - me.c, 512)], a_core, "a_core", 0, me.core_peer())

    for copy in xs_in:
        copy.wait_recv()
    for j in range(2):
        total = own_in[2 * me.x + j].astype(F32)
        for k in range(3):
            total = total + x_in[k, j].astype(F32)
        mid_in[j] = total.astype(BF16)
    ys_in = go(mid_in.at[1 - me.y], y_in, "y_in", 0, me.y_peer())

    ac.wait_recv()
    a_mid[...] = (a_low[rows(me.c, 512), :].astype(F32) + a_core[...].astype(F32)).astype(BF16)
    az = [go(a_mid.at[rows(me.z_of(k), 128)], a_z.at[k - 1], "a_z", k, me.z_peer(k)) for k in (1, 3, 2)]

    for copy in ys_out:
        copy.wait_recv()
    for xx in range(4):
        y_out[xx] = (own_out[2 * xx + me.y].astype(F32) + y_out[xx].astype(F32)).astype(BF16)
    xs_out = [go(y_out.at[me.x_of(k)], x_out.at[k - 1], "x_out", k, me.x_peer(k)) for k in (1, 3, 2)]

    for copy in ts:
        copy.wait_recv()
    tabs[2] = tabs[1] + t_got[1] + t_got[2] + t_got[3]
    ts = [go(tabs.at[2], t_got.at[3 + k], "t_q", k, me.q_peer(k)) for k in (1, 3, 2)]
    for copy in az:
        copy.wait_recv()
    total = a_mid[rows(me.z, 128), :].astype(F32)
    for k in range(3):
        total = total + a_z[k].astype(F32)
    a_mid2[...] = total.astype(BF16)
    aq = [go(a_mid2.at[rows(me.q_of(k), 32)], a_q.at[k - 1], "a_q", k, me.q_peer(k)) for k in (1, 3, 2)]

    for copy in ts:
        copy.wait_recv()
    tabs[3] = tabs[2] + t_got[4] + t_got[5] + t_got[6]
    ts = [go(tabs.at[3], t_got.at[6 + k], "t_x", k, me.x_peer(k)) for k in (1, 3, 2)]
    for copy in aq:
        copy.wait_recv()
    total = a_mid2[rows(me.q, 32), :].astype(F32)
    for k in range(3):
        total = total + a_q[k].astype(F32)
    a_last[...] = total
    a_out_ref[...] = total
    ax = [go(a_last.at[rows(me.x_of(k), 8)], b_ref.at[me.x], "a_x", k, me.x_peer(k)) for k in (1, 3, 2)]
    b_ref[me.x] = a_last[rows(me.x, 8), :]

    ys_in.wait_recv()
    gwin_ref[...] = mid_in[me.y].astype(F32) + y_in[...].astype(F32)
    for copy in xs_out:
        copy.wait_recv()
    total = y_out[me.x].astype(F32)
    for k in range(3):
        total = total + x_out[k].astype(F32)
    gwout_ref[...] = total
    for copy in ts:
        copy.wait_recv()
    table_ref[...] = tabs[3] + t_got[7] + t_got[8] + t_got[9]
    for copy in ax:
        copy.wait_recv()
    for copy in started:
        copy.wait_send()
    for rel, y in ((0, 1 - me.y), (1, me.y)):
        for xx in range(4):
            core_copy(rel, xx, y).wait_send()
    for xx in range(4):
        to_y(xx).wait_send()


SEM_Y_OUT = 60
SEMS = 64


def backward(p, q, kv, own, inv, da, norm, gmix, small, inputs, gain, w, gmid, gwi, gwo):
    shape = jax.ShapeDtypeStruct
    return pl.pallas_call(
        backward_kernel,
        out_shape=(
            shape((TOK, WIDTH), F32),
            shape((48, FF), F32),
            shape((192, WIDTH), F32),
            shape((4, 8, WIDTH), F32),
            shape((32, WIDTH), F32),
            shape((BUCKETS, 128), F32),
        ),
        in_specs=[VMEM] * 13 + [ANY] * 2,
        out_specs=(VMEM,) * 6,
        scratch_shapes=[
            pltpu.VMEM((1536, 256), BF16),
            pltpu.VMEM((1536, 256), BF16),
            pltpu.VMEM((128, 512), F32),
            pltpu.VMEM((3, 5, 128, 128), F32),
            pltpu.VMEM((256, 1536), BF16),
            pltpu.VMEM((256, 1536), F32),
            pltpu.VMEM((2048, 384), BF16),
            pltpu.VMEM((8, TOK, 384), BF16),
            pltpu.VMEM((4, TOK, 384), BF16),
            pltpu.VMEM((4, TOK, 384), BF16),
            pltpu.VMEM((512, 384), BF16),
            pltpu.VMEM((512, 256), BF16),
            pltpu.VMEM((4, TOK, 256), BF16),
            pltpu.VMEM((4, TOK, 384), BF16),
            pltpu.VMEM((512, WIDTH), BF16),
            pltpu.VMEM((3, TOK, WIDTH), BF16),
            pltpu.VMEM((1024, WIDTH), F32),
            pltpu.VMEM((1024, WIDTH), BF16),
            pltpu.VMEM((512, WIDTH), BF16),
            pltpu.VMEM((512, WIDTH), BF16),
            pltpu.VMEM((3, 128, WIDTH), BF16),
            pltpu.VMEM((128, WIDTH), BF16),
            pltpu.VMEM((3, 32, WIDTH), BF16),
            pltpu.VMEM((32, WIDTH), F32),
            pltpu.VMEM((128, WIDTH), F32),
            pltpu.VMEM((3, BUCKETS, 128), F32),
            pltpu.VMEM((4, BUCKETS, 128), F32),
            pltpu.VMEM((10, BUCKETS, 128), F32),
            pltpu.VMEM((8, 48, FF), BF16),
            pltpu.VMEM((8, 192, WIDTH), BF16),
            pltpu.VMEM((8, 48, FF), BF16),
            pltpu.VMEM((8, 192, WIDTH), BF16),
            pltpu.VMEM((3, 2, 48, FF), BF16),
            pltpu.VMEM((2, 48, FF), BF16),
            pltpu.VMEM((48, FF), BF16),
            pltpu.VMEM((4, 192, WIDTH), BF16),
            pltpu.VMEM((3, 192, WIDTH), BF16),
            pltpu.SemaphoreType.DMA((2,)),
            pltpu.SemaphoreType.DMA((SEMS,)),
            pltpu.SemaphoreType.DMA((SEMS,)),
        ],
        compiler_params=pltpu.CompilerParams(
            collective_id=2, has_side_effects=True, vmem_limit_bytes=VMEM_LIMIT
        ),
    )(p, q, kv, own, inv, da, norm, gmix, small, inputs, gain, w, gmid, gwi, gwo)


def body(
    block_input, gain_one, qkv_weight, out_weight, rel_table, gain_two, router_weight, routes, w_in, w_out, cotangent
):
    inputs = block_input[0]
    att, own, q, kv, p, inv, norm = forward(inputs, gain_one[None], qkv_weight, rel_table)
    y, gmid, gmix, small, da, gwi, gwo = expert(
        att, inputs, out_weight, gain_two[None], router_weight, routes[0], w_in, w_out, cotangent[0]
    )
    gin, gwin, gwout, b, a, table = backward(
        p, q, kv, own, inv, da, norm, gmix, small, inputs, gain_one[None], qkv_weight, gmid,
        gwi.reshape(8, 2, 48, FF), gwo.reshape(8, 2, 192, WIDTH),
    )
    b = b[:, :6]

    def columns(*spans):
        part = jnp.concatenate([b[:, :, s : s + n] for s, n in spans], axis=2)
        return jnp.transpose(part, (1, 0, 2)).reshape(6, WIDTH)

    grad_qkv = jnp.stack([columns((0, 192)), columns((256, 192)), columns((512, 128), (448, 64))])
    grad_out = a.reshape(4, 8, WIDTH)[:3, 6:].reshape(6, WIDTH)
    total = jnp.sum(b[:, :, 640:], axis=0)
    return (
        y[None],
        gin[None],
        total[:, 0],
        grad_qkv,
        grad_out,
        table[:, :HEADS],
        total[:, 1],
        total[:, 8:16],
        gwin[None],
        gwout[None],
    )


def solution(mesh):
    tokens = P("expert", "ctx", None)
    split = P(("ctx", "expert"))
    return jax.shard_map(
        body,
        mesh=mesh,
        in_specs=(
            tokens, P(), P(), P(), P(), P(), P(), tokens, P("expert", None, None), P("expert", None, None), tokens,
        ),
        out_specs=(
            tokens, tokens, split, P(None, ("ctx", "expert"), None), split, P(), split, split, tokens, tokens,
        ),
        check_vma=False,
    )
```

```python
import jax
import jax.numpy as jnp
import numpy as np
from jax import lax
from jax.experimental import pallas as pl
from jax.experimental.pallas import tpu as pltpu
from jax.sharding import PartitionSpec as P

HEADS = 12
HEAD_DIM = 64
BUCKETS = 32
MAX_DISTANCE = 128
EPSILON = 1e-06
SCALE = HEAD_DIM ** (-0.5)
TOK = 128
WIDTH = 768
FF = 3072
CAP = 24
F32 = jnp.float32
BF16 = jnp.bfloat16
MESH = pl.DeviceIdType.MESH
VMEM = pl.BlockSpec(memory_space=pltpu.VMEM)
SMEM = pl.BlockSpec(memory_space=pltpu.SMEM)
ANY = pl.BlockSpec(memory_space=pl.ANY)
VMEM_LIMIT = 63 * 1024 * 1024


def bucket_edges(buckets, reach):
    half = buckets // 2
    exact = half // 2
    spans = np.arange(1, reach + 1)
    spread = np.log(np.maximum(spans, exact) / exact) / np.log(reach / exact) * (half - exact)
    large = np.minimum(exact + spread.astype(np.int64), half - 1)
    level = np.where(spans < exact, spans, large)
    return [int(np.argmax(level >= b)) + 1 for b in range(1, half)]


EDGES = bucket_edges(BUCKETS, MAX_DISTANCE)


def dot(a, b):
    return jnp.dot(a, b, preferred_element_type=F32)


def dot_nt(a, b):
    return lax.dot_general(a, b, (((1,), (1,)), ((), ())), preferred_element_type=F32)


def dot_tn(a, b):
    return lax.dot_general(a, b, (((0,), (0,)), ((), ())), preferred_element_type=F32)


def iota(shape, dim):
    return lax.broadcasted_iota(jnp.int32, shape, dim)


class Place:
    def __init__(self):
        self.i = lax.axis_index("ctx")
        self.e = lax.axis_index("expert")
        self.x = lax.div(self.i, 4)
        self.y = lax.rem(lax.div(self.i, 2), 2)
        self.c = lax.rem(self.i, 2)
        self.z = lax.div(self.e, 2)
        self.h = lax.rem(self.e, 2)
        self.q = self.h * 2 + self.y

    def x_of(self, step):
        return lax.rem(self.x + 4 + step, 4)

    def x_peer(self, step):
        return (4 * self.x_of(step) + 2 * self.y + self.c, self.e)

    def core_peer(self):
        return (4 * self.x + 2 * self.y + 1 - self.c, self.e)

    def y_peer(self):
        return (4 * self.x + 2 * (1 - self.y) + self.c, self.e)

    def z_of(self, step):
        return lax.rem(self.z + 4 + step, 4)

    def z_peer(self, step):
        return (self.i, 2 * self.z_of(step) + self.h)

    def q_of(self, step):
        return lax.rem(self.q + 4 + step, 4)

    def q_peer(self, step):
        q = self.q_of(step)
        return (4 * self.x + 2 * lax.rem(q, 2) + self.c, 2 * self.z + lax.div(q, 2))

    def corner_peer(self):
        return (4 * self.x + 2 * (1 - self.y) + self.c, 2 * self.z + 1 - self.h)

    def e_of(self, step):
        return lax.rem(self.e + 8 + step, 8)

    def e_peer(self, step):
        return (self.i, self.e_of(step))


def greet(peers):
    barrier = pltpu.get_barrier_semaphore()
    for peer in peers:
        pl.semaphore_signal(barrier, inc=1, device_id=peer, device_id_type=MESH)
    pl.semaphore_wait(barrier, len(peers))


def rcopy(src, dst, send, recv, slot, peer):
    return pltpu.make_async_remote_copy(
        src_ref=src,
        dst_ref=dst,
        send_sem=send.at[slot],
        recv_sem=recv.at[slot],
        device_id=peer,
        device_id_type=MESH,
    )


def rows(index, size):
    return pl.ds(pl.multiple_of(index * size, size), size)


def pair(first, half_first, second, half_second):
    if first is second and (half_first, half_second) == (0, 1):
        return first
    low = pltpu.roll(first, 64, 1) if half_first else first
    high = second if half_second else pltpu.roll(second, 64, 1)
    return jnp.where(iota(low.shape, 1) < 64, low, high)


def norm_places():
    col = iota((1, 1024), 1)
    r = col & 7
    xx = (col >> 3) & 3
    yl = (col >> 5) & 1
    e = (((col >> 7) & 3) << 1) + ((col >> 6) & 1)
    c = (col >> 9) & 1
    d = jnp.where(r < 6, 192 * xx + 96 * yl + 48 * c + 6 * e + r, -1)
    return (iota((WIDTH, 1024), 0) == d).astype(F32).astype(BF16)


def att_places(group):
    col = iota((1, 1024), 1)
    r = col & 7
    e = (((col >> 7) & 3) << 1) + ((col >> 6) & 1)
    f = 96 * ((col >> 5) & 1) + 48 * ((col >> 9) & 1) + 6 * e + r
    f = jnp.where((r < 6) & (((col >> 3) & 3) == group), f, -1)
    lane = iota((256, 1024), 0)
    feature = jnp.where(lane >= 128, lane - 128, jnp.where(lane >= 64, lane + 64, -2))
    return (feature == f).astype(F32).astype(BF16)


def bucket_tile(offset):
    length = jnp.abs(offset)
    level = jnp.where(offset > 0, BUCKETS // 2, 0)
    for edge in EDGES:
        level = level + (length >= edge).astype(jnp.int32)
    return level


SEMS = 192


class Mail:
    def __init__(self, send, recv):
        self.send, self.recv, self.used, self.started = send, recv, 0, []

    def block(self, count):
        base = self.used
        self.used += count
        assert self.used <= SEMS
        return base

    def copy(self, src, dst, slot, peer):
        return rcopy(src, dst, self.send, self.recv, slot, peer)

    def go(self, src, dst, slot, peer):
        copy = self.copy(src, dst, slot, peer)
        copy.start()
        self.started.append(copy)
        return copy

    def sent(self, copy):
        copy.wait_send()
        self.started = [other for other in self.started if other is not copy]

    def go_later(self, make):
        copy = Made(lambda: self.copy(*make()))
        copy.make().start()
        self.started.append(copy)
        return copy


class Made:
    def __init__(self, make):
        self.make = make

    def wait_recv(self):
        self.make().wait_recv()

    def wait_send(self):
        self.make().wait_send()


def wait_all(copies):
    for copy in copies:
        copy.wait_recv()


def layer_kernel(
    inp_ref, gain1_ref, w_ref, table_ref, out_w_ref, gain2_ref, router_ref, routes_ref, w_in_hbm, w_out_hbm, cot_ref,
    y_ref, gin_ref, gwin_ref, gwout_ref, gqkv_ref, gout_ref, gain_ref, gtable_ref,
    norm_all, norm_own, q_all, kv, qexp, p_ref, scale, own, att,
    middle, select, rows_out, rows_got, back_got, gwi, gwo, gmid, gmix, da_send, da,
    core_kv, y_kv, home_q, home_kv, small,
    o_core, o_z, o_mid2, o_q, o_last, o_x,
    q_core, q_z, q_mid2, q_q, q_last, q_x,
    k_core, k_z, k_mid2, k_q, k_last, k_x,
    trow, tabs, t_got, got_in, got_out, x_far, x_near, y_in, y_out, z_far, z_near,
    local, send, recv,
):
    me = Place()
    mail = Mail(send, recv)
    near = [1, 3, 2]
    others = [1, 7, 2, 6, 3, 5, 4]
    barrier = pltpu.get_barrier_semaphore()
    peers = [me.x_peer(k) for k in near] + [me.core_peer(), me.y_peer(), me.corner_peer()]
    peers = peers + [me.e_peer(k) for k in others]
    for peer in peers:
        pl.semaphore_signal(barrier, inc=1, device_id=peer, device_id_type=MESH)

    inputs = inp_ref[...].astype(F32)
    root1 = lax.rsqrt(jnp.mean(inputs * inputs, axis=1, keepdims=True) + EPSILON)
    normed = (inputs * root1 * gain1_ref[...].reshape(1, WIDTH)).astype(BF16)
    proj = [dot(normed, w_ref[p]) for p in range(3)]

    def join(p, a, s, b):
        first = proj[p][:, 128 * (a // 2) : 128 * (a // 2) + 128]
        second = first if (p == s and a // 2 == b // 2) else proj[s][:, 128 * (b // 2) : 128 * (b // 2) + 128]
        return pair(first, a % 2, second, b % 2)

    block = rows(me.i, TOK)
    mine = rows(me.x, TOK)
    s_kv, s_q, s_y, s_c, s_f = [mail.block(4) for _ in range(5)]
    def source(step, y, c):
        return rows(4 * me.x_of(-step) + 2 * y + c, TOK)

    ys, cs = {}, {}

    def pass_on(step):
        def to(slot, peer):
            part = kv.at[source(step, me.y, me.c)]
            return part, part, slot + step, peer()

        ys[step] = mail.go_later(lambda: to(s_y, me.y_peer))
        cs[step] = mail.go_later(lambda: to(s_c, me.core_peer))

    tile = iota((128, 128), 0) - iota((128, 128), 1)
    lanes = iota((512, 256), 1)
    def attention(s_ref, bias, m_ref, l_ref, acc, o_part, o_t, kv_send, q_send):
        for g in range(4):
            a = 3 * g
            kv_send[g, :, pl.ds(0, 128)] = join(1, a, 1, a + 1).astype(BF16)
            kv_send[g, :, pl.ds(128, 128)] = join(1, a + 2, 2, a + 2).astype(BF16)
            kv_send[g, :, pl.ds(256, 128)] = join(2, a, 2, a + 1).astype(BF16)
            q_send[g, :, pl.ds(0, 128)] = join(0, a, 0, a + 1).astype(BF16)
            q_send[g, :, pl.ds(128, 128)] = jnp.where(iota((TOK, 128), 1) < 64, join(0, a + 2, 0, a + 2), 0.0).astype(BF16)
        pl.semaphore_wait(barrier, len(peers))
        kvs = {k: mail.go(kv_send.at[me.x_of(k)], kv.at[block], s_kv + k, me.x_peer(k)) for k in near}
        kv[block, :] = kv_send[me.x]
        qs = {k: mail.go(q_send.at[me.x_of(k)], q_all.at[mine], s_q + k, me.x_peer(k)) for k in near}
        q_all[mine, :] = q_send[me.x]

        pass_on(0)
        norm_own[...] = dot(normed, norm_places()).astype(BF16)
        norm_all[mine, :] = norm_own[...]
        for h in range(3):
            head = 3 * me.x + h

            def chain(first, n):
                value = jnp.full((128, 128), 1.0, F32) * table_ref[head, first]
                for level, edge in enumerate(EDGES):
                    value = jnp.where(n >= edge, table_ref[head, first + level + 1], value)
                return value

            bias[h, 0] = jnp.full((128, 128), 1.0, F32) * table_ref[head, BUCKETS // 2 - 1]
            bias[h, 1] = chain(0, 128 - tile)
            bias[h, 2] = jnp.where(tile > 0, chain(BUCKETS // 2, tile), chain(0, -tile))
            bias[h, 3] = chain(BUCKETS // 2, 128 + tile)
            bias[h, 4] = jnp.full((128, 128), 1.0, F32) * table_ref[head, BUCKETS - 1]
        m_ref[...] = jnp.full(m_ref.shape, -jnp.inf, F32)
        l_ref[...] = jnp.zeros(l_ref.shape, F32)
        wait_all(qs.values())
        queries = q_all[...].astype(F32) * SCALE
        for h in range(3):
            inside = (lanes >= 64 * h) & (lanes < 64 * h + 64)
            qexp[pl.ds(512 * h, 512), :] = jnp.where(inside, queries, 0.0).astype(BF16)

        def score(first, last, half, y, c):
            def one(step, carry):
                xx = me.x_of(-step)
                b = 4 * xx + 2 * y + c
                keys = kv[rows(b, TOK), pl.ds(0, 256)]
                for h in range(3):
                    s = dot_nt(keys, qexp[pl.ds(512 * h, 512), :])
                    for t in range(4):
                        kind = jnp.clip(b - (4 * t + 2 * me.y + me.c), -2, 2) + 2
                        part = s[:, 128 * t : 128 * t + 128] + bias[h, kind]
                        cols = pl.ds(128 * t, 128)
                        s_ref[h, rows(2 * xx + c, TOK), cols] = part
                        m_ref[half, h, :, cols] = jnp.maximum(
                            m_ref[half, h, :, cols], jnp.max(part.reshape(16, 8, 128), axis=0)
                        )
                return carry

            lax.fori_loop(first, last, one, 0)

        def weigh(half, y):
            for h in range(3):
                top = jnp.max(m_ref[half, h], axis=0, keepdims=True)
                acc[...] = jnp.zeros(acc.shape, F32)

                def one(xx, carry):
                    part = jnp.exp(s_ref[h, rows(xx, 256), :] - top)
                    l_ref[half, h] += jnp.sum(part.reshape(32, 8, 512), axis=0)
                    low = part.astype(BF16)
                    span = rows(2 * xx + y, 256)
                    p_ref[span, pl.ds(512 * h, 512)] = low
                    acc[...] += dot_tn(kv[span, pl.ds(128, 256)], low)
                    return carry

                lax.fori_loop(0, 4, one, 0)
                at = pl.ds((128, 192, 64)[h], 64)
                o_part[half, at, :] = acc[at, :]

        score(0, 1, 0, me.y, me.c)
        for k in near:
            kvs[k].wait_recv()
            pass_on(k)
        score(1, 4, 0, me.y, me.c)
        for k in range(4):
            cs[k].wait_recv()
        score(0, 4, 0, me.y, 1 - me.c)
        fs = {}
        for k in (0, 1, 3, 2):
            ys[k].wait_recv()

            def to(k=k):
                part = kv.at[source(k, 1 - me.y, me.c)]
                return part, part, s_f + k, me.core_peer()

            fs[k] = mail.go_later(to)
        weigh(0, me.y)
        score(0, 4, 1, 1 - me.y, me.c)
        wait_all(fs.values())
        score(0, 4, 1, 1 - me.y, 1 - me.c)
        weigh(1, 1 - me.y)

        factors = jnp.zeros((128, 512), F32)
        which = iota((128, 512), 0)
        o_t[...] = jnp.zeros(o_t.shape, F32)
        for h in range(3):
            tops = [jnp.max(m_ref[half, h], axis=0, keepdims=True) for half in range(2)]
            top = jnp.maximum(tops[0], tops[1])
            fade = [jnp.exp(t - top) for t in tops]
            sums = [jnp.sum(l_ref[half, h], axis=0, keepdims=True) for half in range(2)]
            inv = 1.0 / (sums[0] * fade[0] + sums[1] * fade[1])
            fade = [f * inv for f in fade]
            at = pl.ds((128, 192, 64)[h], 64)
            o_t[at, :] = o_part[0, at, :] * fade[0] + o_part[1, at, :] * fade[1]
            for half in range(2):
                factors = jnp.where(which == 3 * half + h, fade[half], factors)
        scale[...] = factors.T
        own[...] = o_t[...].T.astype(BF16)
        for copy in list(kvs.values()) + list(qs.values()):
            mail.sent(copy)

    pl.run_scoped(
        attention,
        pltpu.VMEM((3, 1024, 512), F32),
        pltpu.VMEM((3, 5, 128, 128), F32),
        pltpu.VMEM((2, 3, 8, 512), F32),
        pltpu.VMEM((2, 3, 8, 512), F32),
        pltpu.VMEM((256, 512), F32),
        pltpu.VMEM((2, 256, 512), F32),
        pltpu.VMEM((256, 512), F32),
        pltpu.VMEM((4, TOK, 384), BF16),
        pltpu.VMEM((4, TOK, 256), BF16),
    )
    s_o, s_n = mail.block(4), mail.block(4)
    os = [mail.go(own.at[rows(me.x_of(k), TOK)], att.at[me.x], s_o + k, me.x_peer(k)) for k in near]
    ns = [mail.go(norm_own, norm_all.at[mine], s_n + k, me.x_peer(k)) for k in near]
    att[me.x] = own[mine, :]

    s_there, s_home = mail.block(8), mail.block(8)
    gain2 = gain2_ref[...].reshape(1, WIDTH)
    slots = rows(me.e, 2 * CAP)
    keep = {}

    def experts(hidden, ginner, made, garr, arrived, gprod):
        load_in = pltpu.make_async_copy(w_in_hbm, gwi, local.at[0])
        load_in.start()
        load_out = pltpu.make_async_copy(w_out_hbm, gwo, local.at[1])
        load_out.start()
        wait_all(os)
        mixed = inputs
        for g in range(4):
            mixed = mixed + dot(att[g, :, pl.ds(0, 128)], out_w_ref[pl.ds(192 * g + 64, 128), :])
            mixed = mixed + dot(att[g, :, pl.ds(128, 128)], out_w_ref[pl.ds(192 * g, 128), :])
        middle[...] = mixed
        root = lax.rsqrt(jnp.mean(mixed * mixed, axis=1, keepdims=True) + EPSILON)
        normed_two = (mixed * root * gain2).astype(BF16)
        logits = dot_nt(normed_two, router_ref[...])
        shifted = jnp.exp(logits - jnp.max(logits, axis=1, keepdims=True))
        router = shifted / jnp.sum(shifted, axis=1, keepdims=True)
        diagonal = iota((TOK, TOK), 0) == iota((TOK, TOK), 1)
        named = jnp.sum(jnp.where(diagonal, routes_ref[...].astype(F32), 0.0), axis=1, keepdims=True).astype(jnp.int32)
        chosen = (named == iota((TOK, 8), 1)).astype(F32)
        gate = jnp.sum(chosen * router, axis=1, keepdims=True)
        earlier = (iota((TOK, TOK), 0) > iota((TOK, TOK), 1)).astype(F32).astype(BF16)
        ranks = dot(earlier, chosen.astype(BF16))
        slot = jnp.sum(chosen * ranks, axis=1, keepdims=True).astype(jnp.int32)
        target = named * (2 * CAP) + slot
        column = iota((TOK, 16 * CAP), 1)
        select[pl.ds(0, TOK), :] = (column == target).astype(F32).astype(BF16)
        select[pl.ds(TOK, TOK), :] = (column == target + CAP).astype(F32).astype(BF16)
        dy = cot_ref[...].astype(F32)
        both = jnp.concatenate([normed_two, (gate * dy).astype(BF16)], axis=0)
        rows_out[...] = dot_tn(select[...], both).astype(BF16)
        there = [
            mail.go_later(
                lambda k=k: (rows_out.at[rows(me.e_of(k), 2 * CAP)], rows_got.at[slots], s_there + k, me.e_peer(k))
            )
            for k in others
        ]
        rows_got[slots, :] = rows_out[slots, :]
        made[...] = jnp.zeros(made.shape, F32)
        garr[...] = jnp.zeros(garr.shape, F32)
        load_in.wait()
        load_out.wait()
        wait_all(there)
        got = rows_got[...].astype(F32).reshape(8, 2 * CAP, WIDTH)
        arrived[...] = got[:, :CAP].reshape(8 * CAP, WIDTH).astype(BF16)
        gprod[...] = got[:, CAP:].reshape(8 * CAP, WIDTH).astype(BF16)
        chunk = 768

        def through(j, carry):
            cols = rows(j, chunk)
            for k in range(3):
                part = rows(3 * j + k, 256)
                inner = dot(arrived[...], gwi[:, :, :, part].reshape(WIDTH, 256))
                square = inner * inner
                slope = np.float32(np.sqrt(2 / np.pi))
                t = jnp.tanh(slope * inner * (1.0 + 0.044715 * square))
                half = 0.5 * (1.0 + t)
                hidden[:, part] = (inner * half).astype(BF16)
                w_out = gwo[pl.ds(2 * j, 2)].reshape(chunk, WIDTH)[256 * k : 256 * k + 256]
                back = dot_nt(gprod[...], w_out)
                lean = half + 0.5 * inner * (1.0 - t * t) * slope * (1.0 + 3 * 0.044715 * square)
                ginner[:, part] = (lean * back).astype(BF16)
            made[...] += dot(hidden[:, cols], gwo[pl.ds(2 * j, 2)].reshape(chunk, WIDTH))
            garr[...] += dot_nt(ginner[:, cols], gwi[:, :, :, cols].reshape(WIDTH, chunk))
            return carry

        lax.fori_loop(0, FF // chunk, through, 0)
        back = jnp.concatenate([made[...].reshape(8, CAP, WIDTH), garr[...].reshape(8, CAP, WIDTH)], axis=1)
        for copy in there:
            mail.sent(copy)
        rows_out[...] = back.reshape(16 * CAP, WIDTH).astype(BF16)
        keep["home"] = [
            mail.go_later(
                lambda k=k: (rows_out.at[rows(me.e_of(k), 2 * CAP)], back_got.at[slots], s_home + k, me.e_peer(k))
            )
            for k in others
        ]
        back_got[slots, :] = rows_out[slots, :]

        def grads_in(j, carry):
            cols = rows(j, 256)
            gwi[:, :, :, cols] = dot_tn(arrived[...], ginner[:, cols]).astype(BF16).reshape(8, 2, 48, 256)
            return carry

        lax.fori_loop(0, FF // 256, grads_in, 0)
        s_in = mail.block(1)
        keep["core_in"] = mail.go_later(lambda: (gwi.at[:, 1 - me.c], got_in, s_in, me.core_peer()))

        def grads_out(j, carry):
            gwo[j] = dot_tn(hidden[:, rows(j, 384)], gprod[...]).astype(BF16).reshape(2, 192, WIDTH)
            return carry

        lax.fori_loop(0, 8, grads_out, 0)
        s_out = mail.block(1)
        keep["core_out"] = mail.go_later(lambda: (gwo.at[:, 1 - me.c], got_out, s_out, me.core_peer()))
        return gate, chosen, router, root, normed_two

    gate, chosen, router, root, normed_two = pl.run_scoped(
        experts,
        pltpu.VMEM((8 * CAP, FF), BF16),
        pltpu.VMEM((8 * CAP, FF), BF16),
        pltpu.VMEM((8 * CAP, WIDTH), F32),
        pltpu.VMEM((8 * CAP, WIDTH), F32),
        pltpu.VMEM((8 * CAP, WIDTH), BF16),
        pltpu.VMEM((8 * CAP, WIDTH), BF16),
    )

    keep["core_in"].wait_recv()

    def add_in(j, carry):
        gwi[j, me.c] = (gwi[j, me.c].astype(F32) + got_in[j].astype(F32)).astype(BF16)
        return carry

    lax.fori_loop(0, 8, add_in, 0)
    s_far, s_ring = mail.block(2), mail.block(4)
    right, left = me.x_of(1), me.x_of(3)
    far = me.x_of(2)
    fars = [
        mail.go(gwi.at[2 * far, me.c], x_far.at[0], s_far, me.x_peer(1)),
        mail.go(gwi.at[2 * far + 1, me.c], x_far.at[1], s_far + 1, me.x_peer(3)),
    ]
    ring = [
        mail.go(gwi.at[2 * right + 1, me.c], x_near.at[1], s_ring, me.x_peer(1)),
        mail.go(gwi.at[2 * left, me.c], x_near.at[2], s_ring + 1, me.x_peer(3)),
    ]

    wait_all(keep["home"])
    returned = dot(select[pl.ds(0, TOK), :], back_got[...])
    gnorm = dot(select[pl.ds(TOK, TOK), :], back_got[...])
    mid = middle[...]
    dy = cot_ref[...].astype(F32)
    y_ref[...] = (mid + gate * returned).astype(BF16)
    ggate = jnp.sum(dy * returned, axis=1, keepdims=True)
    glogits = ggate * gate * (chosen - router)
    high = glogits.astype(BF16)
    rest = (glogits - high.astype(F32)).astype(BF16)
    gnorm = gnorm + dot(high, router_ref[...]) + dot(rest, router_ref[...])
    small[...] = jnp.zeros(small.shape, F32)
    small[pl.ds(8, 8), :] = dot_tn(high, normed_two) + dot_tn(rest, normed_two)
    small[pl.ds(0, 1), :] = jnp.sum(gnorm * mid * root, axis=0, keepdims=True)
    u = gain2 * gnorm
    gmiddle = dy + root * u - mid * (root * root * root * jnp.mean(u * mid, axis=1, keepdims=True))
    gmid[...] = gmiddle
    gmix[...] = gmiddle.astype(BF16)
    upper = iota((TOK, 128), 1) >= 64
    for g in range(4):
        front = dot_nt(gmix[...], out_w_ref[pl.ds(192 * g + 64, 128), :])
        da_send[g, :, pl.ds(0, 128)] = jnp.where(upper, front, 0.0).astype(BF16)
        da_send[g, :, pl.ds(128, 128)] = dot_nt(gmix[...], out_w_ref[pl.ds(192 * g, 128), :]).astype(BF16)
    s_da = mail.block(4)
    das = [mail.go(da_send.at[me.x_of(k)], da.at[mine], s_da + k, me.x_peer(k)) for k in near]
    da[mine, :] = da_send[me.x]

    def rest(doexp, drow, accb, ds, dq, dkv, y_send, fin_kv, fin_q, dproj, o_low, q_low, k_low):
        att_wide = dot(att[0], att_places(0))
        for g in range(1, 4):
            att_wide = att_wide + dot(att[g], att_places(g))
        att_wide = att_wide.astype(BF16)
        for part in range(4):
            block_rows = dot_tn(att_wide[:, 256 * part : 256 * part + 256], gmix[...]).astype(BF16)
            o_low[part // 2, pl.ds(2 * (part % 2), 2), :, :, pl.ds(0, WIDTH)] = block_rows.reshape(2, 4, 32, WIDTH)
        tiny = dot(small[...].astype(BF16), norm_places()).T.astype(BF16)
        o_low[:, :, :, :, pl.ds(WIDTH, 128)] = tiny.reshape(2, 4, 4, 32, 128)
        core_o = mail.go(o_low.at[1 - me.c], o_core, mail.block(1), me.core_peer())

        keep["core_out"].wait_recv()

        def add_out(j, carry):
            gwo[j, me.c] = (gwo[j, me.c].astype(F32) + got_out[j].astype(F32)).astype(BF16)
            return carry

        lax.fori_loop(0, 8, add_out, 0)
        s_yo = mail.block(4)
        ys_out = [
            mail.go(gwo.at[2 * xx + 1 - me.y, me.c], y_out.at[xx], s_yo + xx, me.y_peer()) for xx in range(4)
        ]
        wait_all(fars)
        near_right = gwi.at[2 * right, me.c]
        near_right[...] = (near_right[...].astype(F32) + x_far[0].astype(F32)).astype(BF16)
        near_left = gwi.at[2 * left + 1, me.c]
        near_left[...] = (near_left[...].astype(F32) + x_far[1].astype(F32)).astype(BF16)
        ring_all = ring + [
            mail.go(near_right, x_near.at[0], s_ring + 2, me.x_peer(1)),
            mail.go(near_left, x_near.at[3], s_ring + 3, me.x_peer(3)),
        ]

        wait_all(das)
        grads = da[...].astype(F32)
        product = grads * own[...].astype(F32)
        sums = jnp.zeros((512, 128), F32)
        for h in range(3):
            at = (128, 192, 64)[h]
            inside = (lanes >= at) & (lanes < at + 64)
            total = jnp.sum(jnp.where(inside, product, 0.0), axis=1, keepdims=True)
            for half in range(2):
                factor = scale[:, pl.ds(3 * half + h, 1)]
                sums = jnp.where(iota((512, 128), 1) == 3 * half + h, total * factor, sums)
        drow[...] = sums.T
        accb[...] = jnp.zeros(accb.shape, F32)
        dq[...] = jnp.zeros(dq.shape, F32)
        s_ckv, s_ykv = mail.block(8), mail.block(4)

        def core_copy(rel, xx, y):
            part = rows(4 * xx + 2 * y + 1 - me.c, TOK)
            return mail.copy(dkv.at[part], core_kv.at[4 * rel + xx], s_ckv + 4 * rel + xx, me.core_peer())

        def attend(rel, y):
            half = 1 - rel
            for h in range(3):
                at = (128, 192, 64)[h]
                inside = (lanes >= at) & (lanes < at + 64)
                kept = jnp.where(inside, da[...].astype(F32), 0.0) * scale[:, pl.ds(3 * half + h, 1)]
                doexp[pl.ds(512 * h, 512), :] = kept.astype(BF16)

            def one(xx, carry):
                span = rows(2 * xx + y, 256)
                keys = kv[span, pl.ds(0, 256)]
                values = kv[span, pl.ds(128, 256)]
                for h in range(3):
                    cols = pl.ds(512 * h, 512)
                    back = dot_nt(values, doexp[cols, :])
                    part = p_ref[span, cols].astype(F32) * (back - drow[pl.ds(3 * half + h, 1), :])
                    ds[:, cols] = part.astype(BF16)
                    for k in range(2):
                        for t in range(4):
                            kind = jnp.clip(4 * xx + 2 * y + k - (4 * t + 2 * me.y + me.c), -2, 2) + 2
                            accb[h, kind] += part[128 * k : 128 * k + 128, 128 * t : 128 * t + 128]
                for h in range(3):
                    cols = pl.ds(512 * h, 512)
                    dq[pl.ds(64 * h, 64), :] += dot_tn(keys, ds[:, cols])[64 * h : 64 * h + 64]
                gk = dot(ds[...], qexp[...])
                gv = dot(p_ref[span, :], doexp[...])
                dkv[span, pl.ds(0, 128)] = gk[:, :128].astype(BF16)
                dkv[span, pl.ds(128, 128)] = (gk[:, 128:] + gv[:, :128]).astype(BF16)
                dkv[span, pl.ds(256, 128)] = gv[:, 128:].astype(BF16)
                core_copy(rel, xx, y).start()
                return carry

            lax.fori_loop(0, 4, one, 0)

        attend(0, 1 - me.y)

        def to_y(xx):
            return mail.copy(y_send.at[xx], y_kv.at[xx], s_ykv + xx, me.y_peer())

        def forward_y(xx, carry):
            core_copy(0, xx, 1 - me.y).wait_recv()
            part = dkv[rows(4 * xx + 2 * (1 - me.y) + me.c, TOK), :].astype(F32)
            y_send[xx] = (part + core_kv[xx].astype(F32)).astype(BF16)
            to_y(xx).start()
            return carry

        lax.fori_loop(0, 4, forward_y, 0)

        class Sum:
            def __init__(self, low, core, z_got, mid2, q_got, last, x_got, first):
                self.low, self.core, self.z_got = low, core, z_got
                self.mid2, self.q_got, self.last, self.x_got = mid2, q_got, last, x_got
                self.first = first

            def peer(self, axis, k):
                return me.z_peer(k) if axis == "z" else me.q_peer(k)

            def of(self, axis, k):
                return me.z_of(k) if axis == "z" else me.q_of(k)

            def begin(self):
                self.copies = [mail.go(self.low.at[1 - me.c], self.core, mail.block(1), me.core_peer())]

            def part(self, index):
                return self.low.at[me.c, :, index] if self.first == "q" else self.low.at[me.c, index]

            def stage_one(self):
                wait_all(self.copies)
                total = self.low[me.c].astype(F32) + self.core[...].astype(F32)
                self.low[me.c] = total.astype(BF16)
                base = mail.block(4)
                self.copies = [
                    mail.go(self.part(self.of(self.first, k)), self.z_got.at[k - 1], base + k, self.peer(self.first, k))
                    for k in near
                ]

            def stage_two(self):
                wait_all(self.copies)
                total = self.part(me.q if self.first == "q" else me.z)[...].astype(F32)
                for k in range(3):
                    total = total + self.z_got[k].astype(F32)
                self.mid2[...] = total.astype(BF16)
                base = mail.block(4)
                second = "z" if self.first == "q" else "q"
                self.copies = [
                    mail.go(self.mid2.at[self.of(second, k)], self.q_got.at[k - 1], base + k, self.peer(second, k))
                    for k in near
                ]

            def stage_three(self):
                wait_all(self.copies)
                total = self.mid2[me.z if self.first == "q" else me.q].astype(F32)
                for k in range(3):
                    total = total + self.q_got[k].astype(F32)
                self.last[...] = total
                base = mail.block(4)
                self.copies = [
                    mail.go(self.last.at[rows(me.x_of(k), 8)], self.x_got.at[me.x], base + k, me.x_peer(k)) for k in near
                ]
                self.x_got[me.x] = self.last[rows(me.x, 8), :]

            def finish(self):
                wait_all(self.copies)

        of_out = Sum(o_low, o_core, o_z, o_mid2, o_q, o_last, o_x, "z")
        of_out.copies = [core_o]
        of_q = Sum(q_low, q_core, q_z, q_mid2, q_q, q_last, q_x, "z")
        of_kv = Sum(k_low, k_core, k_z, k_mid2, k_q, k_last, k_x, "q")
        of_out.stage_one()

        attend(1, me.y)

        fin_q[...] = (dq[...] * SCALE).T.astype(BF16)
        s_xq, s_xkv = mail.block(4), mail.block(4)
        home = [mail.go(fin_q.at[rows(me.x_of(k), TOK)], home_q.at[me.x], s_xq + k, me.x_peer(k)) for k in near]
        home_q[me.x] = fin_q[mine, :]
        wait_all(ns)
        for part in range(4):
            span = pl.ds(256 * part, 256)
            block_rows = dot_tn(norm_all[:, span], fin_q[...]).astype(BF16)
            q_low[part // 2, pl.ds(2 * (part % 2), 2)] = block_rows.reshape(2, 4, 32, fin_q.shape[1])
        of_q.begin()
        for k in near + [0]:
            xx = me.x_of(k)
            core_copy(1, xx, me.y).wait_recv()
            to_y(xx).wait_recv()
            part = dkv[rows(4 * xx + 2 * me.y + me.c, TOK), :].astype(F32)
            part = (part + core_kv[4 + xx].astype(F32) + y_kv[xx].astype(F32)).astype(BF16)
            fin_kv[rows(xx, TOK), :] = part
            if k:
                home.append(mail.go(fin_kv.at[rows(xx, TOK)], home_kv.at[me.x], s_xkv + k, me.x_peer(k)))
            else:
                home_kv[me.x] = part
        for part in range(4):
            span = pl.ds(256 * part, 256)
            block_rows = dot_tn(norm_all[:, span], fin_kv[...]).astype(BF16)
            k_low[part // 2, pl.ds(2 * (part % 2), 2)] = block_rows.reshape(2, 4, 32, fin_kv.shape[1])
        of_kv.begin()
        of_q.stage_one()
        of_out.stage_two()

        of_kv.stage_one()
        before, center, after = bucket_tile(tile - 128), bucket_tile(tile), bucket_tile(tile + 128)

        def bucket_sum(b, carry):
            for h in range(3):
                near_sum = (
                    jnp.where(before == b, accb[h, 1], 0.0)
                    + jnp.where(center == b, accb[h, 2], 0.0)
                    + jnp.where(after == b, accb[h, 3], 0.0)
                )
                trow[h, pl.ds(b, 1), :] = jnp.sum(near_sum, axis=0, keepdims=True)
            return carry

        lax.fori_loop(0, BUCKETS, bucket_sum, 0)
        table = jnp.zeros((BUCKETS, 128), F32)
        for h in range(3):
            trow[h, pl.ds(BUCKETS // 2 - 1, 1), :] += jnp.sum(accb[h, 0], axis=0, keepdims=True)
            trow[h, pl.ds(BUCKETS - 1, 1), :] += jnp.sum(accb[h, 4], axis=0, keepdims=True)
            total = jnp.sum(trow[h], axis=1, keepdims=True)
            table = jnp.where(iota((BUCKETS, 128), 1) == 3 * me.x + h, total, table)
        tabs[0] = table
        t_core = mail.go(tabs.at[0], t_got.at[0], mail.block(1), me.core_peer())

        wait_all(ring_all)
        for j in range(2):
            total = gwi[2 * me.x + j, me.c].astype(F32) + x_near[j].astype(F32) + x_near[2 + j].astype(F32)
            gwi[2 * me.x + j, me.c] = total.astype(BF16)
        y_hop = mail.go(gwi.at[2 * me.x + 1 - me.y, me.c], y_in, mail.block(1), me.y_peer())
        wait_all(ys_out)
        for xx in range(4):
            y_out[xx] = (gwo[2 * xx + me.y, me.c].astype(F32) + y_out[xx].astype(F32)).astype(BF16)
        s_zf, s_zn = mail.block(2), mail.block(4)
        z_fars = [
            mail.go(y_out.at[far, pl.ds(0, 96)], z_far.at[0], s_zf, me.x_peer(1)),
            mail.go(y_out.at[far, pl.ds(96, 96)], z_far.at[1], s_zf + 1, me.x_peer(3)),
        ]
        z_ring = [
            mail.go(y_out.at[right, pl.ds(96, 96)], z_near.at[1], s_zn, me.x_peer(1)),
            mail.go(y_out.at[left, pl.ds(0, 96)], z_near.at[2], s_zn + 1, me.x_peer(3)),
        ]
        of_q.stage_two()
        of_out.stage_three()
        t_core.wait_recv()
        tabs[1] = tabs[0] + t_got[0]
        s_tz = mail.block(4)
        ts = [mail.go(tabs.at[1], t_got.at[k], s_tz + k, me.z_peer(k)) for k in near]
        of_kv.stage_two()

        wait_all(home)

        def piece(p, j):
            g, t = j // 3, j % 3
            if p == 0:
                return home_q[g, :, pl.ds(128 * (t // 2), 128)].astype(F32), t % 2
            if p == 1:
                return home_kv[g, :, pl.ds(128 * (t // 2), 128)].astype(F32), t % 2
            at, half = ((2, 0), (2, 1), (1, 1))[t]
            return home_kv[g, :, pl.ds(128 * at, 128)].astype(F32), half

        for p in range(3):
            for n in range(6):
                first, half_first = piece(p, 2 * n)
                second, half_second = piece(p, 2 * n + 1)
                dproj[p, :, pl.ds(128 * n, 128)] = pair(first, half_first, second, half_second).astype(BF16)
        gnorm = dot_nt(dproj[0], w_ref[0]) + dot_nt(dproj[1], w_ref[1]) + dot_nt(dproj[2], w_ref[2])
        inputs = inp_ref[...].astype(F32)
        root1 = lax.rsqrt(jnp.mean(inputs * inputs, axis=1, keepdims=True) + EPSILON)
        gain1 = gain1_ref[...].reshape(1, WIDTH)
        u = gain1 * gnorm
        mean = jnp.mean(u * inputs, axis=1, keepdims=True)
        gin_ref[...] = gmid[...] + root1 * u - inputs * (root1 * root1 * root1 * mean)

        of_q.stage_three()
        wait_all(ts)
        tabs[2] = tabs[1] + t_got[1] + t_got[2] + t_got[3]
        s_tq = mail.block(4)
        ts = [mail.go(tabs.at[2], t_got.at[3 + k], s_tq + k, me.q_peer(k)) for k in near]
        wait_all(z_fars)
        y_out[right, pl.ds(0, 96), :] = (
            y_out[right, pl.ds(0, 96), :].astype(F32) + z_far[0].astype(F32)
        ).astype(BF16)
        y_out[left, pl.ds(96, 96), :] = (
            y_out[left, pl.ds(96, 96), :].astype(F32) + z_far[1].astype(F32)
        ).astype(BF16)
        z_ring = z_ring + [
            mail.go(y_out.at[right, pl.ds(0, 96)], z_near.at[0], s_zn + 2, me.x_peer(1)),
            mail.go(y_out.at[left, pl.ds(96, 96)], z_near.at[3], s_zn + 3, me.x_peer(3)),
        ]
        of_kv.stage_three()
        wait_all(ts)
        tabs[3] = tabs[2] + t_got[4] + t_got[5] + t_got[6]
        s_tx = mail.block(4)
        ts = [mail.go(tabs.at[3], t_got.at[6 + k], s_tx + k, me.x_peer(k)) for k in near]

        row = iota((16, WIDTH), 0)
        pick = (iota((16, WIDTH), 1) == 6 * (8 * me.i + me.e) + row) & (row < 6)
        pick = pick.astype(F32).astype(BF16)
        picked = [dot(pick, w_ref[p])[:8] for p in range(3)]
        gain_col = jnp.sum(jnp.where(pick[:8].astype(F32) > 0, gain1, 0.0), axis=1, keepdims=True)

        of_out.finish()
        total = o_x[0] + o_x[1] + o_x[2] + o_x[3]
        gout_ref[...] = total
        y_hop.wait_recv()
        gwin_ref[...] = gwi[2 * me.x + me.y, me.c].astype(F32) + y_in[...].astype(F32)
        wait_all(z_ring)
        gwout_ref[pl.ds(0, 96), :] = (
            y_out[me.x, pl.ds(0, 96), :].astype(F32) + z_near[0].astype(F32) + z_near[2].astype(F32)
        )
        gwout_ref[pl.ds(96, 96), :] = (
            y_out[me.x, pl.ds(96, 96), :].astype(F32) + z_near[1].astype(F32) + z_near[3].astype(F32)
        )
        wait_all(ts)
        gtable_ref[...] = tabs[3] + t_got[7] + t_got[8] + t_got[9]
        of_q.finish()
        of_kv.finish()

        def found(p, j):
            g, t = j // 3, j % 3
            if p == 0:
                return q_x[g, :, pl.ds(128 * (t // 2), 128)], t % 2
            if p == 1:
                return k_x[g, :, pl.ds(128 * (t // 2), 128)], t % 2
            at, half = ((2, 0), (2, 1), (1, 1))[t]
            return k_x[g, :, pl.ds(128 * at, 128)], half

        with_gain = jnp.zeros((8, 1), F32)
        for p in range(3):
            for n in range(6):
                first, half_first = found(p, 2 * n)
                second, half_second = found(p, 2 * n + 1)
                cols = pl.ds(128 * n, 128)
                part = pair(first, half_first, second, half_second)
                gqkv_ref[p, :, cols] = part
                with_gain = with_gain + jnp.sum(
                    part * picked[p][:, 128 * n : 128 * n + 128], axis=1, keepdims=True
                )
        real = iota((8, 1), 0) < 6
        gain_ref[...] = jnp.where(real, with_gain / jnp.where(real, gain_col, 1.0), 0.0) * jnp.ones((8, 128), F32)
        for copy in mail.started:
            copy.wait_send()
        for rel, y in ((0, 1 - me.y), (1, me.y)):
            for xx in range(4):
                core_copy(rel, xx, y).wait_send()
        for xx in range(4):
            to_y(xx).wait_send()

    pl.run_scoped(
        rest,
        pltpu.VMEM((1536, 256), BF16),
        pltpu.VMEM((128, 512), F32),
        pltpu.VMEM((3, 5, 128, 128), F32),
        pltpu.VMEM((256, 1536), BF16),
        pltpu.VMEM((256, 512), F32),
        pltpu.VMEM((2048, 384), BF16),
        pltpu.VMEM((4, TOK, 384), BF16),
        pltpu.VMEM((512, 384), BF16),
        pltpu.VMEM((512, 256), BF16),
        pltpu.VMEM((3, TOK, WIDTH), BF16),
        pltpu.VMEM((2, 4, 4, 32, WIDTH + 128), BF16),
        pltpu.VMEM((2, 4, 4, 32, 256), BF16),
        pltpu.VMEM((2, 4, 4, 32, 384), BF16),
    )


def sum_buffers(width):
    return [
        pltpu.VMEM((4, 4, 32, width), BF16),
        pltpu.VMEM((3, 4, 32, width), BF16),
        pltpu.VMEM((4, 32, width), BF16),
        pltpu.VMEM((3, 32, width), BF16),
        pltpu.VMEM((32, width), F32),
        pltpu.VMEM((4, 8, width), F32),
    ]


def layer(*arrays):
    shape = jax.ShapeDtypeStruct
    vm = pltpu.VMEM
    return pl.pallas_call(
        layer_kernel,
        out_shape=(
            shape((TOK, WIDTH), BF16),
            shape((TOK, WIDTH), F32),
            shape((48, FF), F32),
            shape((192, WIDTH), F32),
            shape((3, 8, WIDTH), F32),
            shape((8, WIDTH + 128), F32),
            shape((8, 128), F32),
            shape((BUCKETS, 128), F32),
        ),
        in_specs=[VMEM] * 3 + [SMEM] + [VMEM] * 4 + [ANY] * 2 + [VMEM],
        out_specs=(VMEM,) * 8,
        scratch_shapes=[
            vm((512, 1024), BF16),
            vm((TOK, 1024), BF16),
            vm((512, 256), BF16),
            vm((2048, 384), BF16),
            vm((1536, 256), BF16),
            vm((2048, 1536), BF16),
            vm((512, 128), F32),
            vm((512, 256), BF16),
            vm((4, TOK, 256), BF16),
            vm((TOK, WIDTH), F32),
            vm((2 * TOK, 16 * CAP), BF16),
            vm((16 * CAP, WIDTH), BF16),
            vm((16 * CAP, WIDTH), BF16),
            vm((16 * CAP, WIDTH), BF16),
            vm((8, 2, 48, FF), BF16),
            vm((8, 2, 192, WIDTH), BF16),
            vm((TOK, WIDTH), F32),
            vm((TOK, WIDTH), BF16),
            vm((4, TOK, 256), BF16),
            vm((512, 256), BF16),
            vm((8, TOK, 384), BF16),
            vm((4, TOK, 384), BF16),
            vm((4, TOK, 256), BF16),
            vm((4, TOK, 384), BF16),
            vm((128, WIDTH), F32),
        ]
        + sum_buffers(WIDTH + 128)
        + sum_buffers(256)
        + sum_buffers(384)
        + [
            vm((3, BUCKETS, 128), F32),
            vm((4, BUCKETS, 128), F32),
            vm((10, BUCKETS, 128), F32),
            vm((8, 48, FF), BF16),
            vm((8, 192, WIDTH), BF16),
            vm((2, 48, FF), BF16),
            vm((4, 48, FF), BF16),
            vm((48, FF), BF16),
            vm((4, 192, WIDTH), BF16),
            vm((2, 96, WIDTH), BF16),
            vm((4, 96, WIDTH), BF16),
            pltpu.SemaphoreType.DMA((2,)),
            pltpu.SemaphoreType.DMA((SEMS,)),
            pltpu.SemaphoreType.DMA((SEMS,)),
        ],
        compiler_params=pltpu.CompilerParams(
            collective_id=0, has_side_effects=True, vmem_limit_bytes=VMEM_LIMIT
        ),
    )(*arrays)


def body(
    block_input, gain_one, qkv_weight, out_weight, rel_table, gain_two, router_weight, routes, w_in, w_out, cotangent
):
    y, gin, gwin, gwout, gqkv, gout, gain, table = layer(
        block_input[0], gain_one, qkv_weight, rel_table.T, out_weight, gain_two, router_weight.T,
        routes.reshape(1, TOK), w_in.reshape(8, 2, 48, FF), w_out.reshape(8, 2, 192, WIDTH), cotangent[0],
    )
    return (
        y[None],
        gin[None],
        gain[:6, 0],
        gqkv[:, :6],
        gout[:6, :WIDTH],
        table[:, :HEADS],
        gout[:6, WIDTH],
        gout[:6, WIDTH + 8 : WIDTH + 16],
        gwin[None],
        gwout[None],
    )


def solution(mesh):
    tokens = P("expert", "ctx", None)
    split = P(("ctx", "expert"))
    return jax.shard_map(
        body,
        mesh=mesh,
        in_specs=(
            tokens, P(), P(), P(), P(), P(), P(), tokens, P("expert", None, None), P("expert", None, None), tokens,
        ),
        out_specs=(
            tokens, tokens, split, P(None, ("ctx", "expert"), None), split, P(), split, split, tokens, tokens,
        ),
        check_vma=False,
    )
```

```python
import jax
import jax.numpy as jnp
import numpy as np
from jax import lax
from jax.experimental import pallas as pl
from jax.experimental.pallas import tpu as pltpu
from jax.sharding import PartitionSpec as P

HEADS = 12
HEAD_DIM = 64
BUCKETS = 32
MAX_DISTANCE = 128
EPSILON = 1e-06
SCALE = HEAD_DIM ** (-0.5)
TOK = 128
WIDTH = 768
FF = 3072
CAP = 24
F32 = jnp.float32
BF16 = jnp.bfloat16
MESH = pl.DeviceIdType.MESH
VMEM = pl.BlockSpec(memory_space=pltpu.VMEM)
SMEM = pl.BlockSpec(memory_space=pltpu.SMEM)
ANY = pl.BlockSpec(memory_space=pl.ANY)
VMEM_LIMIT = 63 * 1024 * 1024


def bucket_edges(buckets, reach):
    half = buckets // 2
    exact = half // 2
    spans = np.arange(1, reach + 1)
    spread = np.log(np.maximum(spans, exact) / exact) / np.log(reach / exact) * (half - exact)
    large = np.minimum(exact + spread.astype(np.int64), half - 1)
    level = np.where(spans < exact, spans, large)
    return [int(np.argmax(level >= b)) + 1 for b in range(1, half)]


EDGES = bucket_edges(BUCKETS, MAX_DISTANCE)


def dot(a, b):
    return jnp.dot(a, b, preferred_element_type=F32)


def dot_nt(a, b):
    return lax.dot_general(a, b, (((1,), (1,)), ((), ())), preferred_element_type=F32)


def dot_tn(a, b):
    return lax.dot_general(a, b, (((0,), (0,)), ((), ())), preferred_element_type=F32)


def iota(shape, dim):
    return lax.broadcasted_iota(jnp.int32, shape, dim)


class Place:
    def __init__(self):
        self.i = lax.axis_index("ctx")
        self.e = lax.axis_index("expert")
        self.x = lax.div(self.i, 4)
        self.y = lax.rem(lax.div(self.i, 2), 2)
        self.c = lax.rem(self.i, 2)
        self.z = lax.div(self.e, 2)
        self.h = lax.rem(self.e, 2)
        self.q = self.h * 2 + self.y

    def x_of(self, step):
        return lax.rem(self.x + 4 + step, 4)

    def x_peer(self, step):
        return (4 * self.x_of(step) + 2 * self.y + self.c, self.e)

    def core_peer(self):
        return (4 * self.x + 2 * self.y + 1 - self.c, self.e)

    def y_peer(self):
        return (4 * self.x + 2 * (1 - self.y) + self.c, self.e)

    def z_of(self, step):
        return lax.rem(self.z + 4 + step, 4)

    def z_peer(self, step):
        return (self.i, 2 * self.z_of(step) + self.h)

    def q_of(self, step):
        return lax.rem(self.q + 4 + step, 4)

    def q_peer(self, step):
        q = self.q_of(step)
        return (4 * self.x + 2 * lax.rem(q, 2) + self.c, 2 * self.z + lax.div(q, 2))

    def corner_peer(self):
        return (4 * self.x + 2 * (1 - self.y) + self.c, 2 * self.z + 1 - self.h)

    def e_of(self, step):
        return lax.rem(self.e + 8 + step, 8)

    def e_peer(self, step):
        return (self.i, self.e_of(step))


def greet(peers):
    barrier = pltpu.get_barrier_semaphore()
    for peer in peers:
        pl.semaphore_signal(barrier, inc=1, device_id=peer, device_id_type=MESH)
    pl.semaphore_wait(barrier, len(peers))


def rcopy(src, dst, send, recv, slot, peer):
    return pltpu.make_async_remote_copy(
        src_ref=src,
        dst_ref=dst,
        send_sem=send.at[slot],
        recv_sem=recv.at[slot],
        device_id=peer,
        device_id_type=MESH,
    )


def rows(index, size):
    return pl.ds(pl.multiple_of(index * size, size), size)


def pair(first, half_first, second, half_second):
    if first is second and (half_first, half_second) == (0, 1):
        return first
    low = pltpu.roll(first, 64, 1) if half_first else first
    high = second if half_second else pltpu.roll(second, 64, 1)
    return jnp.where(iota(low.shape, 1) < 64, low, high)


def norm_places():
    col = iota((1, 1024), 1)
    r = col & 7
    xx = (col >> 3) & 3
    yl = (col >> 5) & 1
    e = (((col >> 7) & 3) << 1) + ((col >> 6) & 1)
    c = (col >> 9) & 1
    d = jnp.where(r < 6, 192 * xx + 96 * yl + 48 * c + 6 * e + r, -1)
    return (iota((WIDTH, 1024), 0) == d).astype(F32).astype(BF16)


def att_places(group):
    col = iota((1, 1024), 1)
    r = col & 7
    e = (((col >> 7) & 3) << 1) + ((col >> 6) & 1)
    f = 96 * ((col >> 5) & 1) + 48 * ((col >> 9) & 1) + 6 * e + r
    f = jnp.where((r < 6) & (((col >> 3) & 3) == group), f, -1)
    lane = iota((256, 1024), 0)
    feature = jnp.where(lane >= 128, lane - 128, jnp.where(lane >= 64, lane + 64, -2))
    return (feature == f).astype(F32).astype(BF16)


def bucket_tile(offset):
    length = jnp.abs(offset)
    level = jnp.where(offset > 0, BUCKETS // 2, 0)
    for edge in EDGES:
        level = level + (length >= edge).astype(jnp.int32)
    return level


SEMS = 192


class Mail:
    def __init__(self, send, recv):
        self.send, self.recv, self.used, self.started = send, recv, 0, []

    def block(self, count):
        base = self.used
        self.used += count
        assert self.used <= SEMS
        return base

    def copy(self, src, dst, slot, peer):
        return rcopy(src, dst, self.send, self.recv, slot, peer)

    def go(self, src, dst, slot, peer):
        copy = self.copy(src, dst, slot, peer)
        copy.start()
        self.started.append(copy)
        return copy

    def sent(self, copy):
        copy.wait_send()
        self.started = [other for other in self.started if other is not copy]

    def go_later(self, make):
        copy = Made(lambda: self.copy(*make()))
        copy.make().start()
        self.started.append(copy)
        return copy


class Made:
    def __init__(self, make):
        self.make = make

    def wait_recv(self):
        self.make().wait_recv()

    def wait_send(self):
        self.make().wait_send()


def wait_all(copies):
    for copy in copies:
        copy.wait_recv()


def layer_kernel(
    inp_ref, gain1_ref, w_ref, table_ref, out_w_ref, gain2_ref, router_ref, routes_ref, w_in_hbm, w_out_hbm, cot_ref,
    y_ref, gin_ref, gwin_ref, gwout_ref, gqkv_ref, gout_ref, gain_ref, gtable_ref,
    norm_all, norm_own, q_all, kv, qexp, p_ref, scale, own, att,
    middle, select, rows_out, rows_got, back_got, gwi, gwo, gmid, gmix, da_send, da,
    core_kv, y_kv, home_q, home_kv, small,
    o_core, o_z, o_mid2, o_q, o_last, o_x,
    q_core, q_z, q_mid2, q_q, q_last, q_x,
    k_core, k_z, k_mid2, k_q, k_last, k_x,
    trow, tabs, t_got, got_in, got_out, x_far, x_near, y_in, y_out, z_far, z_near,
    local, send, recv,
):
    me = Place()
    mail = Mail(send, recv)
    near = [1, 3, 2]
    others = [1, 7, 2, 6, 3, 5, 4]
    barrier = pltpu.get_barrier_semaphore()
    peers = [me.x_peer(k) for k in near] + [me.core_peer(), me.y_peer(), me.corner_peer()]
    peers = peers + [me.e_peer(k) for k in others]
    for peer in peers:
        pl.semaphore_signal(barrier, inc=1, device_id=peer, device_id_type=MESH)

    inputs = inp_ref[...].astype(F32)
    root1 = lax.rsqrt(jnp.mean(inputs * inputs, axis=1, keepdims=True) + EPSILON)
    normed = (inputs * root1 * gain1_ref[...].reshape(1, WIDTH)).astype(BF16)
    proj = [dot(normed, w_ref[p]) for p in range(3)]

    def join(p, a, s, b):
        first = proj[p][:, 128 * (a // 2) : 128 * (a // 2) + 128]
        second = first if (p == s and a // 2 == b // 2) else proj[s][:, 128 * (b // 2) : 128 * (b // 2) + 128]
        return pair(first, a % 2, second, b % 2)

    block = rows(me.i, TOK)
    mine = rows(me.x, TOK)
    s_kv, s_q, s_y, s_c, s_f = [mail.block(4) for _ in range(5)]
    def source(step, y, c):
        return rows(4 * me.x_of(-step) + 2 * y + c, TOK)

    ys, cs = {}, {}

    def pass_on(step):
        def to(slot, peer):
            part = kv.at[source(step, me.y, me.c)]
            return part, part, slot + step, peer()

        ys[step] = mail.go_later(lambda: to(s_y, me.y_peer))
        cs[step] = mail.go_later(lambda: to(s_c, me.core_peer))

    tile = iota((128, 128), 0) - iota((128, 128), 1)
    lanes = iota((512, 256), 1)
    def attention(s_ref, bias, m_ref, l_ref, acc, o_part, o_t, kv_send, q_send, q_turned):
        for g in range(4):
            a = 3 * g
            kv_send[g, :, pl.ds(0, 128)] = join(1, a, 1, a + 1).astype(BF16)
            kv_send[g, :, pl.ds(128, 128)] = join(1, a + 2, 2, a + 2).astype(BF16)
            kv_send[g, :, pl.ds(256, 128)] = join(2, a, 2, a + 1).astype(BF16)
            q_send[g, :, pl.ds(0, 128)] = join(0, a, 0, a + 1).astype(BF16)
            q_send[g, :, pl.ds(128, 128)] = jnp.where(iota((TOK, 128), 1) < 64, join(0, a + 2, 0, a + 2), 0.0).astype(BF16)
        pl.semaphore_wait(barrier, len(peers))
        kvs = {k: mail.go(kv_send.at[me.x_of(k)], kv.at[block], s_kv + k, me.x_peer(k)) for k in near}
        kv[block, :] = kv_send[me.x]
        qs = {k: mail.go(q_send.at[me.x_of(k)], q_all.at[mine], s_q + k, me.x_peer(k)) for k in near}
        q_all[mine, :] = q_send[me.x]

        pass_on(0)
        norm_own[...] = dot(normed, norm_places()).astype(BF16)
        norm_all[mine, :] = norm_own[...]
        for h in range(3):
            head = 3 * me.x + h

            def chain(first, n):
                value = jnp.full((128, 128), 1.0, F32) * table_ref[head, first]
                for level, edge in enumerate(EDGES):
                    value = jnp.where(n >= edge, table_ref[head, first + level + 1], value)
                return value

            bias[h, 0] = jnp.full((128, 128), 1.0, F32) * table_ref[head, BUCKETS // 2 - 1]
            bias[h, 1] = chain(0, 128 - tile)
            bias[h, 2] = jnp.where(tile > 0, chain(BUCKETS // 2, tile), chain(0, -tile))
            bias[h, 3] = chain(BUCKETS // 2, 128 + tile)
            bias[h, 4] = jnp.full((128, 128), 1.0, F32) * table_ref[head, BUCKETS - 1]
        m_ref[...] = jnp.full(m_ref.shape, -jnp.inf, F32)
        l_ref[...] = jnp.zeros(l_ref.shape, F32)
        for k in near:
            kvs[k].wait_recv()
            pass_on(k)
        wait_all(qs.values())
        queries = q_all[...].astype(F32) * SCALE
        for h in range(3):
            inside = (lanes >= 64 * h) & (lanes < 64 * h + 64)
            part = jnp.where(inside, queries, 0.0)
            qexp[pl.ds(512 * h, 512), :] = part.astype(BF16)
            q_turned[:, pl.ds(512 * h, 512)] = part.T.astype(BF16)

        def score(steps, half, y):
            for h in range(3):
                turned = q_turned[:, pl.ds(512 * h, 512)]

                def one(step, carry):
                    xx = me.x_of(-step)
                    s = dot(kv[rows(2 * xx + y, 256), pl.ds(0, 256)], turned)
                    for k in range(2):
                        b = 4 * xx + 2 * y + k
                        for t in range(4):
                            kind = jnp.clip(b - (4 * t + 2 * me.y + me.c), -2, 2) + 2
                            part = s[128 * k : 128 * k + 128, 128 * t : 128 * t + 128] + bias[h, kind]
                            cols = pl.ds(128 * t, 128)
                            s_ref[h, rows(2 * xx + k, TOK), cols] = part
                            m_ref[half, h, :, cols] = jnp.maximum(
                                m_ref[half, h, :, cols], jnp.max(part.reshape(16, 8, 128), axis=0)
                            )
                    return carry

                lax.fori_loop(steps[0], steps[1], one, 0)

        def weigh(half, y):
            for h in range(3):
                top = jnp.max(m_ref[half, h], axis=0, keepdims=True)
                acc[...] = jnp.zeros(acc.shape, F32)

                def one(xx, carry):
                    part = jnp.exp(s_ref[h, rows(xx, 256), :] - top)
                    l_ref[half, h] += jnp.sum(part.reshape(32, 8, 512), axis=0)
                    low = part.astype(BF16)
                    span = rows(2 * xx + y, 256)
                    p_ref[span, pl.ds(512 * h, 512)] = low
                    acc[...] += dot_tn(kv[span, pl.ds(128, 256)], low)
                    return carry

                lax.fori_loop(0, 4, one, 0)
                at = pl.ds((128, 192, 64)[h], 64)
                o_part[half, at, :] = acc[at, :]

        cs[0].wait_recv()
        score((0, 1), 0, me.y)
        for k in near:
            cs[k].wait_recv()
        score((1, 4), 0, me.y)
        fs = {}
        for k in (0, 1, 3, 2):
            ys[k].wait_recv()

            def to(k=k):
                part = kv.at[source(k, 1 - me.y, me.c)]
                return part, part, s_f + k, me.core_peer()

            fs[k] = mail.go_later(to)
        weigh(0, me.y)
        wait_all(fs.values())
        score((0, 4), 1, 1 - me.y)
        weigh(1, 1 - me.y)

        factors = jnp.zeros((128, 512), F32)
        which = iota((128, 512), 0)
        o_t[...] = jnp.zeros(o_t.shape, F32)
        for h in range(3):
            tops = [jnp.max(m_ref[half, h], axis=0, keepdims=True) for half in range(2)]
            top = jnp.maximum(tops[0], tops[1])
            fade = [jnp.exp(t - top) for t in tops]
            sums = [jnp.sum(l_ref[half, h], axis=0, keepdims=True) for half in range(2)]
            inv = 1.0 / (sums[0] * fade[0] + sums[1] * fade[1])
            fade = [f * inv for f in fade]
            at = pl.ds((128, 192, 64)[h], 64)
            o_t[at, :] = o_part[0, at, :] * fade[0] + o_part[1, at, :] * fade[1]
            for half in range(2):
                factors = jnp.where(which == 3 * half + h, fade[half], factors)
        scale[...] = factors.T
        own[...] = o_t[...].T.astype(BF16)
        for copy in list(kvs.values()) + list(qs.values()):
            mail.sent(copy)

    pl.run_scoped(
        attention,
        pltpu.VMEM((3, 1024, 512), F32),
        pltpu.VMEM((3, 5, 128, 128), F32),
        pltpu.VMEM((2, 3, 8, 512), F32),
        pltpu.VMEM((2, 3, 8, 512), F32),
        pltpu.VMEM((256, 512), F32),
        pltpu.VMEM((2, 256, 512), F32),
        pltpu.VMEM((256, 512), F32),
        pltpu.VMEM((4, TOK, 384), BF16),
        pltpu.VMEM((4, TOK, 256), BF16),
        pltpu.VMEM((256, 1536), BF16),
    )
    s_o, s_n = mail.block(4), mail.block(4)
    os = [mail.go(own.at[rows(me.x_of(k), TOK)], att.at[me.x], s_o + k, me.x_peer(k)) for k in near]
    att[me.x] = own[mine, :]

    s_there, s_home = mail.block(8), mail.block(8)
    gain2 = gain2_ref[...].reshape(1, WIDTH)
    slots = rows(me.e, 2 * CAP)
    keep = {}

    def experts(hidden, ginner, made, garr, arrived, gprod):
        load_in = pltpu.make_async_copy(w_in_hbm, gwi, local.at[0])
        load_in.start()
        load_out = pltpu.make_async_copy(w_out_hbm, gwo, local.at[1])
        load_out.start()
        wait_all(os)
        ns = [mail.go_later(lambda k=k: (norm_own, norm_all.at[mine], s_n + k, me.x_peer(k))) for k in near]
        mixed = inputs
        for g in range(4):
            mixed = mixed + dot(att[g, :, pl.ds(0, 128)], out_w_ref[pl.ds(192 * g + 64, 128), :])
            mixed = mixed + dot(att[g, :, pl.ds(128, 128)], out_w_ref[pl.ds(192 * g, 128), :])
        middle[...] = mixed
        root = lax.rsqrt(jnp.mean(mixed * mixed, axis=1, keepdims=True) + EPSILON)
        normed_two = (mixed * root * gain2).astype(BF16)
        logits = dot_nt(normed_two, router_ref[...])
        shifted = jnp.exp(logits - jnp.max(logits, axis=1, keepdims=True))
        router = shifted / jnp.sum(shifted, axis=1, keepdims=True)
        diagonal = iota((TOK, TOK), 0) == iota((TOK, TOK), 1)
        named = jnp.sum(jnp.where(diagonal, routes_ref[...].astype(F32), 0.0), axis=1, keepdims=True).astype(jnp.int32)
        chosen = (named == iota((TOK, 8), 1)).astype(F32)
        gate = jnp.sum(chosen * router, axis=1, keepdims=True)
        earlier = (iota((TOK, TOK), 0) > iota((TOK, TOK), 1)).astype(F32).astype(BF16)
        ranks = dot(earlier, chosen.astype(BF16))
        slot = jnp.sum(chosen * ranks, axis=1, keepdims=True).astype(jnp.int32)
        target = named * (2 * CAP) + slot
        column = iota((TOK, 16 * CAP), 1)
        select[pl.ds(0, TOK), :] = (column == target).astype(F32).astype(BF16)
        select[pl.ds(TOK, TOK), :] = (column == target + CAP).astype(F32).astype(BF16)
        dy = cot_ref[...].astype(F32)
        both = jnp.concatenate([normed_two, (gate * dy).astype(BF16)], axis=0)
        rows_out[...] = dot_tn(select[...], both).astype(BF16)
        there = [
            mail.go_later(
                lambda k=k: (rows_out.at[rows(me.e_of(k), 2 * CAP)], rows_got.at[slots], s_there + k, me.e_peer(k))
            )
            for k in others
        ]
        rows_got[slots, :] = rows_out[slots, :]
        made[...] = jnp.zeros(made.shape, F32)
        garr[...] = jnp.zeros(garr.shape, F32)
        load_in.wait()
        load_out.wait()
        wait_all(there)
        got = rows_got[...].astype(F32).reshape(8, 2 * CAP, WIDTH)
        arrived[...] = got[:, :CAP].reshape(8 * CAP, WIDTH).astype(BF16)
        gprod[...] = got[:, CAP:].reshape(8 * CAP, WIDTH).astype(BF16)
        chunk = 768

        def through(j, carry):
            cols = rows(j, chunk)
            for k in range(3):
                part = rows(3 * j + k, 256)
                inner = dot(arrived[...], gwi[:, :, :, part].reshape(WIDTH, 256))
                square = inner * inner
                slope = np.float32(np.sqrt(2 / np.pi))
                t = jnp.tanh(slope * inner * (1.0 + 0.044715 * square))
                half = 0.5 * (1.0 + t)
                hidden[:, part] = (inner * half).astype(BF16)
                w_out = gwo[pl.ds(2 * j, 2)].reshape(chunk, WIDTH)[256 * k : 256 * k + 256]
                back = dot_nt(gprod[...], w_out)
                lean = half + 0.5 * inner * (1.0 - t * t) * slope * (1.0 + 3 * 0.044715 * square)
                ginner[:, part] = (lean * back).astype(BF16)
            made[...] += dot(hidden[:, cols], gwo[pl.ds(2 * j, 2)].reshape(chunk, WIDTH))
            garr[...] += dot_nt(ginner[:, cols], gwi[:, :, :, cols].reshape(WIDTH, chunk))
            return carry

        lax.fori_loop(0, FF // chunk, through, 0)
        back = jnp.concatenate([made[...].reshape(8, CAP, WIDTH), garr[...].reshape(8, CAP, WIDTH)], axis=1)
        for copy in there:
            mail.sent(copy)
        rows_out[...] = back.reshape(16 * CAP, WIDTH).astype(BF16)
        keep["home"] = [
            mail.go_later(
                lambda k=k: (rows_out.at[rows(me.e_of(k), 2 * CAP)], back_got.at[slots], s_home + k, me.e_peer(k))
            )
            for k in others
        ]
        back_got[slots, :] = rows_out[slots, :]

        def grads_out(j, carry):
            gwo[j] = dot_tn(hidden[:, rows(j, 384)], gprod[...]).astype(BF16).reshape(2, 192, WIDTH)
            return carry

        lax.fori_loop(0, 8, grads_out, 0)
        s_out = mail.block(1)
        keep["core_out"] = mail.go_later(lambda: (gwo.at[:, 1 - me.c], got_out, s_out, me.core_peer()))
        def grads_in(j, carry):
            cols = rows(j, 256)
            gwi[:, :, :, cols] = dot_tn(arrived[...], ginner[:, cols]).astype(BF16).reshape(8, 2, 48, 256)
            return carry

        lax.fori_loop(0, FF // 256, grads_in, 0)
        s_in = mail.block(1)
        keep["core_in"] = mail.go_later(lambda: (gwi.at[:, 1 - me.c], got_in, s_in, me.core_peer()))

        keep["norms"] = ns
        return gate, chosen, router, root, normed_two

    gate, chosen, router, root, normed_two = pl.run_scoped(
        experts,
        pltpu.VMEM((8 * CAP, FF), BF16),
        pltpu.VMEM((8 * CAP, FF), BF16),
        pltpu.VMEM((8 * CAP, WIDTH), F32),
        pltpu.VMEM((8 * CAP, WIDTH), F32),
        pltpu.VMEM((8 * CAP, WIDTH), BF16),
        pltpu.VMEM((8 * CAP, WIDTH), BF16),
    )

    right, left, far = me.x_of(1), me.x_of(3), me.x_of(2)
    keep["core_out"].wait_recv()

    def add_out(j, carry):
        gwo[j, me.c] = (gwo[j, me.c].astype(F32) + got_out[j].astype(F32)).astype(BF16)
        return carry

    lax.fori_loop(0, 8, add_out, 0)
    s_yo = mail.block(4)

    def over_y(k, xx):
        return mail.go(gwo.at[2 * xx + 1 - me.y, me.c], y_out.at[xx], s_yo + k, me.y_peer())

    ys_out = [over_y(0, far), over_y(1, right)]

    keep["core_in"].wait_recv()

    def add_in(j, carry):
        gwi[j, me.c] = (gwi[j, me.c].astype(F32) + got_in[j].astype(F32)).astype(BF16)
        return carry

    lax.fori_loop(0, 8, add_in, 0)
    s_far, s_ring = mail.block(2), mail.block(4)
    fars = [
        mail.go(gwi.at[2 * far, me.c], x_far.at[0], s_far, me.x_peer(1)),
        mail.go(gwi.at[2 * far + 1, me.c], x_far.at[1], s_far + 1, me.x_peer(3)),
    ]
    wait_all(keep["home"])
    returned = dot(select[pl.ds(0, TOK), :], back_got[...])
    gnorm = dot(select[pl.ds(TOK, TOK), :], back_got[...])
    mid = middle[...]
    dy = cot_ref[...].astype(F32)
    y_ref[...] = (mid + gate * returned).astype(BF16)
    ggate = jnp.sum(dy * returned, axis=1, keepdims=True)
    glogits = ggate * gate * (chosen - router)
    high = glogits.astype(BF16)
    rest = (glogits - high.astype(F32)).astype(BF16)
    gnorm = gnorm + dot(high, router_ref[...]) + dot(rest, router_ref[...])
    small[...] = jnp.zeros(small.shape, F32)
    small[pl.ds(8, 8), :] = dot_tn(high, normed_two) + dot_tn(rest, normed_two)
    small[pl.ds(0, 1), :] = jnp.sum(gnorm * mid * root, axis=0, keepdims=True)
    u = gain2 * gnorm
    gmiddle = dy + root * u - mid * (root * root * root * jnp.mean(u * mid, axis=1, keepdims=True))
    gmid[...] = gmiddle
    gmix[...] = gmiddle.astype(BF16)
    upper = iota((TOK, 128), 1) >= 64
    for g in range(4):
        front = dot_nt(gmix[...], out_w_ref[pl.ds(192 * g + 64, 128), :])
        da_send[g, :, pl.ds(0, 128)] = jnp.where(upper, front, 0.0).astype(BF16)
        da_send[g, :, pl.ds(128, 128)] = dot_nt(gmix[...], out_w_ref[pl.ds(192 * g, 128), :]).astype(BF16)
    s_da = mail.block(4)
    das = [mail.go(da_send.at[me.x_of(k)], da.at[mine], s_da + k, me.x_peer(k)) for k in near]
    da[mine, :] = da_send[me.x]
    ring = [
        mail.go(gwi.at[2 * right + 1, me.c], x_near.at[1], s_ring, me.x_peer(1)),
        mail.go(gwi.at[2 * left, me.c], x_near.at[2], s_ring + 1, me.x_peer(3)),
    ]

    def rest(doexp, drow, accb, ds, dq, dkv, y_send, fin_kv, fin_q, dproj, o_low, q_low, k_low):
        att_wide = dot(att[0], att_places(0))
        for g in range(1, 4):
            att_wide = att_wide + dot(att[g], att_places(g))
        att_wide = att_wide.astype(BF16)
        for part in range(4):
            block_rows = dot_tn(att_wide[:, 256 * part : 256 * part + 256], gmix[...]).astype(BF16)
            o_low[part // 2, pl.ds(2 * (part % 2), 2), :, :, pl.ds(0, WIDTH)] = block_rows.reshape(2, 4, 32, WIDTH)
        tiny = dot(small[...].astype(BF16), norm_places()).T.astype(BF16)
        o_low[:, :, :, :, pl.ds(WIDTH, 128)] = tiny.reshape(2, 4, 4, 32, 128)
        core_o = mail.go(o_low.at[1 - me.c], o_core, mail.block(1), me.core_peer())

        wait_all(fars)
        near_right = gwi.at[2 * right, me.c]
        near_right[...] = (near_right[...].astype(F32) + x_far[0].astype(F32)).astype(BF16)
        near_left = gwi.at[2 * left + 1, me.c]
        near_left[...] = (near_left[...].astype(F32) + x_far[1].astype(F32)).astype(BF16)
        ring_all = ring + [
            mail.go(near_right, x_near.at[0], s_ring + 2, me.x_peer(1)),
            mail.go(near_left, x_near.at[3], s_ring + 3, me.x_peer(3)),
        ]

        wait_all(das)
        grads = da[...].astype(F32)
        product = grads * own[...].astype(F32)
        sums = jnp.zeros((512, 128), F32)
        for h in range(3):
            at = (128, 192, 64)[h]
            inside = (lanes >= at) & (lanes < at + 64)
            total = jnp.sum(jnp.where(inside, product, 0.0), axis=1, keepdims=True)
            for half in range(2):
                factor = scale[:, pl.ds(3 * half + h, 1)]
                sums = jnp.where(iota((512, 128), 1) == 3 * half + h, total * factor, sums)
        drow[...] = sums.T
        accb[...] = jnp.zeros(accb.shape, F32)
        dq[...] = jnp.zeros(dq.shape, F32)
        s_ckv, s_ykv = mail.block(8), mail.block(4)

        def core_copy(rel, xx, y):
            part = rows(4 * xx + 2 * y + 1 - me.c, TOK)
            return mail.copy(dkv.at[part], core_kv.at[4 * rel + xx], s_ckv + 4 * rel + xx, me.core_peer())

        def attend(rel, y):
            half = 1 - rel
            for h in range(3):
                at = (128, 192, 64)[h]
                inside = (lanes >= at) & (lanes < at + 64)
                kept = jnp.where(inside, da[...].astype(F32), 0.0) * scale[:, pl.ds(3 * half + h, 1)]
                doexp[pl.ds(512 * h, 512), :] = kept.astype(BF16)

            def one(xx, carry):
                span = rows(2 * xx + y, 256)
                keys = kv[span, pl.ds(0, 256)]
                values = kv[span, pl.ds(128, 256)]
                for h in range(3):
                    cols = pl.ds(512 * h, 512)
                    back = dot_nt(values, doexp[cols, :])
                    part = p_ref[span, cols].astype(F32) * (back - drow[pl.ds(3 * half + h, 1), :])
                    ds[:, cols] = part.astype(BF16)
                    for k in range(2):
                        for t in range(4):
                            kind = jnp.clip(4 * xx + 2 * y + k - (4 * t + 2 * me.y + me.c), -2, 2) + 2
                            accb[h, kind] += part[128 * k : 128 * k + 128, 128 * t : 128 * t + 128]
                for h in range(3):
                    cols = pl.ds(512 * h, 512)
                    dq[pl.ds(64 * h, 64), :] += dot_tn(keys, ds[:, cols])[64 * h : 64 * h + 64]
                gk = dot(ds[...], qexp[...])
                gv = dot(p_ref[span, :], doexp[...])
                dkv[span, pl.ds(0, 128)] = gk[:, :128].astype(BF16)
                dkv[span, pl.ds(128, 128)] = (gk[:, 128:] + gv[:, :128]).astype(BF16)
                dkv[span, pl.ds(256, 128)] = gv[:, 128:].astype(BF16)
                core_copy(rel, xx, y).start()
                return carry

            lax.fori_loop(0, 4, one, 0)

        attend(0, 1 - me.y)

        def to_y(xx):
            return mail.copy(y_send.at[xx], y_kv.at[xx], s_ykv + xx, me.y_peer())

        def forward_y(xx, carry):
            core_copy(0, xx, 1 - me.y).wait_recv()
            part = dkv[rows(4 * xx + 2 * (1 - me.y) + me.c, TOK), :].astype(F32)
            y_send[xx] = (part + core_kv[xx].astype(F32)).astype(BF16)
            to_y(xx).start()
            return carry

        lax.fori_loop(0, 4, forward_y, 0)
        y_rest = [over_y(2, left), over_y(3, me.x)]

        class Sum:
            def __init__(self, low, core, z_got, mid2, q_got, last, x_got, first):
                self.low, self.core, self.z_got = low, core, z_got
                self.mid2, self.q_got, self.last, self.x_got = mid2, q_got, last, x_got
                self.first = first

            def peer(self, axis, k):
                return me.z_peer(k) if axis == "z" else me.q_peer(k)

            def of(self, axis, k):
                return me.z_of(k) if axis == "z" else me.q_of(k)

            def begin(self):
                self.copies = [mail.go(self.low.at[1 - me.c], self.core, mail.block(1), me.core_peer())]

            def part(self, index):
                return self.low.at[me.c, :, index] if self.first == "q" else self.low.at[me.c, index]

            def stage_one(self):
                wait_all(self.copies)
                total = self.low[me.c].astype(F32) + self.core[...].astype(F32)
                self.low[me.c] = total.astype(BF16)
                base = mail.block(4)
                self.copies = [
                    mail.go(self.part(self.of(self.first, k)), self.z_got.at[k - 1], base + k, self.peer(self.first, k))
                    for k in near
                ]

            def stage_two(self):
                wait_all(self.copies)
                total = self.part(me.q if self.first == "q" else me.z)[...].astype(F32)
                for k in range(3):
                    total = total + self.z_got[k].astype(F32)
                self.mid2[...] = total.astype(BF16)
                base = mail.block(4)
                second = "z" if self.first == "q" else "q"
                self.copies = [
                    mail.go(self.mid2.at[self.of(second, k)], self.q_got.at[k - 1], base + k, self.peer(second, k))
                    for k in near
                ]

            def stage_three(self):
                wait_all(self.copies)
                total = self.mid2[me.z if self.first == "q" else me.q].astype(F32)
                for k in range(3):
                    total = total + self.q_got[k].astype(F32)
                self.last[...] = total
                base = mail.block(4)
                self.copies = [
                    mail.go(self.last.at[rows(me.x_of(k), 8)], self.x_got.at[me.x], base + k, me.x_peer(k)) for k in near
                ]
                self.x_got[me.x] = self.last[rows(me.x, 8), :]

            def finish(self):
                wait_all(self.copies)

        of_out = Sum(o_low, o_core, o_z, o_mid2, o_q, o_last, o_x, "z")
        of_out.copies = [core_o]
        of_q = Sum(q_low, q_core, q_z, q_mid2, q_q, q_last, q_x, "z")
        of_kv = Sum(k_low, k_core, k_z, k_mid2, k_q, k_last, k_x, "z")
        of_out.stage_one()

        attend(1, me.y)

        fin_q[...] = (dq[...] * SCALE).T.astype(BF16)
        s_xq, s_xkv = mail.block(4), mail.block(4)
        home = [mail.go(fin_q.at[rows(me.x_of(k), TOK)], home_q.at[me.x], s_xq + k, me.x_peer(k)) for k in near]
        home_q[me.x] = fin_q[mine, :]
        wait_all(keep["norms"])
        for part in range(4):
            span = pl.ds(256 * part, 256)
            block_rows = dot_tn(norm_all[:, span], fin_q[...]).astype(BF16)
            q_low[part // 2, pl.ds(2 * (part % 2), 2)] = block_rows.reshape(2, 4, 32, fin_q.shape[1])
        of_q.begin()
        for k in near + [0]:
            xx = me.x_of(k)
            core_copy(1, xx, me.y).wait_recv()
            to_y(xx).wait_recv()
            part = dkv[rows(4 * xx + 2 * me.y + me.c, TOK), :].astype(F32)
            part = (part + core_kv[4 + xx].astype(F32) + y_kv[xx].astype(F32)).astype(BF16)
            fin_kv[rows(xx, TOK), :] = part
            if k:
                home.append(mail.go(fin_kv.at[rows(xx, TOK)], home_kv.at[me.x], s_xkv + k, me.x_peer(k)))
            else:
                home_kv[me.x] = part
        for part in range(4):
            span = pl.ds(256 * part, 256)
            block_rows = dot_tn(norm_all[:, span], fin_kv[...]).astype(BF16)
            k_low[part // 2, pl.ds(2 * (part % 2), 2)] = block_rows.reshape(2, 4, 32, fin_kv.shape[1])
        of_kv.begin()
        of_q.stage_one()
        of_out.stage_two()

        of_kv.stage_one()
        before, center, after = bucket_tile(tile - 128), bucket_tile(tile), bucket_tile(tile + 128)

        def bucket_sum(b, carry):
            for h in range(3):
                near_sum = (
                    jnp.where(before == b, accb[h, 1], 0.0)
                    + jnp.where(center == b, accb[h, 2], 0.0)
                    + jnp.where(after == b, accb[h, 3], 0.0)
                )
                trow[h, pl.ds(b, 1), :] = jnp.sum(near_sum, axis=0, keepdims=True)
            return carry

        lax.fori_loop(0, BUCKETS, bucket_sum, 0)
        table = jnp.zeros((BUCKETS, 128), F32)
        for h in range(3):
            trow[h, pl.ds(BUCKETS // 2 - 1, 1), :] += jnp.sum(accb[h, 0], axis=0, keepdims=True)
            trow[h, pl.ds(BUCKETS - 1, 1), :] += jnp.sum(accb[h, 4], axis=0, keepdims=True)
            total = jnp.sum(trow[h], axis=1, keepdims=True)
            table = jnp.where(iota((BUCKETS, 128), 1) == 3 * me.x + h, total, table)
        tabs[0] = table
        t_core = mail.go(tabs.at[0], t_got.at[0], mail.block(1), me.core_peer())

        wait_all(ring_all)
        for j in range(2):
            total = gwi[2 * me.x + j, me.c].astype(F32) + x_near[j].astype(F32) + x_near[2 + j].astype(F32)
            gwi[2 * me.x + j, me.c] = total.astype(BF16)
        y_hop = mail.go(gwi.at[2 * me.x + 1 - me.y, me.c], y_in, mail.block(1), me.y_peer())
        wait_all(ys_out + y_rest)
        for xx in range(4):
            y_out[xx] = (gwo[2 * xx + me.y, me.c].astype(F32) + y_out[xx].astype(F32)).astype(BF16)
        s_zf, s_zn = mail.block(2), mail.block(4)
        z_fars = [
            mail.go(y_out.at[far, pl.ds(0, 96)], z_far.at[0], s_zf, me.x_peer(1)),
            mail.go(y_out.at[far, pl.ds(96, 96)], z_far.at[1], s_zf + 1, me.x_peer(3)),
        ]
        z_ring = [
            mail.go(y_out.at[right, pl.ds(96, 96)], z_near.at[1], s_zn, me.x_peer(1)),
            mail.go(y_out.at[left, pl.ds(0, 96)], z_near.at[2], s_zn + 1, me.x_peer(3)),
        ]
        of_q.stage_two()
        of_out.stage_three()
        t_core.wait_recv()
        tabs[1] = tabs[0] + t_got[0]
        s_tz = mail.block(4)
        ts = [mail.go(tabs.at[1], t_got.at[k], s_tz + k, me.z_peer(k)) for k in near]
        of_kv.stage_two()

        wait_all(home)

        def piece(p, j):
            g, t = j // 3, j % 3
            if p == 0:
                return home_q[g, :, pl.ds(128 * (t // 2), 128)].astype(F32), t % 2
            if p == 1:
                return home_kv[g, :, pl.ds(128 * (t // 2), 128)].astype(F32), t % 2
            at, half = ((2, 0), (2, 1), (1, 1))[t]
            return home_kv[g, :, pl.ds(128 * at, 128)].astype(F32), half

        for p in range(3):
            for n in range(6):
                first, half_first = piece(p, 2 * n)
                second, half_second = piece(p, 2 * n + 1)
                dproj[p, :, pl.ds(128 * n, 128)] = pair(first, half_first, second, half_second).astype(BF16)
        gnorm = dot_nt(dproj[0], w_ref[0]) + dot_nt(dproj[1], w_ref[1]) + dot_nt(dproj[2], w_ref[2])
        inputs = inp_ref[...].astype(F32)
        root1 = lax.rsqrt(jnp.mean(inputs * inputs, axis=1, keepdims=True) + EPSILON)
        gain1 = gain1_ref[...].reshape(1, WIDTH)
        u = gain1 * gnorm
        mean = jnp.mean(u * inputs, axis=1, keepdims=True)
        gin_ref[...] = gmid[...] + root1 * u - inputs * (root1 * root1 * root1 * mean)

        of_q.stage_three()
        wait_all(ts)
        tabs[2] = tabs[1] + t_got[1] + t_got[2] + t_got[3]
        s_tq = mail.block(4)
        ts = [mail.go(tabs.at[2], t_got.at[3 + k], s_tq + k, me.q_peer(k)) for k in near]
        wait_all(z_fars)
        y_out[right, pl.ds(0, 96), :] = (
            y_out[right, pl.ds(0, 96), :].astype(F32) + z_far[0].astype(F32)
        ).astype(BF16)
        y_out[left, pl.ds(96, 96), :] = (
            y_out[left, pl.ds(96, 96), :].astype(F32) + z_far[1].astype(F32)
        ).astype(BF16)
        z_ring = z_ring + [
            mail.go(y_out.at[right, pl.ds(0, 96)], z_near.at[0], s_zn + 2, me.x_peer(1)),
            mail.go(y_out.at[left, pl.ds(96, 96)], z_near.at[3], s_zn + 3, me.x_peer(3)),
        ]
        of_kv.stage_three()
        wait_all(ts)
        tabs[3] = tabs[2] + t_got[4] + t_got[5] + t_got[6]
        s_tx = mail.block(4)
        ts = [mail.go(tabs.at[3], t_got.at[6 + k], s_tx + k, me.x_peer(k)) for k in near]

        row = iota((16, WIDTH), 0)
        pick = (iota((16, WIDTH), 1) == 6 * (8 * me.i + me.e) + row) & (row < 6)
        pick = pick.astype(F32).astype(BF16)
        picked = [dot(pick, w_ref[p])[:8] for p in range(3)]
        gain_col = jnp.sum(jnp.where(pick[:8].astype(F32) > 0, gain1, 0.0), axis=1, keepdims=True)

        of_out.finish()
        total = o_x[0] + o_x[1] + o_x[2] + o_x[3]
        gout_ref[...] = total
        y_hop.wait_recv()
        gwin_ref[...] = gwi[2 * me.x + me.y, me.c].astype(F32) + y_in[...].astype(F32)
        wait_all(z_ring)
        gwout_ref[pl.ds(0, 96), :] = (
            y_out[me.x, pl.ds(0, 96), :].astype(F32) + z_near[0].astype(F32) + z_near[2].astype(F32)
        )
        gwout_ref[pl.ds(96, 96), :] = (
            y_out[me.x, pl.ds(96, 96), :].astype(F32) + z_near[1].astype(F32) + z_near[3].astype(F32)
        )
        wait_all(ts)
        gtable_ref[...] = tabs[3] + t_got[7] + t_got[8] + t_got[9]
        of_q.finish()
        of_kv.finish()

        def found(p, j):
            g, t = j // 3, j % 3
            if p == 0:
                return q_x[g, :, pl.ds(128 * (t // 2), 128)], t % 2
            if p == 1:
                return k_x[g, :, pl.ds(128 * (t // 2), 128)], t % 2
            at, half = ((2, 0), (2, 1), (1, 1))[t]
            return k_x[g, :, pl.ds(128 * at, 128)], half

        with_gain = jnp.zeros((8, 1), F32)
        for p in range(3):
            for n in range(6):
                first, half_first = found(p, 2 * n)
                second, half_second = found(p, 2 * n + 1)
                cols = pl.ds(128 * n, 128)
                part = pair(first, half_first, second, half_second)
                gqkv_ref[p, :, cols] = part
                with_gain = with_gain + jnp.sum(
                    part * picked[p][:, 128 * n : 128 * n + 128], axis=1, keepdims=True
                )
        real = iota((8, 1), 0) < 6
        gain_ref[...] = jnp.where(real, with_gain / jnp.where(real, gain_col, 1.0), 0.0) * jnp.ones((8, 128), F32)
        for copy in mail.started:
            copy.wait_send()
        for rel, y in ((0, 1 - me.y), (1, me.y)):
            for xx in range(4):
                core_copy(rel, xx, y).wait_send()
        for xx in range(4):
            to_y(xx).wait_send()

    pl.run_scoped(
        rest,
        pltpu.VMEM((1536, 256), BF16),
        pltpu.VMEM((128, 512), F32),
        pltpu.VMEM((3, 5, 128, 128), F32),
        pltpu.VMEM((256, 1536), BF16),
        pltpu.VMEM((256, 512), F32),
        pltpu.VMEM((2048, 384), BF16),
        pltpu.VMEM((4, TOK, 384), BF16),
        pltpu.VMEM((512, 384), BF16),
        pltpu.VMEM((512, 256), BF16),
        pltpu.VMEM((3, TOK, WIDTH), BF16),
        pltpu.VMEM((2, 4, 4, 32, WIDTH + 128), BF16),
        pltpu.VMEM((2, 4, 4, 32, 256), BF16),
        pltpu.VMEM((2, 4, 4, 32, 384), BF16),
    )


def sum_buffers(width):
    return [
        pltpu.VMEM((4, 4, 32, width), BF16),
        pltpu.VMEM((3, 4, 32, width), BF16),
        pltpu.VMEM((4, 32, width), BF16),
        pltpu.VMEM((3, 32, width), BF16),
        pltpu.VMEM((32, width), F32),
        pltpu.VMEM((4, 8, width), F32),
    ]


def layer(*arrays):
    shape = jax.ShapeDtypeStruct
    vm = pltpu.VMEM
    return pl.pallas_call(
        layer_kernel,
        out_shape=(
            shape((TOK, WIDTH), BF16),
            shape((TOK, WIDTH), F32),
            shape((48, FF), F32),
            shape((192, WIDTH), F32),
            shape((3, 8, WIDTH), F32),
            shape((8, WIDTH + 128), F32),
            shape((8, 128), F32),
            shape((BUCKETS, 128), F32),
        ),
        in_specs=[VMEM] * 3 + [SMEM] + [VMEM] * 4 + [ANY] * 2 + [VMEM],
        out_specs=(VMEM,) * 8,
        scratch_shapes=[
            vm((512, 1024), BF16),
            vm((TOK, 1024), BF16),
            vm((512, 256), BF16),
            vm((2048, 384), BF16),
            vm((1536, 256), BF16),
            vm((2048, 1536), BF16),
            vm((512, 128), F32),
            vm((512, 256), BF16),
            vm((4, TOK, 256), BF16),
            vm((TOK, WIDTH), F32),
            vm((2 * TOK, 16 * CAP), BF16),
            vm((16 * CAP, WIDTH), BF16),
            vm((16 * CAP, WIDTH), BF16),
            vm((16 * CAP, WIDTH), BF16),
            vm((8, 2, 48, FF), BF16),
            vm((8, 2, 192, WIDTH), BF16),
            vm((TOK, WIDTH), F32),
            vm((TOK, WIDTH), BF16),
            vm((4, TOK, 256), BF16),
            vm((512, 256), BF16),
            vm((8, TOK, 384), BF16),
            vm((4, TOK, 384), BF16),
            vm((4, TOK, 256), BF16),
            vm((4, TOK, 384), BF16),
            vm((128, WIDTH), F32),
        ]
        + sum_buffers(WIDTH + 128)
        + sum_buffers(256)
        + sum_buffers(384)
        + [
            vm((3, BUCKETS, 128), F32),
            vm((4, BUCKETS, 128), F32),
            vm((10, BUCKETS, 128), F32),
            vm((8, 48, FF), BF16),
            vm((8, 192, WIDTH), BF16),
            vm((2, 48, FF), BF16),
            vm((4, 48, FF), BF16),
            vm((48, FF), BF16),
            vm((4, 192, WIDTH), BF16),
            vm((2, 96, WIDTH), BF16),
            vm((4, 96, WIDTH), BF16),
            pltpu.SemaphoreType.DMA((2,)),
            pltpu.SemaphoreType.DMA((SEMS,)),
            pltpu.SemaphoreType.DMA((SEMS,)),
        ],
        compiler_params=pltpu.CompilerParams(
            collective_id=0, has_side_effects=True, vmem_limit_bytes=VMEM_LIMIT
        ),
    )(*arrays)


def place_kernel(
    y, gin, gwin, gwout, gqkv, gout, gain, table,
    y_ref, gin_ref, gwin_ref, gwout_ref, gqkv_ref, gout_ref, gain1_ref, gain2_ref, router_ref, table_ref,
):
    y_ref[...] = y[...]
    gin_ref[...] = gin[...]
    gwin_ref[...] = gwin[...]
    gwout_ref[...] = gwout[...]
    gqkv_ref[...] = gqkv[:, :6, :]
    gout_ref[...] = gout[:6, :WIDTH]
    gain1_ref[...] = gain[...].T[:1, :6]
    others = gout[:, WIDTH:].T
    gain2_ref[...] = others[:1, :6]
    router_ref[...] = others[8:16, :6]
    table_ref[...] = table[...].T[:HEADS]


def place(*arrays):
    shape = jax.ShapeDtypeStruct
    return pl.pallas_call(
        place_kernel,
        out_shape=(
            shape((TOK, WIDTH), BF16),
            shape((TOK, WIDTH), F32),
            shape((48, FF), F32),
            shape((192, WIDTH), F32),
            shape((3, 6, WIDTH), F32),
            shape((6, WIDTH), F32),
            shape((1, 6), F32),
            shape((1, 6), F32),
            shape((8, 6), F32),
            shape((HEADS, BUCKETS), F32),
        ),
        in_specs=[VMEM] * 8,
        out_specs=(VMEM,) * 10,
        compiler_params=pltpu.CompilerParams(vmem_limit_bytes=VMEM_LIMIT),
    )(*arrays)


def body(
    block_input, gain_one, qkv_weight, out_weight, rel_table, gain_two, router_weight, routes, w_in, w_out, cotangent
):
    parts = layer(
        block_input[0], gain_one, qkv_weight, rel_table.T, out_weight, gain_two, router_weight.T,
        routes.reshape(1, TOK), w_in.reshape(8, 2, 48, FF), w_out.reshape(8, 2, 192, WIDTH), cotangent[0],
    )
    y, gin, gwin, gwout, gqkv, gout, gain1, gain2, router, table = place(*parts)
    return (
        y[None],
        gin[None],
        gain1.reshape(6),
        gqkv,
        gout,
        table.T,
        gain2.reshape(6),
        router.T,
        gwin[None],
        gwout[None],
    )


def solution(mesh):
    tokens = P("expert", "ctx", None)
    split = P(("ctx", "expert"))
    return jax.shard_map(
        body,
        mesh=mesh,
        in_specs=(
            tokens, P(), P(), P(), P(), P(), P(), tokens, P("expert", None, None), P("expert", None, None), tokens,
        ),
        out_specs=(
            tokens, tokens, split, P(None, ("ctx", "expert"), None), split, P(), split, split, tokens, tokens,
        ),
        check_vma=False,
    )
```

```python
import jax
import jax.numpy as jnp
import numpy as np
from jax import lax
from jax.experimental import pallas as pl
from jax.experimental.pallas import tpu as pltpu
from jax.sharding import PartitionSpec as P

HEADS = 12
HEAD_DIM = 64
BUCKETS = 32
MAX_DISTANCE = 128
EPSILON = 1e-06
SCALE = HEAD_DIM ** (-0.5)
TOK = 128
WIDTH = 768
FF = 3072
CAP = 24
F32 = jnp.float32
BF16 = jnp.bfloat16
MESH = pl.DeviceIdType.MESH
VMEM = pl.BlockSpec(memory_space=pltpu.VMEM)
SMEM = pl.BlockSpec(memory_space=pltpu.SMEM)
ANY = pl.BlockSpec(memory_space=pl.ANY)
VMEM_LIMIT = 63 * 1024 * 1024


def bucket_edges(buckets, reach):
    half = buckets // 2
    exact = half // 2
    spans = np.arange(1, reach + 1)
    spread = np.log(np.maximum(spans, exact) / exact) / np.log(reach / exact) * (half - exact)
    large = np.minimum(exact + spread.astype(np.int64), half - 1)
    level = np.where(spans < exact, spans, large)
    return [int(np.argmax(level >= b)) + 1 for b in range(1, half)]


EDGES = bucket_edges(BUCKETS, MAX_DISTANCE)


def dot(a, b):
    return jnp.dot(a, b, preferred_element_type=F32)


def dot_nt(a, b):
    return lax.dot_general(a, b, (((1,), (1,)), ((), ())), preferred_element_type=F32)


def dot_tn(a, b):
    return lax.dot_general(a, b, (((0,), (0,)), ((), ())), preferred_element_type=F32)


def iota(shape, dim):
    return lax.broadcasted_iota(jnp.int32, shape, dim)


class Place:
    def __init__(self):
        self.i = lax.axis_index("ctx")
        self.e = lax.axis_index("expert")
        self.x = lax.div(self.i, 4)
        self.y = lax.rem(lax.div(self.i, 2), 2)
        self.c = lax.rem(self.i, 2)
        self.z = lax.div(self.e, 2)
        self.h = lax.rem(self.e, 2)
        self.q = self.h * 2 + self.y

    def x_of(self, step):
        return lax.rem(self.x + 4 + step, 4)

    def x_peer(self, step):
        return (4 * self.x_of(step) + 2 * self.y + self.c, self.e)

    def core_peer(self):
        return (4 * self.x + 2 * self.y + 1 - self.c, self.e)

    def y_peer(self):
        return (4 * self.x + 2 * (1 - self.y) + self.c, self.e)

    def z_of(self, step):
        return lax.rem(self.z + 4 + step, 4)

    def z_peer(self, step):
        return (self.i, 2 * self.z_of(step) + self.h)

    def q_of(self, step):
        return lax.rem(self.q + 4 + step, 4)

    def q_peer(self, step):
        q = self.q_of(step)
        return (4 * self.x + 2 * lax.rem(q, 2) + self.c, 2 * self.z + lax.div(q, 2))

    def corner_peer(self):
        return (4 * self.x + 2 * (1 - self.y) + self.c, 2 * self.z + 1 - self.h)

    def e_of(self, step):
        return lax.rem(self.e + 8 + step, 8)

    def e_peer(self, step):
        return (self.i, self.e_of(step))


def greet(peers):
    barrier = pltpu.get_barrier_semaphore()
    for peer in peers:
        pl.semaphore_signal(barrier, inc=1, device_id=peer, device_id_type=MESH)
    pl.semaphore_wait(barrier, len(peers))


def rcopy(src, dst, send, recv, slot, peer):
    return pltpu.make_async_remote_copy(
        src_ref=src,
        dst_ref=dst,
        send_sem=send.at[slot],
        recv_sem=recv.at[slot],
        device_id=peer,
        device_id_type=MESH,
    )


def rows(index, size):
    return pl.ds(pl.multiple_of(index * size, size), size)


def pair(first, half_first, second, half_second):
    if first is second and (half_first, half_second) == (0, 1):
        return first
    low = pltpu.roll(first, 64, 1) if half_first else first
    high = second if half_second else pltpu.roll(second, 64, 1)
    return jnp.where(iota(low.shape, 1) < 64, low, high)


def norm_places():
    col = iota((1, 1024), 1)
    r = col & 7
    xx = (col >> 3) & 3
    yl = (col >> 5) & 1
    e = (((col >> 7) & 3) << 1) + ((col >> 6) & 1)
    c = (col >> 9) & 1
    d = jnp.where(r < 6, 192 * xx + 96 * yl + 48 * c + 6 * e + r, -1)
    return (iota((WIDTH, 1024), 0) == d).astype(F32).astype(BF16)


def att_places(group):
    col = iota((1, 1024), 1)
    r = col & 7
    e = (((col >> 7) & 3) << 1) + ((col >> 6) & 1)
    f = 96 * ((col >> 5) & 1) + 48 * ((col >> 9) & 1) + 6 * e + r
    f = jnp.where((r < 6) & (((col >> 3) & 3) == group), f, -1)
    lane = iota((256, 1024), 0)
    feature = jnp.where(lane >= 128, lane - 128, jnp.where(lane >= 64, lane + 64, -2))
    return (feature == f).astype(F32).astype(BF16)


def bucket_tile(offset):
    length = jnp.abs(offset)
    level = jnp.where(offset > 0, BUCKETS // 2, 0)
    for edge in EDGES:
        level = level + (length >= edge).astype(jnp.int32)
    return level


SEMS = 192


class Mail:
    def __init__(self, send, recv):
        self.send, self.recv, self.used, self.started = send, recv, 0, []

    def block(self, count):
        base = self.used
        self.used += count
        assert self.used <= SEMS
        return base

    def copy(self, src, dst, slot, peer):
        return rcopy(src, dst, self.send, self.recv, slot, peer)

    def go(self, src, dst, slot, peer):
        copy = self.copy(src, dst, slot, peer)
        copy.start()
        self.started.append(copy)
        return copy

    def sent(self, copy):
        copy.wait_send()
        self.started = [other for other in self.started if other is not copy]

    def go_later(self, make):
        copy = Made(lambda: self.copy(*make()))
        copy.make().start()
        self.started.append(copy)
        return copy


class Made:
    def __init__(self, make):
        self.make = make

    def wait_recv(self):
        self.make().wait_recv()

    def wait_send(self):
        self.make().wait_send()


def wait_all(copies):
    for copy in copies:
        copy.wait_recv()


def layer_kernel(
    inp_ref, gain1_ref, w_ref, table_ref, out_w_ref, gain2_ref, router_ref, routes_ref, w_in_hbm, w_out_hbm, cot_ref,
    y_ref, gin_ref, gwin_ref, gwout_ref, gqkv_ref, gout_ref, gain_ref, gtable_ref,
    norm_all, norm_own, q_all, kv, qexp, p_ref, scale, own, att,
    middle, select, rows_out, rows_got, back_got, gwi, gwo, gmid, gmix, da_send, da,
    core_kv, y_kv, home_q, home_kv, small,
    o_core, o_z, o_mid2, o_q, o_last, o_x,
    q_core, q_z, q_mid2, q_q, q_last, q_x,
    k_core, k_z, k_mid2, k_q, k_last, k_x,
    trow, tabs, t_got, got_in, got_out, x_far, x_near, y_in, y_out, z_far, z_near,
    local, send, recv,
):
    me = Place()
    mail = Mail(send, recv)
    near = [1, 3, 2]
    others = [1, 7, 2, 6, 3, 5, 4]
    barrier = pltpu.get_barrier_semaphore()
    peers = [me.x_peer(k) for k in near] + [me.core_peer(), me.y_peer(), me.corner_peer()]
    peers = peers + [me.e_peer(k) for k in others]
    for peer in peers:
        pl.semaphore_signal(barrier, inc=1, device_id=peer, device_id_type=MESH)

    inputs = inp_ref[...].astype(F32)
    root1 = lax.rsqrt(jnp.mean(inputs * inputs, axis=1, keepdims=True) + EPSILON)
    normed = (inputs * root1 * gain1_ref[...].reshape(1, WIDTH)).astype(BF16)
    proj = [dot(normed, w_ref[p]) for p in range(3)]

    def join(p, a, s, b):
        first = proj[p][:, 128 * (a // 2) : 128 * (a // 2) + 128]
        second = first if (p == s and a // 2 == b // 2) else proj[s][:, 128 * (b // 2) : 128 * (b // 2) + 128]
        return pair(first, a % 2, second, b % 2)

    block = rows(me.i, TOK)
    mine = rows(me.x, TOK)
    s_kv, s_q, s_y, s_c, s_f = [mail.block(4) for _ in range(5)]
    def source(step, y, c):
        return rows(4 * me.x_of(-step) + 2 * y + c, TOK)

    ys, cs = {}, {}

    def pass_on(step):
        def to(slot, peer):
            part = kv.at[source(step, me.y, me.c)]
            return part, part, slot + step, peer()

        ys[step] = mail.go_later(lambda: to(s_y, me.y_peer))
        cs[step] = mail.go_later(lambda: to(s_c, me.core_peer))

    tile = iota((128, 128), 0) - iota((128, 128), 1)
    lanes = iota((512, 256), 1)
    def attention(s_ref, bias, m_ref, l_ref, acc, o_part, o_t, kv_send, q_send, q_turned):
        for g in range(4):
            a = 3 * g
            kv_send[g, :, pl.ds(0, 128)] = join(1, a, 1, a + 1).astype(BF16)
            kv_send[g, :, pl.ds(128, 128)] = join(1, a + 2, 2, a + 2).astype(BF16)
            kv_send[g, :, pl.ds(256, 128)] = join(2, a, 2, a + 1).astype(BF16)
            q_send[g, :, pl.ds(0, 128)] = join(0, a, 0, a + 1).astype(BF16)
            q_send[g, :, pl.ds(128, 128)] = jnp.where(iota((TOK, 128), 1) < 64, join(0, a + 2, 0, a + 2), 0.0).astype(BF16)
        pl.semaphore_wait(barrier, len(peers))
        kvs = {k: mail.go(kv_send.at[me.x_of(k)], kv.at[block], s_kv + k, me.x_peer(k)) for k in near}
        kv[block, :] = kv_send[me.x]
        qs = {k: mail.go(q_send.at[me.x_of(k)], q_all.at[mine], s_q + k, me.x_peer(k)) for k in near}
        q_all[mine, :] = q_send[me.x]

        pass_on(0)
        norm_own[...] = dot(normed, norm_places()).astype(BF16)
        norm_all[mine, :] = norm_own[...]
        for h in range(3):
            head = 3 * me.x + h

            def chain(first, n):
                value = jnp.full((128, 128), 1.0, F32) * table_ref[head, first]
                for level, edge in enumerate(EDGES):
                    value = jnp.where(n >= edge, table_ref[head, first + level + 1], value)
                return value

            bias[h, 0] = jnp.full((128, 128), 1.0, F32) * table_ref[head, BUCKETS // 2 - 1]
            bias[h, 1] = chain(0, 128 - tile)
            bias[h, 2] = jnp.where(tile > 0, chain(BUCKETS // 2, tile), chain(0, -tile))
            bias[h, 3] = chain(BUCKETS // 2, 128 + tile)
            bias[h, 4] = jnp.full((128, 128), 1.0, F32) * table_ref[head, BUCKETS - 1]
        m_ref[...] = jnp.full(m_ref.shape, -jnp.inf, F32)
        l_ref[...] = jnp.zeros(l_ref.shape, F32)
        for k in near:
            kvs[k].wait_recv()
            pass_on(k)
        wait_all(qs.values())
        queries = q_all[...].astype(F32) * SCALE
        for h in range(3):
            inside = (lanes >= 64 * h) & (lanes < 64 * h + 64)
            part = jnp.where(inside, queries, 0.0)
            qexp[pl.ds(512 * h, 512), :] = part.astype(BF16)
            q_turned[:, pl.ds(512 * h, 512)] = part.T.astype(BF16)

        def score(steps, half, y):
            for h in range(3):
                turned = q_turned[:, pl.ds(512 * h, 512)]

                def one(step, carry):
                    xx = me.x_of(-step)
                    s = dot(kv[rows(2 * xx + y, 256), pl.ds(0, 256)], turned)
                    for k in range(2):
                        b = 4 * xx + 2 * y + k
                        for t in range(4):
                            kind = jnp.clip(b - (4 * t + 2 * me.y + me.c), -2, 2) + 2
                            part = s[128 * k : 128 * k + 128, 128 * t : 128 * t + 128] + bias[h, kind]
                            cols = pl.ds(128 * t, 128)
                            s_ref[h, rows(2 * xx + k, TOK), cols] = part
                            m_ref[half, h, :, cols] = jnp.maximum(
                                m_ref[half, h, :, cols], jnp.max(part.reshape(16, 8, 128), axis=0)
                            )
                    return carry

                lax.fori_loop(steps[0], steps[1], one, 0, unroll=True)

        def weigh(half, y):
            for h in range(3):
                top = jnp.max(m_ref[half, h], axis=0, keepdims=True)
                acc[...] = jnp.zeros(acc.shape, F32)

                def one(xx, carry):
                    part = jnp.exp(s_ref[h, rows(xx, 256), :] - top)
                    l_ref[half, h] += jnp.sum(part.reshape(32, 8, 512), axis=0)
                    low = part.astype(BF16)
                    span = rows(2 * xx + y, 256)
                    p_ref[span, pl.ds(512 * h, 512)] = low
                    acc[...] += dot_tn(kv[span, pl.ds(128, 256)], low)
                    return carry

                lax.fori_loop(0, 4, one, 0, unroll=True)
                at = pl.ds((128, 192, 64)[h], 64)
                o_part[half, at, :] = acc[at, :]

        cs[0].wait_recv()
        score((0, 1), 0, me.y)
        for k in near:
            cs[k].wait_recv()
        score((1, 4), 0, me.y)
        fs = {}
        for k in (0, 1, 3, 2):
            ys[k].wait_recv()

            def to(k=k):
                part = kv.at[source(k, 1 - me.y, me.c)]
                return part, part, s_f + k, me.core_peer()

            fs[k] = mail.go_later(to)
        weigh(0, me.y)
        wait_all(fs.values())
        score((0, 4), 1, 1 - me.y)
        weigh(1, 1 - me.y)

        factors = jnp.zeros((128, 512), F32)
        which = iota((128, 512), 0)
        o_t[...] = jnp.zeros(o_t.shape, F32)
        for h in range(3):
            tops = [jnp.max(m_ref[half, h], axis=0, keepdims=True) for half in range(2)]
            top = jnp.maximum(tops[0], tops[1])
            fade = [jnp.exp(t - top) for t in tops]
            sums = [jnp.sum(l_ref[half, h], axis=0, keepdims=True) for half in range(2)]
            inv = 1.0 / (sums[0] * fade[0] + sums[1] * fade[1])
            fade = [f * inv for f in fade]
            at = pl.ds((128, 192, 64)[h], 64)
            o_t[at, :] = o_part[0, at, :] * fade[0] + o_part[1, at, :] * fade[1]
            for half in range(2):
                factors = jnp.where(which == 3 * half + h, fade[half], factors)
        scale[...] = factors.T
        own[...] = o_t[...].T.astype(BF16)
        for copy in list(kvs.values()) + list(qs.values()):
            mail.sent(copy)

    pl.run_scoped(
        attention,
        pltpu.VMEM((3, 1024, 512), F32),
        pltpu.VMEM((3, 5, 128, 128), F32),
        pltpu.VMEM((2, 3, 8, 512), F32),
        pltpu.VMEM((2, 3, 8, 512), F32),
        pltpu.VMEM((256, 512), F32),
        pltpu.VMEM((2, 256, 512), F32),
        pltpu.VMEM((256, 512), F32),
        pltpu.VMEM((4, TOK, 384), BF16),
        pltpu.VMEM((4, TOK, 256), BF16),
        pltpu.VMEM((256, 1536), BF16),
    )
    s_o, s_n = mail.block(4), mail.block(4)
    os = [mail.go(own.at[rows(me.x_of(k), TOK)], att.at[me.x], s_o + k, me.x_peer(k)) for k in near]
    att[me.x] = own[mine, :]

    s_there, s_home = mail.block(8), mail.block(8)
    gain2 = gain2_ref[...].reshape(1, WIDTH)
    slots = rows(me.e, 2 * CAP)
    keep = {}

    def experts(hidden, ginner, made, garr, arrived, gprod):
        load_in = pltpu.make_async_copy(w_in_hbm, gwi, local.at[0])
        load_in.start()
        load_out = pltpu.make_async_copy(w_out_hbm, gwo, local.at[1])
        load_out.start()
        wait_all(os)
        ns = [mail.go_later(lambda k=k: (norm_own, norm_all.at[mine], s_n + k, me.x_peer(k))) for k in near]
        mixed = inputs
        for g in range(4):
            mixed = mixed + dot(att[g, :, pl.ds(0, 128)], out_w_ref[pl.ds(192 * g + 64, 128), :])
            mixed = mixed + dot(att[g, :, pl.ds(128, 128)], out_w_ref[pl.ds(192 * g, 128), :])
        middle[...] = mixed
        root = lax.rsqrt(jnp.mean(mixed * mixed, axis=1, keepdims=True) + EPSILON)
        normed_two = (mixed * root * gain2).astype(BF16)
        logits = dot_nt(normed_two, router_ref[...])
        shifted = jnp.exp(logits - jnp.max(logits, axis=1, keepdims=True))
        router = shifted / jnp.sum(shifted, axis=1, keepdims=True)
        diagonal = iota((TOK, TOK), 0) == iota((TOK, TOK), 1)
        named = jnp.sum(jnp.where(diagonal, routes_ref[...].astype(F32), 0.0), axis=1, keepdims=True).astype(jnp.int32)
        chosen = (named == iota((TOK, 8), 1)).astype(F32)
        gate = jnp.sum(chosen * router, axis=1, keepdims=True)
        earlier = (iota((TOK, TOK), 0) > iota((TOK, TOK), 1)).astype(F32).astype(BF16)
        ranks = dot(earlier, chosen.astype(BF16))
        slot = jnp.sum(chosen * ranks, axis=1, keepdims=True).astype(jnp.int32)
        target = named * (2 * CAP) + slot
        column = iota((TOK, 16 * CAP), 1)
        select[pl.ds(0, TOK), :] = (column == target).astype(F32).astype(BF16)
        select[pl.ds(TOK, TOK), :] = (column == target + CAP).astype(F32).astype(BF16)
        dy = cot_ref[...].astype(F32)
        both = jnp.concatenate([normed_two, (gate * dy).astype(BF16)], axis=0)
        rows_out[...] = dot_tn(select[...], both).astype(BF16)
        there = [
            mail.go_later(
                lambda k=k: (rows_out.at[rows(me.e_of(k), 2 * CAP)], rows_got.at[slots], s_there + k, me.e_peer(k))
            )
            for k in others
        ]
        rows_got[slots, :] = rows_out[slots, :]
        made[...] = jnp.zeros(made.shape, F32)
        garr[...] = jnp.zeros(garr.shape, F32)
        load_in.wait()
        load_out.wait()
        wait_all(there)
        got = rows_got[...].astype(F32).reshape(8, 2 * CAP, WIDTH)
        arrived[...] = got[:, :CAP].reshape(8 * CAP, WIDTH).astype(BF16)
        gprod[...] = got[:, CAP:].reshape(8 * CAP, WIDTH).astype(BF16)
        chunk = 768

        def through(j, carry):
            cols = rows(j, chunk)
            for k in range(3):
                part = rows(3 * j + k, 256)
                inner = dot(arrived[...], gwi[:, :, :, part].reshape(WIDTH, 256))
                square = inner * inner
                slope = np.float32(np.sqrt(2 / np.pi))
                t = jnp.tanh(slope * inner * (1.0 + 0.044715 * square))
                half = 0.5 * (1.0 + t)
                hidden[:, part] = (inner * half).astype(BF16)
                w_out = gwo[j].reshape(chunk, WIDTH)[256 * k : 256 * k + 256]
                back = dot_nt(gprod[...], w_out)
                lean = half + 0.5 * inner * (1.0 - t * t) * slope * (1.0 + 3 * 0.044715 * square)
                ginner[:, part] = (lean * back).astype(BF16)
            made[...] += dot(hidden[:, cols], gwo[j].reshape(chunk, WIDTH))
            garr[...] += dot_nt(ginner[:, cols], gwi[:, :, :, cols].reshape(WIDTH, chunk))
            return carry

        lax.fori_loop(0, FF // chunk, through, 0, unroll=2)
        back = jnp.concatenate([made[...].reshape(8, CAP, WIDTH), garr[...].reshape(8, CAP, WIDTH)], axis=1)
        for copy in there:
            mail.sent(copy)
        rows_out[...] = back.reshape(16 * CAP, WIDTH).astype(BF16)
        keep["home"] = [
            mail.go_later(
                lambda k=k: (rows_out.at[rows(me.e_of(k), 2 * CAP)], back_got.at[slots], s_home + k, me.e_peer(k))
            )
            for k in others
        ]
        back_got[slots, :] = rows_out[slots, :]

        arrived_t = arrived[...].T

        def grads_in(j, carry):
            cols = rows(j, 256)
            gwi[:, :, :, cols] = dot(arrived_t, ginner[:, cols]).astype(BF16).reshape(8, 2, 48, 256)
            return carry

        lax.fori_loop(0, FF // 256, grads_in, 0, unroll=4)
        s_in = mail.block(1)
        keep["core_in"] = mail.go_later(lambda: (gwi.at[:, 1 - me.c], got_in, s_in, me.core_peer()))

        def grads_out(y):
            def one(xx, carry):
                part = dot_tn(hidden[:, rows(2 * xx + y, 384)], gprod[...])
                gwo[xx, y] = part.astype(BF16).reshape(2, 192, WIDTH)
                return carry

            lax.fori_loop(0, 4, one, 0, unroll=2)

        s_out = mail.block(2)
        for rel in range(2):
            grads_out(me.y if rel else 1 - me.y)
            keep["core_out", rel] = mail.go_later(
                lambda rel=rel: (
                    gwo.at[:, me.y if rel else 1 - me.y, 1 - me.c], got_out.at[rel], s_out + rel, me.core_peer()
                )
            )

        keep["norms"] = ns
        return gate, chosen, router, root, normed_two

    gate, chosen, router, root, normed_two = pl.run_scoped(
        experts,
        pltpu.VMEM((8 * CAP, FF), BF16),
        pltpu.VMEM((8 * CAP, FF), BF16),
        pltpu.VMEM((8 * CAP, WIDTH), F32),
        pltpu.VMEM((8 * CAP, WIDTH), F32),
        pltpu.VMEM((8 * CAP, WIDTH), BF16),
        pltpu.VMEM((8 * CAP, WIDTH), BF16),
    )

    right, left, far = me.x_of(1), me.x_of(3), me.x_of(2)
    keep["core_in"].wait_recv()

    def add_in(j, carry):
        gwi[j, me.c] = (gwi[j, me.c].astype(F32) + got_in[j].astype(F32)).astype(BF16)
        return carry

    lax.fori_loop(0, 8, add_in, 0)
    s_far, s_ring = mail.block(2), mail.block(4)
    fars = [
        mail.go(gwi.at[2 * far, me.c], x_far.at[0], s_far, me.x_peer(1)),
        mail.go(gwi.at[2 * far + 1, me.c], x_far.at[1], s_far + 1, me.x_peer(3)),
    ]
    wait_all(keep["home"])
    keep["core_out", 0].wait_recv()

    def add_out(xx, carry):
        gwo[xx, 1 - me.y, me.c] = (gwo[xx, 1 - me.y, me.c].astype(F32) + got_out[0, xx].astype(F32)).astype(BF16)
        return carry

    lax.fori_loop(0, 4, add_out, 0)
    s_yo = mail.block(4)

    def over_y(k, xx):
        return mail.go(gwo.at[xx, 1 - me.y, me.c], y_out.at[xx], s_yo + k, me.y_peer())


    ys_out = [over_y(0, far), over_y(1, right)]
    returned = dot(select[pl.ds(0, TOK), :], back_got[...])
    gnorm = dot(select[pl.ds(TOK, TOK), :], back_got[...])
    mid = middle[...]
    dy = cot_ref[...].astype(F32)
    y_ref[...] = (mid + gate * returned).astype(BF16)
    ggate = jnp.sum(dy * returned, axis=1, keepdims=True)
    glogits = ggate * gate * (chosen - router)
    high = glogits.astype(BF16)
    rest = (glogits - high.astype(F32)).astype(BF16)
    gnorm = gnorm + dot(high, router_ref[...]) + dot(rest, router_ref[...])
    small[...] = jnp.zeros(small.shape, F32)
    small[pl.ds(8, 8), :] = dot_tn(high, normed_two) + dot_tn(rest, normed_two)
    small[pl.ds(0, 1), :] = jnp.sum(gnorm * mid * root, axis=0, keepdims=True)
    u = gain2 * gnorm
    gmiddle = dy + root * u - mid * (root * root * root * jnp.mean(u * mid, axis=1, keepdims=True))
    gmid[...] = gmiddle
    gmix[...] = gmiddle.astype(BF16)
    upper = iota((TOK, 128), 1) >= 64
    for g in range(4):
        front = dot_nt(gmix[...], out_w_ref[pl.ds(192 * g + 64, 128), :])
        da_send[g, :, pl.ds(0, 128)] = jnp.where(upper, front, 0.0).astype(BF16)
        da_send[g, :, pl.ds(128, 128)] = dot_nt(gmix[...], out_w_ref[pl.ds(192 * g, 128), :]).astype(BF16)
    s_da = mail.block(4)
    das = [mail.go(da_send.at[me.x_of(k)], da.at[mine], s_da + k, me.x_peer(k)) for k in near]
    da[mine, :] = da_send[me.x]
    ring = [
        mail.go(gwi.at[2 * right + 1, me.c], x_near.at[1], s_ring, me.x_peer(1)),
        mail.go(gwi.at[2 * left, me.c], x_near.at[2], s_ring + 1, me.x_peer(3)),
    ]

    def rest(doexp, drow, accb, ds, dq, dkv, y_send, fin_kv, fin_q, dproj, o_low, q_low, k_low):
        att_wide = dot(att[0], att_places(0))
        for g in range(1, 4):
            att_wide = att_wide + dot(att[g], att_places(g))
        att_wide = att_wide.astype(BF16)
        for part in range(4):
            block_rows = dot_tn(att_wide[:, 256 * part : 256 * part + 256], gmix[...]).astype(BF16)
            o_low[part // 2, pl.ds(2 * (part % 2), 2), :, :, pl.ds(0, WIDTH)] = block_rows.reshape(2, 4, 32, WIDTH)
        tiny = dot(small[...].astype(BF16), norm_places()).T.astype(BF16)
        o_low[:, :, :, :, pl.ds(WIDTH, 128)] = tiny.reshape(2, 4, 4, 32, 128)
        core_o = mail.go(o_low.at[1 - me.c], o_core, mail.block(1), me.core_peer())

        wait_all(fars)
        near_right = gwi.at[2 * right, me.c]
        near_right[...] = (near_right[...].astype(F32) + x_far[0].astype(F32)).astype(BF16)
        near_left = gwi.at[2 * left + 1, me.c]
        near_left[...] = (near_left[...].astype(F32) + x_far[1].astype(F32)).astype(BF16)
        ring_all = ring + [
            mail.go(near_right, x_near.at[0], s_ring + 2, me.x_peer(1)),
            mail.go(near_left, x_near.at[3], s_ring + 3, me.x_peer(3)),
        ]

        wait_all(das)
        grads = da[...].astype(F32)
        product = grads * own[...].astype(F32)
        sums = jnp.zeros((512, 128), F32)
        for h in range(3):
            at = (128, 192, 64)[h]
            inside = (lanes >= at) & (lanes < at + 64)
            total = jnp.sum(jnp.where(inside, product, 0.0), axis=1, keepdims=True)
            for half in range(2):
                factor = scale[:, pl.ds(3 * half + h, 1)]
                sums = jnp.where(iota((512, 128), 1) == 3 * half + h, total * factor, sums)
        drow[...] = sums.T
        accb[...] = jnp.zeros(accb.shape, F32)
        dq[...] = jnp.zeros(dq.shape, F32)
        s_ckv, s_ykv = mail.block(8), mail.block(4)

        def core_copy(rel, xx, y):
            part = rows(4 * xx + 2 * y + 1 - me.c, TOK)
            return mail.copy(dkv.at[part], core_kv.at[4 * rel + xx], s_ckv + 4 * rel + xx, me.core_peer())

        def attend(rel, y):
            half = 1 - rel
            for h in range(3):
                at = (128, 192, 64)[h]
                inside = (lanes >= at) & (lanes < at + 64)
                kept = jnp.where(inside, da[...].astype(F32), 0.0) * scale[:, pl.ds(3 * half + h, 1)]
                doexp[pl.ds(512 * h, 512), :] = kept.astype(BF16)

            def one(xx, carry):
                span = rows(2 * xx + y, 256)
                keys = kv[span, pl.ds(0, 256)]
                values = kv[span, pl.ds(128, 256)]
                for h in range(3):
                    cols = pl.ds(512 * h, 512)
                    back = dot_nt(values, doexp[cols, :])
                    part = p_ref[span, cols].astype(F32) * (back - drow[pl.ds(3 * half + h, 1), :])
                    ds[:, cols] = part.astype(BF16)
                    for k in range(2):
                        for t in range(4):
                            kind = jnp.clip(4 * xx + 2 * y + k - (4 * t + 2 * me.y + me.c), -2, 2) + 2
                            accb[h, kind] += part[128 * k : 128 * k + 128, 128 * t : 128 * t + 128]
                for h in range(3):
                    cols = pl.ds(512 * h, 512)
                    dq[pl.ds(64 * h, 64), :] += dot_tn(keys, ds[:, cols])[64 * h : 64 * h + 64]
                gk = dot(ds[...], qexp[...])
                gv = dot(p_ref[span, :], doexp[...])
                dkv[span, pl.ds(0, 128)] = gk[:, :128].astype(BF16)
                dkv[span, pl.ds(128, 128)] = (gk[:, 128:] + gv[:, :128]).astype(BF16)
                dkv[span, pl.ds(256, 128)] = gv[:, 128:].astype(BF16)
                core_copy(rel, xx, y).start()
                return carry

            lax.fori_loop(0, 4, one, 0, unroll=2)

        attend(0, 1 - me.y)

        def to_y(xx):
            return mail.copy(y_send.at[xx], y_kv.at[xx], s_ykv + xx, me.y_peer())

        def forward_y(xx, carry):
            core_copy(0, xx, 1 - me.y).wait_recv()
            part = dkv[rows(4 * xx + 2 * (1 - me.y) + me.c, TOK), :].astype(F32)
            y_send[xx] = (part + core_kv[xx].astype(F32)).astype(BF16)
            to_y(xx).start()
            return carry

        lax.fori_loop(0, 4, forward_y, 0)
        y_rest = [over_y(2, left), over_y(3, me.x)]

        class Sum:
            def __init__(self, low, core, z_got, mid2, q_got, last, x_got, first):
                self.low, self.core, self.z_got = low, core, z_got
                self.mid2, self.q_got, self.last, self.x_got = mid2, q_got, last, x_got
                self.first = first

            def peer(self, axis, k):
                return me.z_peer(k) if axis == "z" else me.q_peer(k)

            def of(self, axis, k):
                return me.z_of(k) if axis == "z" else me.q_of(k)

            def begin(self):
                self.copies = [mail.go(self.low.at[1 - me.c], self.core, mail.block(1), me.core_peer())]

            def part(self, index):
                return self.low.at[me.c, :, index] if self.first == "q" else self.low.at[me.c, index]

            def stage_one(self):
                wait_all(self.copies)
                total = self.low[me.c].astype(F32) + self.core[...].astype(F32)
                self.low[me.c] = total.astype(BF16)
                base = mail.block(4)
                self.copies = [
                    mail.go(self.part(self.of(self.first, k)), self.z_got.at[k - 1], base + k, self.peer(self.first, k))
                    for k in near
                ]

            def stage_two(self):
                wait_all(self.copies)
                total = self.part(me.q if self.first == "q" else me.z)[...].astype(F32)
                for k in range(3):
                    total = total + self.z_got[k].astype(F32)
                self.mid2[...] = total.astype(BF16)
                base = mail.block(4)
                second = "z" if self.first == "q" else "q"
                self.copies = [
                    mail.go(self.mid2.at[self.of(second, k)], self.q_got.at[k - 1], base + k, self.peer(second, k))
                    for k in near
                ]

            def stage_three(self):
                wait_all(self.copies)
                total = self.mid2[me.z if self.first == "q" else me.q].astype(F32)
                for k in range(3):
                    total = total + self.q_got[k].astype(F32)
                self.last[...] = total
                base = mail.block(4)
                self.copies = [
                    mail.go(self.last.at[rows(me.x_of(k), 8)], self.x_got.at[me.x], base + k, me.x_peer(k)) for k in near
                ]
                self.x_got[me.x] = self.last[rows(me.x, 8), :]

            def finish(self):
                wait_all(self.copies)

        of_out = Sum(o_low, o_core, o_z, o_mid2, o_q, o_last, o_x, "z")
        of_out.copies = [core_o]
        of_q = Sum(q_low, q_core, q_z, q_mid2, q_q, q_last, q_x, "z")
        of_kv = Sum(k_low, k_core, k_z, k_mid2, k_q, k_last, k_x, "z")
        of_out.stage_one()

        attend(1, me.y)

        fin_q[...] = (dq[...] * SCALE).T.astype(BF16)
        s_xq, s_xkv = mail.block(4), mail.block(4)
        home = [mail.go(fin_q.at[rows(me.x_of(k), TOK)], home_q.at[me.x], s_xq + k, me.x_peer(k)) for k in near]
        home_q[me.x] = fin_q[mine, :]

        def over_x(xx):
            total = gwo[xx, me.y, me.c].astype(F32) + got_out[1, xx].astype(F32) + y_out[xx].astype(F32)
            y_out[xx] = total.astype(BF16)

        keep["core_out", 1].wait_recv()
        wait_all(ys_out)
        over_x(far)
        over_x(right)
        s_zf, s_zn = mail.block(2), mail.block(4)
        z_fars = [
            mail.go(y_out.at[far, pl.ds(0, 96)], z_far.at[0], s_zf, me.x_peer(1)),
            mail.go(y_out.at[far, pl.ds(96, 96)], z_far.at[1], s_zf + 1, me.x_peer(3)),
        ]
        z_ring = [mail.go(y_out.at[right, pl.ds(96, 96)], z_near.at[1], s_zn, me.x_peer(1))]
        wait_all(keep["norms"])
        for part in range(4):
            span = pl.ds(256 * part, 256)
            block_rows = dot_tn(norm_all[:, span], fin_q[...]).astype(BF16)
            q_low[part // 2, pl.ds(2 * (part % 2), 2)] = block_rows.reshape(2, 4, 32, fin_q.shape[1])
        of_q.begin()
        for k in near + [0]:
            xx = me.x_of(k)
            core_copy(1, xx, me.y).wait_recv()
            to_y(xx).wait_recv()
            part = dkv[rows(4 * xx + 2 * me.y + me.c, TOK), :].astype(F32)
            part = (part + core_kv[4 + xx].astype(F32) + y_kv[xx].astype(F32)).astype(BF16)
            fin_kv[rows(xx, TOK), :] = part
            if k:
                home.append(mail.go(fin_kv.at[rows(xx, TOK)], home_kv.at[me.x], s_xkv + k, me.x_peer(k)))
            else:
                home_kv[me.x] = part
        for part in range(4):
            span = pl.ds(256 * part, 256)
            block_rows = dot_tn(norm_all[:, span], fin_kv[...]).astype(BF16)
            k_low[part // 2, pl.ds(2 * (part % 2), 2)] = block_rows.reshape(2, 4, 32, fin_kv.shape[1])
        of_kv.begin()
        of_q.stage_one()
        of_out.stage_two()

        of_kv.stage_one()
        before, center, after = bucket_tile(tile - 128), bucket_tile(tile), bucket_tile(tile + 128)

        def bucket_sum(b, carry):
            for h in range(3):
                near_sum = (
                    jnp.where(before == b, accb[h, 1], 0.0)
                    + jnp.where(center == b, accb[h, 2], 0.0)
                    + jnp.where(after == b, accb[h, 3], 0.0)
                )
                trow[h, pl.ds(b, 1), :] = jnp.sum(near_sum, axis=0, keepdims=True)
            return carry

        lax.fori_loop(0, BUCKETS, bucket_sum, 0, unroll=4)
        table = jnp.zeros((BUCKETS, 128), F32)
        for h in range(3):
            trow[h, pl.ds(BUCKETS // 2 - 1, 1), :] += jnp.sum(accb[h, 0], axis=0, keepdims=True)
            trow[h, pl.ds(BUCKETS - 1, 1), :] += jnp.sum(accb[h, 4], axis=0, keepdims=True)
            total = jnp.sum(trow[h], axis=1, keepdims=True)
            table = jnp.where(iota((BUCKETS, 128), 1) == 3 * me.x + h, total, table)
        tabs[0] = table
        t_core = mail.go(tabs.at[0], t_got.at[0], mail.block(1), me.core_peer())

        wait_all(ring_all)
        for j in range(2):
            total = gwi[2 * me.x + j, me.c].astype(F32) + x_near[j].astype(F32) + x_near[2 + j].astype(F32)
            gwi[2 * me.x + j, me.c] = total.astype(BF16)
        y_hop = mail.go(gwi.at[2 * me.x + 1 - me.y, me.c], y_in, mail.block(1), me.y_peer())
        wait_all(y_rest)
        over_x(left)
        over_x(me.x)
        z_ring.append(mail.go(y_out.at[left, pl.ds(0, 96)], z_near.at[2], s_zn + 1, me.x_peer(3)))
        of_q.stage_two()
        of_out.stage_three()
        t_core.wait_recv()
        tabs[1] = tabs[0] + t_got[0]
        s_tz = mail.block(4)
        ts = [mail.go(tabs.at[1], t_got.at[k], s_tz + k, me.z_peer(k)) for k in near]
        of_kv.stage_two()

        wait_all(home)

        def piece(p, j):
            g, t = j // 3, j % 3
            if p == 0:
                return home_q[g, :, pl.ds(128 * (t // 2), 128)].astype(F32), t % 2
            if p == 1:
                return home_kv[g, :, pl.ds(128 * (t // 2), 128)].astype(F32), t % 2
            at, half = ((2, 0), (2, 1), (1, 1))[t]
            return home_kv[g, :, pl.ds(128 * at, 128)].astype(F32), half

        for p in range(3):
            for n in range(6):
                first, half_first = piece(p, 2 * n)
                second, half_second = piece(p, 2 * n + 1)
                dproj[p, :, pl.ds(128 * n, 128)] = pair(first, half_first, second, half_second).astype(BF16)
        gnorm = dot_nt(dproj[0], w_ref[0]) + dot_nt(dproj[1], w_ref[1]) + dot_nt(dproj[2], w_ref[2])
        inputs = inp_ref[...].astype(F32)
        root1 = lax.rsqrt(jnp.mean(inputs * inputs, axis=1, keepdims=True) + EPSILON)
        gain1 = gain1_ref[...].reshape(1, WIDTH)
        u = gain1 * gnorm
        mean = jnp.mean(u * inputs, axis=1, keepdims=True)
        gin_ref[...] = gmid[...] + root1 * u - inputs * (root1 * root1 * root1 * mean)

        of_q.stage_three()
        wait_all(ts)
        tabs[2] = tabs[1] + t_got[1] + t_got[2] + t_got[3]
        s_tq = mail.block(4)
        ts = [mail.go(tabs.at[2], t_got.at[3 + k], s_tq + k, me.q_peer(k)) for k in near]
        wait_all(z_fars)
        y_out[right, pl.ds(0, 96), :] = (
            y_out[right, pl.ds(0, 96), :].astype(F32) + z_far[0].astype(F32)
        ).astype(BF16)
        y_out[left, pl.ds(96, 96), :] = (
            y_out[left, pl.ds(96, 96), :].astype(F32) + z_far[1].astype(F32)
        ).astype(BF16)
        z_ring = z_ring + [
            mail.go(y_out.at[right, pl.ds(0, 96)], z_near.at[0], s_zn + 2, me.x_peer(1)),
            mail.go(y_out.at[left, pl.ds(96, 96)], z_near.at[3], s_zn + 3, me.x_peer(3)),
        ]
        of_kv.stage_three()
        wait_all(ts)
        tabs[3] = tabs[2] + t_got[4] + t_got[5] + t_got[6]
        s_tx = mail.block(4)
        ts = [mail.go(tabs.at[3], t_got.at[6 + k], s_tx + k, me.x_peer(k)) for k in near]

        row = iota((16, WIDTH), 0)
        pick = (iota((16, WIDTH), 1) == 6 * (8 * me.i + me.e) + row) & (row < 6)
        pick = pick.astype(F32).astype(BF16)
        picked = [dot(pick, w_ref[p])[:8] for p in range(3)]
        gain_col = jnp.sum(jnp.where(pick[:8].astype(F32) > 0, gain1, 0.0), axis=1, keepdims=True)

        of_out.finish()
        total = o_x[0] + o_x[1] + o_x[2] + o_x[3]
        gout_ref[...] = total
        y_hop.wait_recv()
        gwin_ref[...] = gwi[2 * me.x + me.y, me.c].astype(F32) + y_in[...].astype(F32)
        wait_all(z_ring)
        gwout_ref[pl.ds(0, 96), :] = (
            y_out[me.x, pl.ds(0, 96), :].astype(F32) + z_near[0].astype(F32) + z_near[2].astype(F32)
        )
        gwout_ref[pl.ds(96, 96), :] = (
            y_out[me.x, pl.ds(96, 96), :].astype(F32) + z_near[1].astype(F32) + z_near[3].astype(F32)
        )
        wait_all(ts)
        gtable_ref[...] = tabs[3] + t_got[7] + t_got[8] + t_got[9]
        of_q.finish()
        of_kv.finish()

        def found(p, j):
            g, t = j // 3, j % 3
            if p == 0:
                return q_x[g, :, pl.ds(128 * (t // 2), 128)], t % 2
            if p == 1:
                return k_x[g, :, pl.ds(128 * (t // 2), 128)], t % 2
            at, half = ((2, 0), (2, 1), (1, 1))[t]
            return k_x[g, :, pl.ds(128 * at, 128)], half

        with_gain = jnp.zeros((8, 1), F32)
        for p in range(3):
            for n in range(6):
                first, half_first = found(p, 2 * n)
                second, half_second = found(p, 2 * n + 1)
                cols = pl.ds(128 * n, 128)
                part = pair(first, half_first, second, half_second)
                gqkv_ref[p, :, cols] = part
                with_gain = with_gain + jnp.sum(
                    part * picked[p][:, 128 * n : 128 * n + 128], axis=1, keepdims=True
                )
        real = iota((8, 1), 0) < 6
        gain_ref[...] = jnp.where(real, with_gain / jnp.where(real, gain_col, 1.0), 0.0) * jnp.ones((8, 128), F32)
        for copy in mail.started:
            copy.wait_send()
        for rel, y in ((0, 1 - me.y), (1, me.y)):
            for xx in range(4):
                core_copy(rel, xx, y).wait_send()
        for xx in range(4):
            to_y(xx).wait_send()

    pl.run_scoped(
        rest,
        pltpu.VMEM((1536, 256), BF16),
        pltpu.VMEM((128, 512), F32),
        pltpu.VMEM((3, 5, 128, 128), F32),
        pltpu.VMEM((256, 1536), BF16),
        pltpu.VMEM((256, 512), F32),
        pltpu.VMEM((2048, 384), BF16),
        pltpu.VMEM((4, TOK, 384), BF16),
        pltpu.VMEM((512, 384), BF16),
        pltpu.VMEM((512, 256), BF16),
        pltpu.VMEM((3, TOK, WIDTH), BF16),
        pltpu.VMEM((2, 4, 4, 32, WIDTH + 128), BF16),
        pltpu.VMEM((2, 4, 4, 32, 256), BF16),
        pltpu.VMEM((2, 4, 4, 32, 384), BF16),
    )


def sum_buffers(width):
    return [
        pltpu.VMEM((4, 4, 32, width), BF16),
        pltpu.VMEM((3, 4, 32, width), BF16),
        pltpu.VMEM((4, 32, width), BF16),
        pltpu.VMEM((3, 32, width), BF16),
        pltpu.VMEM((32, width), F32),
        pltpu.VMEM((4, 8, width), F32),
    ]


def layer(*arrays):
    shape = jax.ShapeDtypeStruct
    vm = pltpu.VMEM
    return pl.pallas_call(
        layer_kernel,
        out_shape=(
            shape((TOK, WIDTH), BF16),
            shape((TOK, WIDTH), F32),
            shape((48, FF), F32),
            shape((192, WIDTH), F32),
            shape((3, 8, WIDTH), F32),
            shape((8, WIDTH + 128), F32),
            shape((8, 128), F32),
            shape((BUCKETS, 128), F32),
        ),
        in_specs=[VMEM] * 3 + [SMEM] + [VMEM] * 4 + [ANY] * 2 + [VMEM],
        out_specs=(VMEM,) * 8,
        scratch_shapes=[
            vm((512, 1024), BF16),
            vm((TOK, 1024), BF16),
            vm((512, 256), BF16),
            vm((2048, 384), BF16),
            vm((1536, 256), BF16),
            vm((2048, 1536), BF16),
            vm((512, 128), F32),
            vm((512, 256), BF16),
            vm((4, TOK, 256), BF16),
            vm((TOK, WIDTH), F32),
            vm((2 * TOK, 16 * CAP), BF16),
            vm((16 * CAP, WIDTH), BF16),
            vm((16 * CAP, WIDTH), BF16),
            vm((16 * CAP, WIDTH), BF16),
            vm((8, 2, 48, FF), BF16),
            vm((4, 2, 2, 192, WIDTH), BF16),
            vm((TOK, WIDTH), F32),
            vm((TOK, WIDTH), BF16),
            vm((4, TOK, 256), BF16),
            vm((512, 256), BF16),
            vm((8, TOK, 384), BF16),
            vm((4, TOK, 384), BF16),
            vm((4, TOK, 256), BF16),
            vm((4, TOK, 384), BF16),
            vm((128, WIDTH), F32),
        ]
        + sum_buffers(WIDTH + 128)
        + sum_buffers(256)
        + sum_buffers(384)
        + [
            vm((3, BUCKETS, 128), F32),
            vm((4, BUCKETS, 128), F32),
            vm((10, BUCKETS, 128), F32),
            vm((8, 48, FF), BF16),
            vm((2, 4, 192, WIDTH), BF16),
            vm((2, 48, FF), BF16),
            vm((4, 48, FF), BF16),
            vm((48, FF), BF16),
            vm((4, 192, WIDTH), BF16),
            vm((2, 96, WIDTH), BF16),
            vm((4, 96, WIDTH), BF16),
            pltpu.SemaphoreType.DMA((2,)),
            pltpu.SemaphoreType.DMA((SEMS,)),
            pltpu.SemaphoreType.DMA((SEMS,)),
        ],
        compiler_params=pltpu.CompilerParams(
            collective_id=0, has_side_effects=True, vmem_limit_bytes=VMEM_LIMIT
        ),
    )(*arrays)


def place_kernel(
    y, gin, gwin, gwout, gqkv, gout, gain, table,
    y_ref, gin_ref, gwin_ref, gwout_ref, gqkv_ref, gout_ref, gain1_ref, gain2_ref, router_ref, table_ref,
):
    y_ref[...] = y[...]
    gin_ref[...] = gin[...]
    gwin_ref[...] = gwin[...]
    gwout_ref[...] = gwout[...]
    gqkv_ref[...] = gqkv[:, :6, :]
    gout_ref[...] = gout[:6, :WIDTH]
    gain1_ref[...] = gain[...].T[:1, :6]
    others = gout[:, WIDTH:].T
    gain2_ref[...] = others[:1, :6]
    router_ref[...] = gout[:6, WIDTH + 8 : WIDTH + 16]
    table_ref[...] = table[...].T[:HEADS]


def place(*arrays):
    shape = jax.ShapeDtypeStruct
    return pl.pallas_call(
        place_kernel,
        out_shape=(
            shape((TOK, WIDTH), BF16),
            shape((TOK, WIDTH), F32),
            shape((48, FF), F32),
            shape((192, WIDTH), F32),
            shape((3, 6, WIDTH), F32),
            shape((6, WIDTH), F32),
            shape((1, 6), F32),
            shape((1, 6), F32),
            shape((6, 8), F32),
            shape((HEADS, BUCKETS), F32),
        ),
        in_specs=[VMEM] * 8,
        out_specs=(VMEM,) * 10,
        compiler_params=pltpu.CompilerParams(vmem_limit_bytes=VMEM_LIMIT),
    )(*arrays)


def body(
    block_input, gain_one, qkv_weight, out_weight, rel_table, gain_two, router_weight, routes, w_in, w_out, cotangent
):
    parts = layer(
        block_input[0], gain_one, qkv_weight, rel_table.T, out_weight, gain_two, router_weight.T,
        routes.reshape(1, TOK), w_in.reshape(8, 2, 48, FF), w_out.reshape(4, 2, 2, 192, WIDTH), cotangent[0],
    )
    y, gin, gwin, gwout, gqkv, gout, gain1, gain2, router, table = place(*parts)
    return (
        y[None],
        gin[None],
        gain1.reshape(6),
        gqkv,
        gout,
        table.T,
        gain2.reshape(6),
        router,
        gwin[None],
        gwout[None],
    )


def solution(mesh):
    tokens = P("expert", "ctx", None)
    split = P(("ctx", "expert"))
    return jax.shard_map(
        body,
        mesh=mesh,
        in_specs=(
            tokens, P(), P(), P(), P(), P(), P(), tokens, P("expert", None, None), P("expert", None, None), tokens,
        ),
        out_specs=(
            tokens, tokens, split, P(None, ("ctx", "expert"), None), split, P(), split, split, tokens, tokens,
        ),
        check_vma=False,
    )
```

```python
import jax
import jax.numpy as jnp
import numpy as np
from jax import lax
from jax.experimental import pallas as pl
from jax.experimental.pallas import tpu as pltpu
from jax.sharding import PartitionSpec as P

HEADS = 12
HEAD_DIM = 64
BUCKETS = 32
MAX_DISTANCE = 128
EPSILON = 1e-06
SCALE = HEAD_DIM ** (-0.5)
TOK = 128
WIDTH = 768
FF = 3072
CAP = 24
F32 = jnp.float32
BF16 = jnp.bfloat16
MESH = pl.DeviceIdType.MESH
VMEM = pl.BlockSpec(memory_space=pltpu.VMEM)
SMEM = pl.BlockSpec(memory_space=pltpu.SMEM)
ANY = pl.BlockSpec(memory_space=pl.ANY)
VMEM_LIMIT = 63 * 1024 * 1024


def bucket_edges(buckets, reach):
    half = buckets // 2
    exact = half // 2
    spans = np.arange(1, reach + 1)
    spread = np.log(np.maximum(spans, exact) / exact) / np.log(reach / exact) * (half - exact)
    large = np.minimum(exact + spread.astype(np.int64), half - 1)
    level = np.where(spans < exact, spans, large)
    return [int(np.argmax(level >= b)) + 1 for b in range(1, half)]


EDGES = bucket_edges(BUCKETS, MAX_DISTANCE)


def dot(a, b):
    return jnp.dot(a, b, preferred_element_type=F32)


def dot_nt(a, b):
    return lax.dot_general(a, b, (((1,), (1,)), ((), ())), preferred_element_type=F32)


def dot_tn(a, b):
    return lax.dot_general(a, b, (((0,), (0,)), ((), ())), preferred_element_type=F32)


def iota(shape, dim):
    return lax.broadcasted_iota(jnp.int32, shape, dim)


class Place:
    def __init__(self):
        self.i = lax.axis_index("ctx")
        self.e = lax.axis_index("expert")
        self.x = lax.div(self.i, 4)
        self.y = lax.rem(lax.div(self.i, 2), 2)
        self.c = lax.rem(self.i, 2)
        self.z = lax.div(self.e, 2)
        self.h = lax.rem(self.e, 2)
        self.q = self.h * 2 + self.y

    def x_of(self, step):
        return lax.rem(self.x + 4 + step, 4)

    def x_peer(self, step):
        return (4 * self.x_of(step) + 2 * self.y + self.c, self.e)

    def core_peer(self):
        return (4 * self.x + 2 * self.y + 1 - self.c, self.e)

    def y_peer(self):
        return (4 * self.x + 2 * (1 - self.y) + self.c, self.e)

    def z_of(self, step):
        return lax.rem(self.z + 4 + step, 4)

    def z_peer(self, step):
        return (self.i, 2 * self.z_of(step) + self.h)

    def q_of(self, step):
        return lax.rem(self.q + 4 + step, 4)

    def q_peer(self, step):
        q = self.q_of(step)
        return (4 * self.x + 2 * lax.rem(q, 2) + self.c, 2 * self.z + lax.div(q, 2))

    def corner_peer(self):
        return (4 * self.x + 2 * (1 - self.y) + self.c, 2 * self.z + 1 - self.h)

    def e_of(self, step):
        return lax.rem(self.e + 8 + step, 8)

    def e_peer(self, step):
        return (self.i, self.e_of(step))


def greet(peers):
    barrier = pltpu.get_barrier_semaphore()
    for peer in peers:
        pl.semaphore_signal(barrier, inc=1, device_id=peer, device_id_type=MESH)
    pl.semaphore_wait(barrier, len(peers))


def rcopy(src, dst, send, recv, slot, peer):
    return pltpu.make_async_remote_copy(
        src_ref=src,
        dst_ref=dst,
        send_sem=send.at[slot],
        recv_sem=recv.at[slot],
        device_id=peer,
        device_id_type=MESH,
    )


def rows(index, size):
    return pl.ds(pl.multiple_of(index * size, size), size)


def pair(first, half_first, second, half_second):
    if first is second and (half_first, half_second) == (0, 1):
        return first
    low = pltpu.roll(first, 64, 1) if half_first else first
    high = second if half_second else pltpu.roll(second, 64, 1)
    return jnp.where(iota(low.shape, 1) < 64, low, high)


def norm_places():
    col = iota((1, 1024), 1)
    r = col & 7
    xx = (col >> 3) & 3
    yl = (col >> 5) & 1
    e = (((col >> 7) & 3) << 1) + ((col >> 6) & 1)
    c = (col >> 9) & 1
    d = jnp.where(r < 6, 192 * xx + 96 * yl + 48 * c + 6 * e + r, -1)
    return (iota((WIDTH, 1024), 0) == d).astype(F32).astype(BF16)


def att_places(group):
    col = iota((1, 1024), 1)
    r = col & 7
    e = (((col >> 7) & 3) << 1) + ((col >> 6) & 1)
    f = 96 * ((col >> 5) & 1) + 48 * ((col >> 9) & 1) + 6 * e + r
    f = jnp.where((r < 6) & (((col >> 3) & 3) == group), f, -1)
    lane = iota((256, 1024), 0)
    feature = jnp.where(lane >= 128, lane - 128, jnp.where(lane >= 64, lane + 64, -2))
    return (feature == f).astype(F32).astype(BF16)


def bucket_tile(offset):
    length = jnp.abs(offset)
    level = jnp.where(offset > 0, BUCKETS // 2, 0)
    for edge in EDGES:
        level = level + (length >= edge).astype(jnp.int32)
    return level


SEMS = 192


class Mail:
    def __init__(self, send, recv):
        self.send, self.recv, self.used, self.started = send, recv, 0, []

    def block(self, count):
        base = self.used
        self.used += count
        assert self.used <= SEMS
        return base

    def copy(self, src, dst, slot, peer):
        return rcopy(src, dst, self.send, self.recv, slot, peer)

    def go(self, src, dst, slot, peer):
        copy = self.copy(src, dst, slot, peer)
        copy.start()
        self.started.append(copy)
        return copy

    def sent(self, copy):
        copy.wait_send()
        self.started = [other for other in self.started if other is not copy]

    def go_later(self, make):
        copy = Made(lambda: self.copy(*make()))
        copy.make().start()
        self.started.append(copy)
        return copy


class Made:
    def __init__(self, make):
        self.make = make

    def wait_recv(self):
        self.make().wait_recv()

    def wait_send(self):
        self.make().wait_send()


def wait_all(copies):
    for copy in copies:
        copy.wait_recv()


def layer_kernel(
    inp_ref, gain1_ref, w_ref, table_ref, out_w_ref, gain2_ref, router_ref, routes_ref, w_in_hbm, w_out_hbm, cot_ref,
    y_ref, gin_ref, gwin_ref, gwout_ref, gqkv_ref, gout_ref, gain_ref, gtable_ref,
    norm_all, norm_own, q_all, kv, qexp, p_ref, scale, own, att,
    middle, select, rows_out, rows_got, back_got, gwi, gwo, gmid, gmix, da_send, da,
    core_kv, y_kv, home_q, home_kv, small,
    o_core, o_z, o_mid2, o_q, o_last, o_x,
    q_core, q_z, q_mid2, q_q, q_last, q_x,
    k_core, k_z, k_mid2, k_q, k_last, k_x,
    trow, tabs, t_got, got_in, got_out, x_far, x_near, y_in, y_out, z_far, z_near,
    local, send, recv,
):
    me = Place()
    mail = Mail(send, recv)
    near = [1, 3, 2]
    others = [1, 7, 2, 6, 3, 5, 4]
    barrier = pltpu.get_barrier_semaphore()
    peers = [me.x_peer(k) for k in near] + [me.core_peer(), me.y_peer(), me.corner_peer()]
    peers = peers + [me.e_peer(k) for k in others]
    for peer in peers:
        pl.semaphore_signal(barrier, inc=1, device_id=peer, device_id_type=MESH)

    inputs = inp_ref[...].astype(F32)
    root1 = lax.rsqrt(jnp.mean(inputs * inputs, axis=1, keepdims=True) + EPSILON)
    normed = (inputs * root1 * gain1_ref[...].reshape(1, WIDTH)).astype(BF16)
    proj = [dot(normed, w_ref[p]) for p in range(3)]

    def join(p, a, s, b):
        first = proj[p][:, 128 * (a // 2) : 128 * (a // 2) + 128]
        second = first if (p == s and a // 2 == b // 2) else proj[s][:, 128 * (b // 2) : 128 * (b // 2) + 128]
        return pair(first, a % 2, second, b % 2)

    block = rows(me.i, TOK)
    mine = rows(me.x, TOK)
    s_kv, s_q, s_y, s_c, s_f = [mail.block(4) for _ in range(5)]
    def source(step, y, c):
        return rows(4 * me.x_of(-step) + 2 * y + c, TOK)

    ys, cs = {}, {}

    def pass_on(step):
        def to(slot, peer):
            part = kv.at[source(step, me.y, me.c)]
            return part, part, slot + step, peer()

        ys[step] = mail.go_later(lambda: to(s_y, me.y_peer))
        cs[step] = mail.go_later(lambda: to(s_c, me.core_peer))

    tile = iota((128, 128), 0) - iota((128, 128), 1)
    lanes = iota((512, 256), 1)
    def attention(s_ref, bias, m_ref, l_ref, acc, o_part, o_t, kv_send, q_send, q_turned):
        for g in range(4):
            a = 3 * g
            kv_send[g, :, pl.ds(0, 128)] = join(1, a, 1, a + 1).astype(BF16)
            kv_send[g, :, pl.ds(128, 128)] = join(1, a + 2, 2, a + 2).astype(BF16)
            kv_send[g, :, pl.ds(256, 128)] = join(2, a, 2, a + 1).astype(BF16)
            q_send[g, :, pl.ds(0, 128)] = join(0, a, 0, a + 1).astype(BF16)
            q_send[g, :, pl.ds(128, 128)] = jnp.where(iota((TOK, 128), 1) < 64, join(0, a + 2, 0, a + 2), 0.0).astype(BF16)
        pl.semaphore_wait(barrier, len(peers))
        kvs = {k: mail.go(kv_send.at[me.x_of(k)], kv.at[block], s_kv + k, me.x_peer(k)) for k in near}
        kv[block, :] = kv_send[me.x]
        qs = {k: mail.go(q_send.at[me.x_of(k)], q_all.at[mine], s_q + k, me.x_peer(k)) for k in near}
        q_all[mine, :] = q_send[me.x]

        pass_on(0)
        norm_own[...] = dot(normed, norm_places()).astype(BF16)
        norm_all[mine, :] = norm_own[...]
        for h in range(3):
            head = 3 * me.x + h

            def chain(first, n):
                value = jnp.full((128, 128), 1.0, F32) * table_ref[head, first]
                for level, edge in enumerate(EDGES):
                    value = jnp.where(n >= edge, table_ref[head, first + level + 1], value)
                return value

            bias[h, 0] = jnp.full((128, 128), 1.0, F32) * table_ref[head, BUCKETS // 2 - 1]
            bias[h, 1] = chain(0, 128 - tile)
            bias[h, 2] = jnp.where(tile > 0, chain(BUCKETS // 2, tile), chain(0, -tile))
            bias[h, 3] = chain(BUCKETS // 2, 128 + tile)
            bias[h, 4] = jnp.full((128, 128), 1.0, F32) * table_ref[head, BUCKETS - 1]
        m_ref[...] = jnp.full(m_ref.shape, -jnp.inf, F32)
        l_ref[...] = jnp.zeros(l_ref.shape, F32)
        for k in near:
            kvs[k].wait_recv()
            pass_on(k)
        wait_all(qs.values())
        queries = q_all[...].astype(F32) * SCALE
        for h in range(3):
            inside = (lanes >= 64 * h) & (lanes < 64 * h + 64)
            part = jnp.where(inside, queries, 0.0)
            qexp[pl.ds(512 * h, 512), :] = part.astype(BF16)
            q_turned[:, pl.ds(512 * h, 512)] = part.T.astype(BF16)

        def score(steps, half, y):
            for h in range(3):
                turned = q_turned[:, pl.ds(512 * h, 512)]

                def one(step, carry):
                    xx = me.x_of(-step)
                    s = dot(kv[rows(2 * xx + y, 256), pl.ds(0, 256)], turned)
                    for k in range(2):
                        b = 4 * xx + 2 * y + k
                        for t in range(4):
                            kind = jnp.clip(b - (4 * t + 2 * me.y + me.c), -2, 2) + 2
                            part = s[128 * k : 128 * k + 128, 128 * t : 128 * t + 128] + bias[h, kind]
                            cols = pl.ds(128 * t, 128)
                            s_ref[h, rows(2 * xx + k, TOK), cols] = part
                            m_ref[half, h, :, cols] = jnp.maximum(
                                m_ref[half, h, :, cols], jnp.max(part.reshape(16, 8, 128), axis=0)
                            )
                    return carry

                lax.fori_loop(steps[0], steps[1], one, 0, unroll=True)

        def weigh(half, y):
            for h in range(3):
                top = jnp.max(m_ref[half, h], axis=0, keepdims=True)
                acc[...] = jnp.zeros(acc.shape, F32)

                def one(xx, carry):
                    part = jnp.exp(s_ref[h, rows(xx, 256), :] - top)
                    l_ref[half, h] += jnp.sum(part.reshape(32, 8, 512), axis=0)
                    low = part.astype(BF16)
                    span = rows(2 * xx + y, 256)
                    p_ref[span, pl.ds(512 * h, 512)] = low
                    acc[...] += dot_tn(kv[span, pl.ds(128, 256)], low)
                    return carry

                lax.fori_loop(0, 4, one, 0, unroll=True)
                at = pl.ds((128, 192, 64)[h], 64)
                o_part[half, at, :] = acc[at, :]

        cs[0].wait_recv()
        score((0, 1), 0, me.y)
        for k in near:
            cs[k].wait_recv()
        score((1, 4), 0, me.y)
        fs = {}
        for k in (0, 1, 3, 2):
            ys[k].wait_recv()

            def to(k=k):
                part = kv.at[source(k, 1 - me.y, me.c)]
                return part, part, s_f + k, me.core_peer()

            fs[k] = mail.go_later(to)
        weigh(0, me.y)
        wait_all(fs.values())
        score((0, 4), 1, 1 - me.y)
        weigh(1, 1 - me.y)

        factors = jnp.zeros((128, 512), F32)
        which = iota((128, 512), 0)
        o_t[...] = jnp.zeros(o_t.shape, F32)
        for h in range(3):
            tops = [jnp.max(m_ref[half, h], axis=0, keepdims=True) for half in range(2)]
            top = jnp.maximum(tops[0], tops[1])
            fade = [jnp.exp(t - top) for t in tops]
            sums = [jnp.sum(l_ref[half, h], axis=0, keepdims=True) for half in range(2)]
            inv = 1.0 / (sums[0] * fade[0] + sums[1] * fade[1])
            fade = [f * inv for f in fade]
            at = pl.ds((128, 192, 64)[h], 64)
            o_t[at, :] = o_part[0, at, :] * fade[0] + o_part[1, at, :] * fade[1]
            for half in range(2):
                factors = jnp.where(which == 3 * half + h, fade[half], factors)
        scale[...] = factors.T
        own[...] = o_t[...].T.astype(BF16)
        for copy in list(kvs.values()) + list(qs.values()):
            mail.sent(copy)

    pl.run_scoped(
        attention,
        pltpu.VMEM((3, 1024, 512), F32),
        pltpu.VMEM((3, 5, 128, 128), F32),
        pltpu.VMEM((2, 3, 8, 512), F32),
        pltpu.VMEM((2, 3, 8, 512), F32),
        pltpu.VMEM((256, 512), F32),
        pltpu.VMEM((2, 256, 512), F32),
        pltpu.VMEM((256, 512), F32),
        pltpu.VMEM((4, TOK, 384), BF16),
        pltpu.VMEM((4, TOK, 256), BF16),
        pltpu.VMEM((256, 1536), BF16),
    )
    s_o, s_n = mail.block(4), mail.block(4)
    os = [mail.go(own.at[rows(me.x_of(k), TOK)], att.at[me.x], s_o + k, me.x_peer(k)) for k in near]
    att[me.x] = own[mine, :]

    s_there, s_home = mail.block(8), mail.block(8)
    gain2 = gain2_ref[...].reshape(1, WIDTH)
    slots = rows(me.e, 2 * CAP)
    keep = {}

    def experts(hidden, ginner, made, garr, arrived, gprod):
        load_in = pltpu.make_async_copy(w_in_hbm, gwi, local.at[0])
        load_in.start()
        load_out = pltpu.make_async_copy(w_out_hbm, gwo, local.at[1])
        load_out.start()
        wait_all(os)
        ns = [mail.go_later(lambda k=k: (norm_own, norm_all.at[mine], s_n + k, me.x_peer(k))) for k in near]
        mixed = inputs
        for g in range(4):
            mixed = mixed + dot(att[g, :, pl.ds(0, 128)], out_w_ref[pl.ds(192 * g + 64, 128), :])
            mixed = mixed + dot(att[g, :, pl.ds(128, 128)], out_w_ref[pl.ds(192 * g, 128), :])
        middle[...] = mixed
        root = lax.rsqrt(jnp.mean(mixed * mixed, axis=1, keepdims=True) + EPSILON)
        normed_two = (mixed * root * gain2).astype(BF16)
        logits = dot_nt(normed_two, router_ref[...])
        shifted = jnp.exp(logits - jnp.max(logits, axis=1, keepdims=True))
        router = shifted / jnp.sum(shifted, axis=1, keepdims=True)
        diagonal = iota((TOK, TOK), 0) == iota((TOK, TOK), 1)
        named = jnp.sum(jnp.where(diagonal, routes_ref[...].astype(F32), 0.0), axis=1, keepdims=True).astype(jnp.int32)
        chosen = (named == iota((TOK, 8), 1)).astype(F32)
        gate = jnp.sum(chosen * router, axis=1, keepdims=True)
        earlier = (iota((TOK, TOK), 0) > iota((TOK, TOK), 1)).astype(F32).astype(BF16)
        ranks = dot(earlier, chosen.astype(BF16))
        slot = jnp.sum(chosen * ranks, axis=1, keepdims=True).astype(jnp.int32)
        target = named * (2 * CAP) + slot
        column = iota((TOK, 16 * CAP), 1)
        select[pl.ds(0, TOK), :] = (column == target).astype(F32).astype(BF16)
        select[pl.ds(TOK, TOK), :] = (column == target + CAP).astype(F32).astype(BF16)
        dy = cot_ref[...].astype(F32)
        both = jnp.concatenate([normed_two, (gate * dy).astype(BF16)], axis=0)
        rows_out[...] = dot_tn(select[...], both).astype(BF16)
        there = [
            mail.go_later(
                lambda k=k: (rows_out.at[rows(me.e_of(k), 2 * CAP)], rows_got.at[slots], s_there + k, me.e_peer(k))
            )
            for k in others
        ]
        rows_got[slots, :] = rows_out[slots, :]
        made[...] = jnp.zeros(made.shape, F32)
        garr[...] = jnp.zeros(garr.shape, F32)
        load_in.wait()
        load_out.wait()
        wait_all(there)
        got = rows_got[...].astype(F32).reshape(8, 2 * CAP, WIDTH)
        arrived[...] = got[:, :CAP].reshape(8 * CAP, WIDTH).astype(BF16)
        gprod[...] = got[:, CAP:].reshape(8 * CAP, WIDTH).astype(BF16)
        chunk = 768

        def through(j, carry):
            cols = rows(j, chunk)
            for k in range(3):
                part = rows(3 * j + k, 256)
                inner = dot(arrived[...], gwi[:, :, :, part].reshape(WIDTH, 256))
                square = inner * inner
                slope = np.float32(np.sqrt(2 / np.pi))
                t = jnp.tanh(slope * inner * (1.0 + 0.044715 * square))
                half = 0.5 * (1.0 + t)
                hidden[:, part] = (inner * half).astype(BF16)
                w_out = gwo[j].reshape(chunk, WIDTH)[256 * k : 256 * k + 256]
                back = dot_nt(gprod[...], w_out)
                lean = half + 0.5 * inner * (1.0 - t * t) * slope * (1.0 + 3 * 0.044715 * square)
                ginner[:, part] = (lean * back).astype(BF16)
            made[...] += dot(hidden[:, cols], gwo[j].reshape(chunk, WIDTH))
            garr[...] += dot_nt(ginner[:, cols], gwi[:, :, :, cols].reshape(WIDTH, chunk))
            return carry

        lax.fori_loop(0, FF // chunk, through, 0, unroll=True)
        back = jnp.concatenate([made[...].reshape(8, CAP, WIDTH), garr[...].reshape(8, CAP, WIDTH)], axis=1)
        for copy in there:
            mail.sent(copy)
        rows_out[...] = back.reshape(16 * CAP, WIDTH).astype(BF16)
        keep["home"] = [
            mail.go_later(
                lambda k=k: (rows_out.at[rows(me.e_of(k), 2 * CAP)], back_got.at[slots], s_home + k, me.e_peer(k))
            )
            for k in others
        ]
        back_got[slots, :] = rows_out[slots, :]

        arrived_t = arrived[...].T

        def grads_in(j, carry):
            cols = rows(j, 256)
            gwi[:, :, :, cols] = dot(arrived_t, ginner[:, cols]).astype(BF16).reshape(8, 2, 48, 256)
            return carry

        lax.fori_loop(0, FF // 256, grads_in, 0, unroll=4)
        s_in = mail.block(1)
        keep["core_in"] = mail.go_later(lambda: (gwi.at[:, 1 - me.c], got_in, s_in, me.core_peer()))

        def grads_out(y):
            def one(xx, carry):
                part = dot_tn(hidden[:, rows(2 * xx + y, 384)], gprod[...])
                gwo[xx, y] = part.astype(BF16).reshape(2, 192, WIDTH)
                return carry

            lax.fori_loop(0, 4, one, 0, unroll=2)

        s_out = mail.block(2)
        for rel in range(2):
            grads_out(me.y if rel else 1 - me.y)
            keep["core_out", rel] = mail.go_later(
                lambda rel=rel: (
                    gwo.at[:, me.y if rel else 1 - me.y, 1 - me.c], got_out.at[rel], s_out + rel, me.core_peer()
                )
            )

        keep["norms"] = ns
        return gate, chosen, router, root, normed_two

    gate, chosen, router, root, normed_two = pl.run_scoped(
        experts,
        pltpu.VMEM((8 * CAP, FF), BF16),
        pltpu.VMEM((8 * CAP, FF), BF16),
        pltpu.VMEM((8 * CAP, WIDTH), F32),
        pltpu.VMEM((8 * CAP, WIDTH), F32),
        pltpu.VMEM((8 * CAP, WIDTH), BF16),
        pltpu.VMEM((8 * CAP, WIDTH), BF16),
    )

    right, left, far = me.x_of(1), me.x_of(3), me.x_of(2)
    keep["core_in"].wait_recv()

    def add_in(j, carry):
        gwi[j, me.c] = (gwi[j, me.c].astype(F32) + got_in[j].astype(F32)).astype(BF16)
        return carry

    lax.fori_loop(0, 8, add_in, 0, unroll=2)
    s_far, s_ring = mail.block(2), mail.block(4)
    fars = [
        mail.go(gwi.at[2 * far, me.c], x_far.at[0], s_far, me.x_peer(1)),
        mail.go(gwi.at[2 * far + 1, me.c], x_far.at[1], s_far + 1, me.x_peer(3)),
    ]
    wait_all(keep["home"])
    keep["core_out", 0].wait_recv()

    def add_out(xx, carry):
        gwo[xx, 1 - me.y, me.c] = (gwo[xx, 1 - me.y, me.c].astype(F32) + got_out[0, xx].astype(F32)).astype(BF16)
        return carry

    lax.fori_loop(0, 4, add_out, 0, unroll=2)
    s_yo = mail.block(4)

    def over_y(k, xx):
        return mail.go(gwo.at[xx, 1 - me.y, me.c], y_out.at[xx], s_yo + k, me.y_peer())


    ys_out = [over_y(0, far), over_y(1, right)]
    returned = dot(select[pl.ds(0, TOK), :], back_got[...])
    gnorm = dot(select[pl.ds(TOK, TOK), :], back_got[...])
    mid = middle[...]
    dy = cot_ref[...].astype(F32)
    y_ref[...] = (mid + gate * returned).astype(BF16)
    ggate = jnp.sum(dy * returned, axis=1, keepdims=True)
    glogits = ggate * gate * (chosen - router)
    high = glogits.astype(BF16)
    rest = (glogits - high.astype(F32)).astype(BF16)
    gnorm = gnorm + dot(high, router_ref[...]) + dot(rest, router_ref[...])
    small[...] = jnp.zeros(small.shape, F32)
    small[pl.ds(8, 8), :] = dot_tn(high, normed_two) + dot_tn(rest, normed_two)
    small[pl.ds(0, 1), :] = jnp.sum(gnorm * mid * root, axis=0, keepdims=True)
    u = gain2 * gnorm
    gmiddle = dy + root * u - mid * (root * root * root * jnp.mean(u * mid, axis=1, keepdims=True))
    gmid[...] = gmiddle
    gmix[...] = gmiddle.astype(BF16)
    upper = iota((TOK, 128), 1) >= 64
    for g in range(4):
        front = dot_nt(gmix[...], out_w_ref[pl.ds(192 * g + 64, 128), :])
        da_send[g, :, pl.ds(0, 128)] = jnp.where(upper, front, 0.0).astype(BF16)
        da_send[g, :, pl.ds(128, 128)] = dot_nt(gmix[...], out_w_ref[pl.ds(192 * g, 128), :]).astype(BF16)
    s_da = mail.block(4)
    das = [mail.go(da_send.at[me.x_of(k)], da.at[mine], s_da + k, me.x_peer(k)) for k in near]
    da[mine, :] = da_send[me.x]
    ring = [
        mail.go(gwi.at[2 * right + 1, me.c], x_near.at[1], s_ring, me.x_peer(1)),
        mail.go(gwi.at[2 * left, me.c], x_near.at[2], s_ring + 1, me.x_peer(3)),
    ]

    def rest(doexp, drow, accb, ds, dq, dkv, y_send, fin_kv, fin_q, dproj, o_low, q_low, k_low):
        att_wide = dot(att[0], att_places(0))
        for g in range(1, 4):
            att_wide = att_wide + dot(att[g], att_places(g))
        att_wide = att_wide.astype(BF16)
        for part in range(4):
            block_rows = dot_tn(att_wide[:, 256 * part : 256 * part + 256], gmix[...]).astype(BF16)
            o_low[part // 2, pl.ds(2 * (part % 2), 2), :, :, pl.ds(0, WIDTH)] = block_rows.reshape(2, 4, 32, WIDTH)
        tiny = dot(small[...].astype(BF16), norm_places()).T.astype(BF16)
        o_low[:, :, :, :, pl.ds(WIDTH, 128)] = tiny.reshape(2, 4, 4, 32, 128)
        core_o = mail.go(o_low.at[1 - me.c], o_core, mail.block(1), me.core_peer())

        wait_all(fars)
        near_right = gwi.at[2 * right, me.c]
        near_right[...] = (near_right[...].astype(F32) + x_far[0].astype(F32)).astype(BF16)
        near_left = gwi.at[2 * left + 1, me.c]
        near_left[...] = (near_left[...].astype(F32) + x_far[1].astype(F32)).astype(BF16)
        ring_all = ring + [
            mail.go(near_right, x_near.at[0], s_ring + 2, me.x_peer(1)),
            mail.go(near_left, x_near.at[3], s_ring + 3, me.x_peer(3)),
        ]

        wait_all(das)
        grads = da[...].astype(F32)
        product = grads * own[...].astype(F32)
        sums = jnp.zeros((512, 128), F32)
        for h in range(3):
            at = (128, 192, 64)[h]
            inside = (lanes >= at) & (lanes < at + 64)
            total = jnp.sum(jnp.where(inside, product, 0.0), axis=1, keepdims=True)
            for half in range(2):
                factor = scale[:, pl.ds(3 * half + h, 1)]
                sums = jnp.where(iota((512, 128), 1) == 3 * half + h, total * factor, sums)
        drow[...] = sums.T
        accb[...] = jnp.zeros(accb.shape, F32)
        dq[...] = jnp.zeros(dq.shape, F32)
        s_ckv, s_ykv = mail.block(8), mail.block(4)

        def core_copy(rel, xx, y):
            part = rows(4 * xx + 2 * y + 1 - me.c, TOK)
            return mail.copy(dkv.at[part], core_kv.at[4 * rel + xx], s_ckv + 4 * rel + xx, me.core_peer())

        def attend(rel, y):
            half = 1 - rel
            for h in range(3):
                at = (128, 192, 64)[h]
                inside = (lanes >= at) & (lanes < at + 64)
                kept = jnp.where(inside, da[...].astype(F32), 0.0) * scale[:, pl.ds(3 * half + h, 1)]
                doexp[pl.ds(512 * h, 512), :] = kept.astype(BF16)

            def one(xx, carry):
                span = rows(2 * xx + y, 256)
                keys = kv[span, pl.ds(0, 256)]
                values = kv[span, pl.ds(128, 256)]
                for h in range(3):
                    cols = pl.ds(512 * h, 512)
                    back = dot_nt(values, doexp[cols, :])
                    part = p_ref[span, cols].astype(F32) * (back - drow[pl.ds(3 * half + h, 1), :])
                    ds[:, cols] = part.astype(BF16)
                    for k in range(2):
                        for t in range(4):
                            kind = jnp.clip(4 * xx + 2 * y + k - (4 * t + 2 * me.y + me.c), -2, 2) + 2
                            accb[h, kind] += part[128 * k : 128 * k + 128, 128 * t : 128 * t + 128]
                for h in range(3):
                    cols = pl.ds(512 * h, 512)
                    dq[pl.ds(64 * h, 64), :] += dot_tn(keys, ds[:, cols])[64 * h : 64 * h + 64]
                gk = dot(ds[...], qexp[...])
                gv = dot(p_ref[span, :], doexp[...])
                dkv[span, pl.ds(0, 128)] = gk[:, :128].astype(BF16)
                dkv[span, pl.ds(128, 128)] = (gk[:, 128:] + gv[:, :128]).astype(BF16)
                dkv[span, pl.ds(256, 128)] = gv[:, 128:].astype(BF16)
                core_copy(rel, xx, y).start()
                return carry

            lax.fori_loop(0, 4, one, 0, unroll=True)

        attend(0, 1 - me.y)

        def to_y(xx):
            return mail.copy(y_send.at[xx], y_kv.at[xx], s_ykv + xx, me.y_peer())

        def forward_y(xx, carry):
            core_copy(0, xx, 1 - me.y).wait_recv()
            part = dkv[rows(4 * xx + 2 * (1 - me.y) + me.c, TOK), :].astype(F32)
            y_send[xx] = (part + core_kv[xx].astype(F32)).astype(BF16)
            to_y(xx).start()
            return carry

        lax.fori_loop(0, 4, forward_y, 0)
        y_rest = [over_y(2, left), over_y(3, me.x)]

        class Sum:
            def __init__(self, low, core, z_got, mid2, q_got, last, x_got, first):
                self.low, self.core, self.z_got = low, core, z_got
                self.mid2, self.q_got, self.last, self.x_got = mid2, q_got, last, x_got
                self.first = first

            def peer(self, axis, k):
                return me.z_peer(k) if axis == "z" else me.q_peer(k)

            def of(self, axis, k):
                return me.z_of(k) if axis == "z" else me.q_of(k)

            def begin(self):
                self.copies = [mail.go(self.low.at[1 - me.c], self.core, mail.block(1), me.core_peer())]

            def part(self, index):
                return self.low.at[me.c, :, index] if self.first == "q" else self.low.at[me.c, index]

            def stage_one(self):
                wait_all(self.copies)
                total = self.low[me.c].astype(F32) + self.core[...].astype(F32)
                self.low[me.c] = total.astype(BF16)
                base = mail.block(4)
                self.copies = [
                    mail.go(self.part(self.of(self.first, k)), self.z_got.at[k - 1], base + k, self.peer(self.first, k))
                    for k in near
                ]

            def stage_two(self):
                wait_all(self.copies)
                total = self.part(me.q if self.first == "q" else me.z)[...].astype(F32)
                for k in range(3):
                    total = total + self.z_got[k].astype(F32)
                self.mid2[...] = total.astype(BF16)
                base = mail.block(4)
                second = "z" if self.first == "q" else "q"
                self.copies = [
                    mail.go(self.mid2.at[self.of(second, k)], self.q_got.at[k - 1], base + k, self.peer(second, k))
                    for k in near
                ]

            def stage_three(self):
                wait_all(self.copies)
                total = self.mid2[me.z if self.first == "q" else me.q].astype(F32)
                for k in range(3):
                    total = total + self.q_got[k].astype(F32)
                self.last[...] = total
                base = mail.block(4)
                self.copies = [
                    mail.go(self.last.at[rows(me.x_of(k), 8)], self.x_got.at[me.x], base + k, me.x_peer(k)) for k in near
                ]
                self.x_got[me.x] = self.last[rows(me.x, 8), :]

            def finish(self):
                wait_all(self.copies)

        of_out = Sum(o_low, o_core, o_z, o_mid2, o_q, o_last, o_x, "z")
        of_out.copies = [core_o]
        of_q = Sum(q_low, q_core, q_z, q_mid2, q_q, q_last, q_x, "z")
        of_kv = Sum(k_low, k_core, k_z, k_mid2, k_q, k_last, k_x, "z")
        of_out.stage_one()

        attend(1, me.y)

        fin_q[...] = (dq[...] * SCALE).T.astype(BF16)
        s_xq, s_xkv = mail.block(4), mail.block(4)
        home = [mail.go(fin_q.at[rows(me.x_of(k), TOK)], home_q.at[me.x], s_xq + k, me.x_peer(k)) for k in near]
        home_q[me.x] = fin_q[mine, :]

        def over_x(xx):
            total = gwo[xx, me.y, me.c].astype(F32) + got_out[1, xx].astype(F32) + y_out[xx].astype(F32)
            y_out[xx] = total.astype(BF16)

        keep["core_out", 1].wait_recv()
        wait_all(ys_out)
        over_x(far)
        over_x(right)
        s_zf, s_zn = mail.block(2), mail.block(4)
        z_fars = [
            mail.go(y_out.at[far, pl.ds(0, 96)], z_far.at[0], s_zf, me.x_peer(1)),
            mail.go(y_out.at[far, pl.ds(96, 96)], z_far.at[1], s_zf + 1, me.x_peer(3)),
        ]
        z_ring = [mail.go(y_out.at[right, pl.ds(96, 96)], z_near.at[1], s_zn, me.x_peer(1))]
        wait_all(keep["norms"])
        for part in range(4):
            span = pl.ds(256 * part, 256)
            block_rows = dot_tn(norm_all[:, span], fin_q[...]).astype(BF16)
            q_low[part // 2, pl.ds(2 * (part % 2), 2)] = block_rows.reshape(2, 4, 32, fin_q.shape[1])
        of_q.begin()
        for k in near + [0]:
            xx = me.x_of(k)
            core_copy(1, xx, me.y).wait_recv()
            to_y(xx).wait_recv()
            part = dkv[rows(4 * xx + 2 * me.y + me.c, TOK), :].astype(F32)
            part = (part + core_kv[4 + xx].astype(F32) + y_kv[xx].astype(F32)).astype(BF16)
            fin_kv[rows(xx, TOK), :] = part
            if k:
                home.append(mail.go(fin_kv.at[rows(xx, TOK)], home_kv.at[me.x], s_xkv + k, me.x_peer(k)))
            else:
                home_kv[me.x] = part
        for part in range(4):
            span = pl.ds(256 * part, 256)
            block_rows = dot_tn(norm_all[:, span], fin_kv[...]).astype(BF16)
            k_low[part // 2, pl.ds(2 * (part % 2), 2)] = block_rows.reshape(2, 4, 32, fin_kv.shape[1])
        of_kv.begin()
        of_q.stage_one()
        of_out.stage_two()

        of_kv.stage_one()
        before, center, after = bucket_tile(tile - 128), bucket_tile(tile), bucket_tile(tile + 128)

        def bucket_sum(b, carry):
            for h in range(3):
                near_sum = (
                    jnp.where(before == b, accb[h, 1], 0.0)
                    + jnp.where(center == b, accb[h, 2], 0.0)
                    + jnp.where(after == b, accb[h, 3], 0.0)
                )
                trow[h, pl.ds(b, 1), :] = jnp.sum(near_sum, axis=0, keepdims=True)
            return carry

        lax.fori_loop(0, BUCKETS, bucket_sum, 0, unroll=4)
        table = jnp.zeros((BUCKETS, 128), F32)
        for h in range(3):
            trow[h, pl.ds(BUCKETS // 2 - 1, 1), :] += jnp.sum(accb[h, 0], axis=0, keepdims=True)
            trow[h, pl.ds(BUCKETS - 1, 1), :] += jnp.sum(accb[h, 4], axis=0, keepdims=True)
            total = jnp.sum(trow[h], axis=1, keepdims=True)
            table = jnp.where(iota((BUCKETS, 128), 1) == 3 * me.x + h, total, table)
        tabs[0] = table
        t_core = mail.go(tabs.at[0], t_got.at[0], mail.block(1), me.core_peer())

        wait_all(ring_all)
        for j in range(2):
            total = gwi[2 * me.x + j, me.c].astype(F32) + x_near[j].astype(F32) + x_near[2 + j].astype(F32)
            gwi[2 * me.x + j, me.c] = total.astype(BF16)
        y_hop = mail.go(gwi.at[2 * me.x + 1 - me.y, me.c], y_in, mail.block(1), me.y_peer())
        wait_all(y_rest)
        over_x(left)
        over_x(me.x)
        z_ring.append(mail.go(y_out.at[left, pl.ds(0, 96)], z_near.at[2], s_zn + 1, me.x_peer(3)))
        of_q.stage_two()
        of_out.stage_three()
        t_core.wait_recv()
        tabs[1] = tabs[0] + t_got[0]
        s_tz = mail.block(4)
        ts = [mail.go(tabs.at[1], t_got.at[k], s_tz + k, me.z_peer(k)) for k in near]
        of_kv.stage_two()

        wait_all(home)

        def piece(p, j):
            g, t = j // 3, j % 3
            if p == 0:
                return home_q[g, :, pl.ds(128 * (t // 2), 128)].astype(F32), t % 2
            if p == 1:
                return home_kv[g, :, pl.ds(128 * (t // 2), 128)].astype(F32), t % 2
            at, half = ((2, 0), (2, 1), (1, 1))[t]
            return home_kv[g, :, pl.ds(128 * at, 128)].astype(F32), half

        for p in range(3):
            for n in range(6):
                first, half_first = piece(p, 2 * n)
                second, half_second = piece(p, 2 * n + 1)
                dproj[p, :, pl.ds(128 * n, 128)] = pair(first, half_first, second, half_second).astype(BF16)
        gnorm = dot_nt(dproj[0], w_ref[0]) + dot_nt(dproj[1], w_ref[1]) + dot_nt(dproj[2], w_ref[2])
        inputs = inp_ref[...].astype(F32)
        root1 = lax.rsqrt(jnp.mean(inputs * inputs, axis=1, keepdims=True) + EPSILON)
        gain1 = gain1_ref[...].reshape(1, WIDTH)
        u = gain1 * gnorm
        mean = jnp.mean(u * inputs, axis=1, keepdims=True)
        gin_ref[...] = gmid[...] + root1 * u - inputs * (root1 * root1 * root1 * mean)

        of_q.stage_three()
        wait_all(ts)
        tabs[2] = tabs[1] + t_got[1] + t_got[2] + t_got[3]
        s_tq = mail.block(4)
        ts = [mail.go(tabs.at[2], t_got.at[3 + k], s_tq + k, me.q_peer(k)) for k in near]
        wait_all(z_fars)
        y_out[right, pl.ds(0, 96), :] = (
            y_out[right, pl.ds(0, 96), :].astype(F32) + z_far[0].astype(F32)
        ).astype(BF16)
        y_out[left, pl.ds(96, 96), :] = (
            y_out[left, pl.ds(96, 96), :].astype(F32) + z_far[1].astype(F32)
        ).astype(BF16)
        z_ring = z_ring + [
            mail.go(y_out.at[right, pl.ds(0, 96)], z_near.at[0], s_zn + 2, me.x_peer(1)),
            mail.go(y_out.at[left, pl.ds(96, 96)], z_near.at[3], s_zn + 3, me.x_peer(3)),
        ]
        of_kv.stage_three()
        wait_all(ts)
        tabs[3] = tabs[2] + t_got[4] + t_got[5] + t_got[6]
        s_tx = mail.block(4)
        ts = [mail.go(tabs.at[3], t_got.at[6 + k], s_tx + k, me.x_peer(k)) for k in near]

        row = iota((16, WIDTH), 0)
        pick = (iota((16, WIDTH), 1) == 6 * (8 * me.i + me.e) + row) & (row < 6)
        pick = pick.astype(F32).astype(BF16)
        picked = [dot(pick, w_ref[p])[:8] for p in range(3)]
        gain_col = jnp.sum(jnp.where(pick[:8].astype(F32) > 0, gain1, 0.0), axis=1, keepdims=True)

        of_out.finish()
        total = o_x[0] + o_x[1] + o_x[2] + o_x[3]
        gout_ref[...] = total
        y_hop.wait_recv()
        gwin_ref[...] = gwi[2 * me.x + me.y, me.c].astype(F32) + y_in[...].astype(F32)
        wait_all(z_ring)
        gwout_ref[pl.ds(0, 96), :] = (
            y_out[me.x, pl.ds(0, 96), :].astype(F32) + z_near[0].astype(F32) + z_near[2].astype(F32)
        )
        gwout_ref[pl.ds(96, 96), :] = (
            y_out[me.x, pl.ds(96, 96), :].astype(F32) + z_near[1].astype(F32) + z_near[3].astype(F32)
        )
        wait_all(ts)
        gtable_ref[...] = tabs[3] + t_got[7] + t_got[8] + t_got[9]
        of_q.finish()
        of_kv.finish()

        def found(p, j):
            g, t = j // 3, j % 3
            if p == 0:
                return q_x[g, :, pl.ds(128 * (t // 2), 128)], t % 2
            if p == 1:
                return k_x[g, :, pl.ds(128 * (t // 2), 128)], t % 2
            at, half = ((2, 0), (2, 1), (1, 1))[t]
            return k_x[g, :, pl.ds(128 * at, 128)], half

        with_gain = jnp.zeros((8, 1), F32)
        for p in range(3):
            for n in range(6):
                first, half_first = found(p, 2 * n)
                second, half_second = found(p, 2 * n + 1)
                cols = pl.ds(128 * n, 128)
                part = pair(first, half_first, second, half_second)
                gqkv_ref[p, :, cols] = part
                with_gain = with_gain + jnp.sum(
                    part * picked[p][:, 128 * n : 128 * n + 128], axis=1, keepdims=True
                )
        real = iota((8, 1), 0) < 6
        gain_ref[...] = jnp.where(real, with_gain / jnp.where(real, gain_col, 1.0), 0.0) * jnp.ones((8, 128), F32)
        for copy in mail.started:
            copy.wait_send()
        for rel, y in ((0, 1 - me.y), (1, me.y)):
            for xx in range(4):
                core_copy(rel, xx, y).wait_send()
        for xx in range(4):
            to_y(xx).wait_send()

    pl.run_scoped(
        rest,
        pltpu.VMEM((1536, 256), BF16),
        pltpu.VMEM((128, 512), F32),
        pltpu.VMEM((3, 5, 128, 128), F32),
        pltpu.VMEM((256, 1536), BF16),
        pltpu.VMEM((256, 512), F32),
        pltpu.VMEM((2048, 384), BF16),
        pltpu.VMEM((4, TOK, 384), BF16),
        pltpu.VMEM((512, 384), BF16),
        pltpu.VMEM((512, 256), BF16),
        pltpu.VMEM((3, TOK, WIDTH), BF16),
        pltpu.VMEM((2, 4, 4, 32, WIDTH + 128), BF16),
        pltpu.VMEM((2, 4, 4, 32, 256), BF16),
        pltpu.VMEM((2, 4, 4, 32, 384), BF16),
    )


def sum_buffers(width):
    return [
        pltpu.VMEM((4, 4, 32, width), BF16),
        pltpu.VMEM((3, 4, 32, width), BF16),
        pltpu.VMEM((4, 32, width), BF16),
        pltpu.VMEM((3, 32, width), BF16),
        pltpu.VMEM((32, width), F32),
        pltpu.VMEM((4, 8, width), F32),
    ]


def layer(*arrays):
    shape = jax.ShapeDtypeStruct
    vm = pltpu.VMEM
    return pl.pallas_call(
        layer_kernel,
        out_shape=(
            shape((TOK, WIDTH), BF16),
            shape((TOK, WIDTH), F32),
            shape((48, FF), F32),
            shape((192, WIDTH), F32),
            shape((3, 8, WIDTH), F32),
            shape((8, WIDTH + 128), F32),
            shape((8, 128), F32),
            shape((BUCKETS, 128), F32),
        ),
        in_specs=[VMEM] * 3 + [SMEM] + [VMEM] * 4 + [ANY] * 2 + [VMEM],
        out_specs=(VMEM,) * 8,
        scratch_shapes=[
            vm((512, 1024), BF16),
            vm((TOK, 1024), BF16),
            vm((512, 256), BF16),
            vm((2048, 384), BF16),
            vm((1536, 256), BF16),
            vm((2048, 1536), BF16),
            vm((512, 128), F32),
            vm((512, 256), BF16),
            vm((4, TOK, 256), BF16),
            vm((TOK, WIDTH), F32),
            vm((2 * TOK, 16 * CAP), BF16),
            vm((16 * CAP, WIDTH), BF16),
            vm((16 * CAP, WIDTH), BF16),
            vm((16 * CAP, WIDTH), BF16),
            vm((8, 2, 48, FF), BF16),
            vm((4, 2, 2, 192, WIDTH), BF16),
            vm((TOK, WIDTH), F32),
            vm((TOK, WIDTH), BF16),
            vm((4, TOK, 256), BF16),
            vm((512, 256), BF16),
            vm((8, TOK, 384), BF16),
            vm((4, TOK, 384), BF16),
            vm((4, TOK, 256), BF16),
            vm((4, TOK, 384), BF16),
            vm((128, WIDTH), F32),
        ]
        + sum_buffers(WIDTH + 128)
        + sum_buffers(256)
        + sum_buffers(384)
        + [
            vm((3, BUCKETS, 128), F32),
            vm((4, BUCKETS, 128), F32),
            vm((10, BUCKETS, 128), F32),
            vm((8, 48, FF), BF16),
            vm((2, 4, 192, WIDTH), BF16),
            vm((2, 48, FF), BF16),
            vm((4, 48, FF), BF16),
            vm((48, FF), BF16),
            vm((4, 192, WIDTH), BF16),
            vm((2, 96, WIDTH), BF16),
            vm((4, 96, WIDTH), BF16),
            pltpu.SemaphoreType.DMA((2,)),
            pltpu.SemaphoreType.DMA((SEMS,)),
            pltpu.SemaphoreType.DMA((SEMS,)),
        ],
        compiler_params=pltpu.CompilerParams(
            collective_id=0, has_side_effects=True, vmem_limit_bytes=VMEM_LIMIT
        ),
    )(*arrays)


def place_kernel(
    y, gin, gwin, gwout, gqkv, gout, gain, table,
    y_ref, gin_ref, gwin_ref, gwout_ref, gqkv_ref, gout_ref, gain1_ref, gain2_ref, router_ref, table_ref,
):
    y_ref[...] = y[...]
    gin_ref[...] = gin[...]
    gwin_ref[...] = gwin[...]
    gwout_ref[...] = gwout[...]
    gqkv_ref[...] = gqkv[:, :6, :]
    gout_ref[...] = gout[:6, :WIDTH]
    gain1_ref[...] = gain[...].T[:1, :6]
    others = gout[:, WIDTH:].T
    gain2_ref[...] = others[:1, :6]
    router_ref[...] = gout[:6, WIDTH + 8 : WIDTH + 16]
    table_ref[...] = table[...].T[:HEADS]


def place(*arrays):
    shape = jax.ShapeDtypeStruct
    return pl.pallas_call(
        place_kernel,
        out_shape=(
            shape((TOK, WIDTH), BF16),
            shape((TOK, WIDTH), F32),
            shape((48, FF), F32),
            shape((192, WIDTH), F32),
            shape((3, 6, WIDTH), F32),
            shape((6, WIDTH), F32),
            shape((1, 6), F32),
            shape((1, 6), F32),
            shape((6, 8), F32),
            shape((HEADS, BUCKETS), F32),
        ),
        in_specs=[VMEM] * 8,
        out_specs=(VMEM,) * 10,
        compiler_params=pltpu.CompilerParams(vmem_limit_bytes=VMEM_LIMIT),
    )(*arrays)


def body(
    block_input, gain_one, qkv_weight, out_weight, rel_table, gain_two, router_weight, routes, w_in, w_out, cotangent
):
    parts = layer(
        block_input[0], gain_one, qkv_weight, rel_table.T, out_weight, gain_two, router_weight.T,
        routes.reshape(1, TOK), w_in.reshape(8, 2, 48, FF), w_out.reshape(4, 2, 2, 192, WIDTH), cotangent[0],
    )
    y, gin, gwin, gwout, gqkv, gout, gain1, gain2, router, table = place(*parts)
    return (
        y[None],
        gin[None],
        gain1.reshape(6),
        gqkv,
        gout,
        table.T,
        gain2.reshape(6),
        router,
        gwin[None],
        gwout[None],
    )


def solution(mesh):
    tokens = P("expert", "ctx", None)
    split = P(("ctx", "expert"))
    return jax.shard_map(
        body,
        mesh=mesh,
        in_specs=(
            tokens, P(), P(), P(), P(), P(), P(), tokens, P("expert", None, None), P("expert", None, None), tokens,
        ),
        out_specs=(
            tokens, tokens, split, P(None, ("ctx", "expert"), None), split, P(), split, split, tokens, tokens,
        ),
        check_vma=False,
    )
```
